32 devices in a mesh: dom: 8 (over z, x), grp: 4 (over y, core).
Axes of the slice: x: 2, y: 2, z: 4, core: 2. Of those that a mesh axis runs over, the one named last changes fastest.
Arguments:
- features: bfloat16 [16384, 128], P('dom'), may hold values from -6 to 6
- weight_self: bfloat16 [128, 1024], P(None, 'grp'), may hold values from -0.5 to 0.5
- weight_neigh: bfloat16 [128, 1024], P(None, 'grp'), may hold values from -3 to 3
- cotangent: bfloat16 [16384, 1024], P('dom', 'grp'), may hold values from -6 to 6
- inner_rows: int32 [8, 64], P('dom'), may hold values from 0 to 15
- inner_cols: int32 [8, 64], P('dom'), may hold values from 0 to 15
- inner_values: bfloat16 [8, 64, 128, 128], P('dom'), may hold values from 0 to 1, as said below
- send_blocks: int32 [8, 8, 3], P('dom'), may hold values from 0 to 15
- outer_rows: int32 [8, 24], P('dom'), may hold values from 0 to 15
- outer_values: bfloat16 [8, 24, 128, 128], P('dom'), may hold values from 0 to 1, as said below
- live_count: int32 [8, 8], P('dom'), may hold values from 0 to 3
Outputs:
- layer_out: bfloat16 [16384, 1024], P('dom', 'grp')
- feature_grad: float32 [16384, 128], P('dom')
- self_grad: float32 [128, 1024], P(None, 'grp')
- neigh_grad: float32 [128, 1024], P(None, 'grp')
The draws below stay inside these ranges and needn't reach their ends.
Inputs may be any that keep to these rules, and one draw needn't show every extreme that they name: `inner_values`: edge weights are zero or positive; most are zero. `outer_values`: edge weights are zero or positive; most are zero.
All inputs are finite; a program needn't handle non-finite values.
Results may differ from the reference program's by a relative error of at most 0.0055.
Values may be sent and summed in bfloat16 or wider, within the bound.
No kernel may reach another device: no remote copies, remote signals or barrier semaphores. Data moves between devices by JAX's collectives and lax.ppermute only.
A program may use at most 128 MiB of HBM per device.

```python
import jax
import jax.numpy as jnp
from jax import lax

F = 128
H = 1024
BLK = 128
NODE_DEV = 2048
NI = 64
SLOTS = 3
LOC_BLK = 16
BSLOTS = 24
NODES = 16384
N_DOM = 8


def sparse_weights(key, shape):
    uniform_a = jax.random.uniform(jax.random.fold_in(key, 11), shape, jnp.float32)
    uniform_b = jax.random.uniform(jax.random.fold_in(key, 12), shape, jnp.float32)
    return jnp.where(uniform_a > 0.97, 0.02 + 0.97 * uniform_b, 0.0)


def draw_inner_values(key, part):
    return sparse_weights(jax.random.fold_in(key, 1), (N_DOM, NI, BLK, BLK)).astype(jnp.bfloat16)


def draw_outer_values(key, part):
    return sparse_weights(jax.random.fold_in(key, 2), (N_DOM, N_DOM * SLOTS, BLK, BLK)).astype(jnp.bfloat16)


def touch_ends(array, key, low, largest):
    longest = array.shape.index(max(array.shape))
    spots = []
    for shift in (0, 1):
        where = [jax.random.randint(jax.random.fold_in(key, axis), (), 0, length) for axis, length in enumerate(array.shape)]
        where[longest] = (where[longest] + shift) % array.shape[longest]
        spots.append(tuple(where))
    return array.at[spots[0]].set(low).at[spots[1]].set(largest)


def block_levels(key, shape, cuts, smallest, largest):
    loudness, own = 1.0, jax.random.fold_in(key, 6)
    for axis_at, parts in cuts:
        heights = jnp.exp(jax.random.uniform(jax.random.fold_in(own, axis_at), (parts,), jnp.float32, smallest / len(cuts), largest / len(cuts)))
        loudness = loudness * jnp.repeat(heights, shape[axis_at] // parts).reshape([-1 if axis == axis_at else 1 for axis in range(len(shape))])
    return loudness


def gaussian(stream_key, extent, width, reach, pieces=(), kind=jnp.bfloat16):
    gain = block_levels(stream_key, extent, pieces, -0.22, 0.18) if pieces else 1.0
    values = jax.random.normal(stream_key, extent, jnp.float32) * width * gain
    return jnp.minimum(jnp.maximum(values, -reach), reach).astype(kind)


def setup_inputs(seed: int = 0) -> dict:
    streams_of = jax.random.split(jax.random.key(seed), 12)
    features = gaussian(streams_of[0], (NODES, F), 1.0, 6.0, ((0, 8),))
    weight_self = gaussian(streams_of[1], (F, H), F ** -0.5, 0.5, ((1, 4),))
    weight_neigh = gaussian(streams_of[2], (F, H), 0.5, 3.0, ((1, 4),))
    cotangent = gaussian(streams_of[3], (NODES, H), 1.0, 6.0, ((0, 8), (1, 4)))
    inner_rows = touch_ends(jax.random.randint(streams_of[4], (N_DOM, NI), 0, LOC_BLK), jax.random.fold_in(streams_of[4], 1), 0, LOC_BLK - 1).astype(jnp.int32)
    inner_cols = touch_ends(jax.random.randint(streams_of[5], (N_DOM, NI), 0, LOC_BLK), jax.random.fold_in(streams_of[5], 1), 0, LOC_BLK - 1).astype(jnp.int32)
    inner_values = draw_inner_values(jax.random.fold_in(streams_of[11], 71), 0)
    send_blocks = touch_ends(jax.random.randint(streams_of[7], (N_DOM, N_DOM, SLOTS), 0, LOC_BLK), jax.random.fold_in(streams_of[7], 1), 0, LOC_BLK - 1).astype(jnp.int32)
    outer_rows = touch_ends(jax.random.randint(streams_of[8], (N_DOM, BSLOTS), 0, LOC_BLK), jax.random.fold_in(streams_of[8], 1), 0, LOC_BLK - 1).astype(jnp.int32)
    outer_values = draw_outer_values(jax.random.fold_in(streams_of[11], 71), 0)
    live_count = touch_ends(jax.random.randint(streams_of[10], (N_DOM, N_DOM), 0, SLOTS + 1), jax.random.fold_in(streams_of[10], 1), 0, SLOTS).astype(jnp.int32)
    return {"features": features, "weight_self": weight_self, "weight_neigh": weight_neigh, "cotangent": cotangent, "inner_rows": inner_rows, "inner_cols": inner_cols, "inner_values": inner_values, "send_blocks": send_blocks, "outer_rows": outer_rows, "outer_values": outer_values, "live_count": live_count}


def reference(features, weight_self, weight_neigh, cotangent, inner_rows, inner_cols, inner_values, send_blocks, outer_rows, outer_values, live_count):
    loc_blocks = NODE_DEV // BLK
    slot_total = N_DOM * SLOTS
    slot_peer = jnp.arange(slot_total, dtype=jnp.int32) // SLOTS
    slot_index = jnp.arange(slot_total, dtype=jnp.int32) % SLOTS
    feat_blocks = features.reshape(N_DOM, loc_blocks, BLK, F)

    def block_sum(values, indices):
        return jax.ops.segment_sum(values, indices, num_segments=loc_blocks)

    def forward_one(device):
        inner_a = inner_values[device].astype(jnp.float32)
        outer_a = outer_values[device].astype(jnp.float32)
        live_mask = (slot_index < live_count[device][slot_peer]).astype(jnp.float32)
        inner_x = feat_blocks[device][inner_cols[device]].astype(jnp.float32)
        outer_x = feat_blocks[slot_peer, send_blocks[slot_peer, device, slot_index]].astype(jnp.float32)
        block_total = block_sum(jnp.einsum('nij,njf->nif', inner_a, inner_x), inner_rows[device])
        block_total = block_total + block_sum(jnp.einsum('nij,njf->nif', outer_a, outer_x) * live_mask[:, None, None], outer_rows[device])
        degree = 1.0 + block_sum(jnp.sum(inner_a, axis=-1), inner_rows[device])
        degree = degree + block_sum(jnp.sum(outer_a, axis=-1) * live_mask[:, None], outer_rows[device])
        aggregate = ((feat_blocks[device].astype(jnp.float32) + block_total) / degree[..., None]).astype(jnp.bfloat16)
        return aggregate, degree

    aggregate, degree = lax.map(forward_one, jnp.arange(N_DOM, dtype=jnp.int32))
    rows_x = features.reshape(N_DOM, NODE_DEV, F)
    rows_a = aggregate.reshape(N_DOM, NODE_DEV, F)
    rows_g = cotangent.reshape(N_DOM, NODE_DEV, H)

    def project(carried, batch_items):
        feature_rows, agg_rows, cot_rows = batch_items
        preact = jnp.dot(feature_rows, weight_self, preferred_element_type=jnp.float32) + jnp.dot(agg_rows, weight_neigh, preferred_element_type=jnp.float32)
        layer_out = jax.nn.silu(preact).astype(jnp.bfloat16)
        sigmoid_v = jax.nn.sigmoid(preact)
        grad_pre = (cot_rows.astype(jnp.float32) * sigmoid_v * (1.0 + preact * (1.0 - sigmoid_v))).astype(jnp.bfloat16)
        grad_self = carried[0] + jnp.dot(feature_rows.T, grad_pre, preferred_element_type=jnp.float32)
        grad_neigh = carried[1] + jnp.dot(agg_rows.T, grad_pre, preferred_element_type=jnp.float32)
        self_back = jnp.dot(grad_pre, weight_self.T, preferred_element_type=jnp.float32)
        neigh_back = jnp.dot(grad_pre, weight_neigh.T, preferred_element_type=jnp.float32)
        return (grad_self, grad_neigh), (layer_out, self_back, neigh_back)

    zero_grad = jnp.zeros((F, H), jnp.float32)
    (grad_self, grad_neigh), (layer_out, self_back, neigh_back) = lax.scan(project, (zero_grad, zero_grad), (rows_x, rows_a, rows_g))
    scaled = (neigh_back.reshape(N_DOM, loc_blocks, BLK, F) / degree[..., None]).astype(jnp.bfloat16)

    def backward_one(accumulated, device):
        inner_a = inner_values[device].astype(jnp.float32)
        outer_a = outer_values[device].astype(jnp.float32)
        live_mask = (slot_index < live_count[device][slot_peer]).astype(jnp.float32)
        inner_s = scaled[device][inner_rows[device]].astype(jnp.float32)
        accumulated = accumulated.at[device, inner_cols[device]].add(jnp.einsum('nij,nif->njf', inner_a, inner_s))
        outer_s = scaled[device][outer_rows[device]].astype(jnp.float32)
        outer_terms = jnp.einsum('nij,nif->njf', outer_a, outer_s) * live_mask[:, None, None]
        accumulated = accumulated.at[slot_peer, send_blocks[slot_peer, device, slot_index]].add(outer_terms)
        return accumulated, None

    accumulated, _ = lax.scan(backward_one, jnp.zeros((N_DOM, loc_blocks, BLK, F), jnp.float32), jnp.arange(N_DOM, dtype=jnp.int32))
    feature_grad = (self_back.reshape(N_DOM, loc_blocks, BLK, F) + scaled.astype(jnp.float32) + accumulated).reshape(NODES, F)
    return layer_out.reshape(NODES, H), feature_grad, grad_self, grad_neigh
```

```python
import functools

import jax
import jax.numpy as jnp
from jax import lax
from jax.experimental import pallas as pl
from jax.experimental.pallas import tpu as pltpu
from jax.sharding import PartitionSpec as P

F32 = jnp.float32
BF16 = jnp.bfloat16
MIB = 1 << 20
GROUP = 8
ROWS_LAST = (((1,), (1,)), ((), ()))
ROWS_FIRST = (((0,), (0,)), ((), ()))
WHOLE = pl.BlockSpec(memory_space=pltpu.VMEM)
SCALARS = pl.BlockSpec(memory_space=pltpu.SMEM)
ANYWHERE = pl.BlockSpec(memory_space=pl.ANY)


def dot(a, b):
    return jnp.dot(a, b, preferred_element_type=F32)


def params(mib):
    return pltpu.CompilerParams(vmem_limit_bytes=int(mib * MIB))


def cost(flops, moved):
    return pl.CostEstimate(flops=int(flops), bytes_accessed=int(moved), transcendentals=0)


def gather_kernel(half, targets, feat, out, sem):
    peers, slots = targets.shape
    block = half * 2
    mine = lax.axis_index("grp") % 2
    for p in range(peers):
        for s in range(slots):
            start = pl.multiple_of(targets[p, s] * block + mine * half, half)
            pltpu.make_async_copy(feat.at[pl.ds(start, half)], out.at[p, s], sem).start()
    pltpu.make_async_copy(out, out, sem).wait()


def gather_halves(features, targets, block):
    peers, slots = targets.shape
    return pl.pallas_call(
        functools.partial(gather_kernel, block // 2),
        out_shape=jax.ShapeDtypeStruct((peers, slots, block // 2, features.shape[1]), BF16),
        in_specs=[SCALARS, ANYWHERE],
        out_specs=ANYWHERE,
        scratch_shapes=[pltpu.SemaphoreType.DMA],
        name="gather_halves",
    )(targets, features)


def inner_kernel(rows, cols, feat, a, total, wide):
    step = pl.program_id(0)
    loc, block, width = total.shape
    feat_width = width // 2

    @pl.when(step == 0)
    def _():
        x = feat[...].reshape(loc, block, feat_width)
        wide[:, :, :feat_width] = x
        wide[:, :, feat_width:] = jnp.ones((loc, block, feat_width), BF16)
        total[:, :, :feat_width] = x.astype(F32)
        total[:, :, feat_width:] = jnp.ones((loc, block, feat_width), F32)

    count = a.shape[0]
    products = [dot(a[k], wide[cols[0, step * count + k]]) for k in range(count)]
    for k in range(count):
        total[rows[0, step * count + k]] += products[k]


def inner_sums(rows, cols, features, values):
    count, block, _ = values.shape
    nodes, feat_width = features.shape
    loc = nodes // block
    return pl.pallas_call(
        inner_kernel,
        out_shape=jax.ShapeDtypeStruct((loc, block, 2 * feat_width), F32),
        grid=(count // GROUP,),
        in_specs=[
            SCALARS,
            SCALARS,
            pl.BlockSpec((nodes, feat_width), lambda i: (0, 0)),
            pl.BlockSpec((GROUP, block, block), lambda i: (i, 0, 0)),
        ],
        out_specs=pl.BlockSpec((loc, block, 2 * feat_width), lambda i: (0, 0, 0)),
        scratch_shapes=[pltpu.VMEM((loc, block, 2 * feat_width), BF16)],
        compiler_params=params(16),
        cost_estimate=cost(count * block * block * feat_width * 4, 6 * MIB),
        name="inner_sums",
    )(rows, cols, features, values)


def layer_kernel(
    chunk_blocks,
    outer_rows, live, own, other, outer, total, feat, cot, w_self, w_neigh,
    layer_out, grads, send_n, keep_n, send_s, keep_s,
    x_wide, a_all, far, weights, turned, grad_sum, sems,
):
    step = pl.program_id(0)
    peers, slots, half, feat_width = own.shape
    count, block, _ = a_all.shape
    loc = far.shape[0]
    group = lax.axis_size("grp")
    part = feat_width // group
    me = lax.axis_index("grp")

    @pl.when(step == 0)
    def _():
        mine = me % 2
        copies = [
            pltpu.make_async_copy(
                own, x_wide.at[:, :, pl.ds(pl.multiple_of(mine * half, half), half), pl.ds(0, feat_width)], sems.at[0]
            ),
            pltpu.make_async_copy(
                other,
                x_wide.at[:, :, pl.ds(pl.multiple_of((1 - mine) * half, half), half), pl.ds(0, feat_width)],
                sems.at[1],
            ),
            pltpu.make_async_copy(outer, a_all, sems.at[2]),
        ]
        for copy in copies:
            copy.start()
        x_wide[:, :, :, feat_width:] = jnp.ones((peers, slots, block, feat_width), BF16)
        far[...] = jnp.zeros_like(far)
        grad_sum[...] = jnp.zeros_like(grad_sum)
        weights[:feat_width] = w_self[...]
        weights[feat_width:] = w_neigh[...]
        for place, away in enumerate((3, 1, 2, 0)):
            start = pl.multiple_of((me ^ away) * part, part)
            turned[pl.ds(place * part, part)] = w_self[pl.ds(start, part)]
            turned[pl.ds(feat_width + place * part, part)] = w_neigh[pl.ds(start, part)]
        for copy in copies:
            copy.wait()

        def some(g, _):
            products = []
            for k in range(GROUP):
                n = g * GROUP + k
                products.append(dot(a_all[n], x_wide[n // slots, n % slots]))
            for k in range(GROUP):
                n = g * GROUP + k
                alive = (n % slots < live[0, n // slots]).astype(F32)
                far[outer_rows[0, n]] += products[k] * alive
            return 0

        lax.fori_loop(0, count // GROUP, some, 0)

    rows = chunk_blocks * block
    here = (total[...] + far[pl.ds(step * chunk_blocks, chunk_blocks)]).reshape(rows, 2 * feat_width)
    over = 1.0 / here[:, feat_width:]
    agg = (here[:, :feat_width] * over).astype(BF16)
    both = jnp.concatenate([feat[...], agg], axis=1)
    pre = dot(both, weights[...])
    sig = 0.5 * jnp.tanh(0.5 * pre) + 0.5
    smooth = pre * sig
    layer_out[...] = smooth.astype(BF16)
    grad_pre = (cot[...].astype(F32) * (sig + smooth * (1.0 - sig))).astype(BF16)
    grad_sum[...] += lax.dot_general(both, grad_pre, ROWS_FIRST, preferred_element_type=F32)
    self_t = lax.dot_general(turned[:feat_width], grad_pre, ROWS_LAST, preferred_element_type=F32).astype(BF16)
    neigh = lax.dot_general(grad_pre, turned[feat_width:], ROWS_LAST, preferred_element_type=F32)
    neigh = (neigh * over).astype(BF16)
    eye = lax.broadcasted_iota(jnp.int32, (feat_width, feat_width), 0) == lax.broadcasted_iota(
        jnp.int32, (feat_width, feat_width), 1
    )
    neigh_t = lax.dot_general(eye.astype(BF16), neigh, ROWS_LAST, preferred_element_type=F32).astype(BF16)
    for b in range(chunk_blocks):
        lanes = slice(b * block, (b + 1) * block)
        for y in range(2):
            send_n[y, b] = neigh_t[y * part : (y + 1) * part, lanes]
            keep_n[y, b] = neigh_t[(2 + y) * part : (3 + y) * part, lanes]
            send_s[y, b] = self_t[y * part : (y + 1) * part, lanes]
            keep_s[y, b] = self_t[(2 + y) * part : (3 + y) * part, lanes]

    @pl.when(step == pl.num_programs(0) - 1)
    def _():
        grads[...] = grad_sum[...].astype(BF16)


def layer(outer_rows, live, own, other, outer, total, features, cotangent, w_self, w_neigh):
    nodes, feat_width = features.shape
    hidden = cotangent.shape[1]
    loc, block, _ = total.shape
    peers, slots, half, _ = own.shape
    count = outer.shape[0]
    chunk = 4
    rows = chunk * block
    part = feat_width // lax.axis_size("grp")
    piece = jax.ShapeDtypeStruct((2, loc, part, block), BF16)
    piece_spec = pl.BlockSpec((2, chunk, part, block), lambda i: (0, i, 0, 0))
    far_bytes = count * block * (block + 2 * feat_width) * 2
    return pl.pallas_call(
        functools.partial(layer_kernel, chunk),
        out_shape=(
            jax.ShapeDtypeStruct((nodes, hidden), BF16),
            jax.ShapeDtypeStruct((2 * feat_width, hidden), BF16),
            piece, piece, piece, piece,
        ),
        grid=(loc // chunk,),
        in_specs=[
            SCALARS, SCALARS, ANYWHERE, ANYWHERE, ANYWHERE,
            pl.BlockSpec((chunk, block, 2 * feat_width), lambda i: (i, 0, 0)),
            pl.BlockSpec((rows, feat_width), lambda i: (i, 0)),
            pl.BlockSpec((rows, hidden), lambda i: (i, 0)),
            pl.BlockSpec((feat_width, hidden), lambda i: (0, 0)),
            pl.BlockSpec((feat_width, hidden), lambda i: (0, 0)),
        ],
        out_specs=(
            pl.BlockSpec((rows, hidden), lambda i: (i, 0)),
            pl.BlockSpec((2 * feat_width, hidden), lambda i: (0, 0)),
            piece_spec, piece_spec, piece_spec, piece_spec,
        ),
        scratch_shapes=[
            pltpu.VMEM((peers, slots, block, 2 * feat_width), BF16),
            pltpu.VMEM((count, block, block), BF16),
            pltpu.VMEM((loc, block, 2 * feat_width), F32),
            pltpu.VMEM((2 * feat_width, hidden), BF16),
            pltpu.VMEM((2 * feat_width, hidden), BF16),
            pltpu.VMEM((2 * feat_width, hidden), F32),
            pltpu.SemaphoreType.DMA((3,)),
        ],
        compiler_params=params(20 + far_bytes / MIB),
        cost_estimate=cost(1.2e9, 8 * MIB),
        name="layer",
    )(outer_rows, live, own, other, outer, total, features, cotangent, w_self, w_neigh)


def outer_back_kernel(outer_rows, live, keep, got, came, outer, scaled, payload):
    peers, slots, part, block = payload.shape
    scaled[...] = (keep[1].astype(F32) + got[1].astype(F32) + came[...].astype(F32)).astype(BF16)

    def some(g, _):
        products = []
        for k in range(GROUP):
            n = g * GROUP + k
            products.append(dot(scaled[outer_rows[0, n]], outer[n]))
        for k in range(GROUP):
            n = g * GROUP + k
            alive = (n % slots < live[0, n // slots]).astype(F32)
            payload[n // slots, n % slots] = (products[k] * alive).astype(BF16)
        return 0

    lax.fori_loop(0, outer.shape[0] // GROUP, some, 0)


def outer_back(outer_rows, live, keep, got, came, outer, peers):
    loc, part, block = came.shape
    count = outer.shape[0]
    return pl.pallas_call(
        outer_back_kernel,
        out_shape=(
            jax.ShapeDtypeStruct((loc, part, block), BF16),
            jax.ShapeDtypeStruct((peers, count // peers, part, block), BF16),
        ),
        in_specs=[SCALARS, SCALARS, WHOLE, WHOLE, WHOLE, WHOLE],
        out_specs=(WHOLE, WHOLE),
        compiler_params=params(8 + count * block * (block + part) * 2 / MIB),
        cost_estimate=cost(count * block * block * part * 2, 2 * MIB),
        name="outer_back",
    )(outer_rows, live, keep, got, came, outer)


def inner_back_kernel(rows, cols, scaled, keep, got, came, a, total):
    step = pl.program_id(0)

    @pl.when(step == 0)
    def _():
        total[...] = (
            keep[1].astype(F32) + got[1].astype(F32) + came[...].astype(F32) + scaled[...].astype(F32)
        )

    count = a.shape[0]
    products = [dot(scaled[rows[0, step * count + k]], a[k]) for k in range(count)]
    for k in range(count):
        total[cols[0, step * count + k]] += products[k]


def inner_back(rows, cols, scaled, keep, got, came, values):
    count, block, _ = values.shape
    loc, part, _ = scaled.shape
    zero3 = lambda i: (0, 0, 0)
    zero4 = lambda i: (0, 0, 0, 0)
    group = 2 * GROUP
    return pl.pallas_call(
        inner_back_kernel,
        out_shape=jax.ShapeDtypeStruct((loc, part, block), F32),
        grid=(count // group,),
        in_specs=[
            SCALARS,
            SCALARS,
            pl.BlockSpec(scaled.shape, zero3),
            pl.BlockSpec(keep.shape, zero4),
            pl.BlockSpec(got.shape, zero4),
            pl.BlockSpec(came.shape, zero3),
            pl.BlockSpec((group, block, block), lambda i: (i, 0, 0)),
        ],
        out_specs=pl.BlockSpec((loc, part, block), zero3),
        compiler_params=params(8),
        cost_estimate=cost(count * block * block * part * 2, 3 * MIB),
        name="inner_back",
    )(rows, cols, scaled, keep, got, came, values)


def add_returned_kernel(targets, returned, total, out, summed):
    peers, slots, _, _ = returned.shape
    summed[...] = total[...]

    def some(q, _):
        for s in range(slots):
            summed[targets[q, s]] += returned[q, s].astype(F32)
        return 0

    lax.fori_loop(0, peers, some, 0)
    out[...] = summed[...].astype(BF16)


def add_returned(targets, returned, total):
    return pl.pallas_call(
        add_returned_kernel,
        out_shape=jax.ShapeDtypeStruct(total.shape, BF16),
        in_specs=[SCALARS, WHOLE, WHOLE],
        out_specs=WHOLE,
        scratch_shapes=[pltpu.VMEM(total.shape, F32)],
        compiler_params=params(8 + returned.size * 2 / MIB),
        cost_estimate=cost(total.size * 8, 2 * MIB),
        name="add_returned",
    )(targets, returned, total)


def turn_kernel(mine, across, beside, out):
    loc, part, block = mine.shape
    me = lax.axis_index("grp")
    feat_width = out.shape[1]
    row = lax.broadcasted_iota(jnp.int32, (feat_width, feat_width), 0)
    lane = lax.broadcasted_iota(jnp.int32, (feat_width, feat_width), 1)
    stacked = row // part
    away = jnp.where(stacked == 1, 2, jnp.where(stacked == 2, 1, stacked))
    order = (((me ^ away) * part + row % part) == lane).astype(BF16)
    for b in range(loc):
        stack = jnp.concatenate([mine[b], across[b], beside[0, b], beside[1, b]], axis=0)
        out[b * block : (b + 1) * block] = lax.dot_general(stack, order, ROWS_FIRST, preferred_element_type=F32)


def turn(mine, across, beside, feat_width):
    loc, part, block = mine.shape
    return pl.pallas_call(
        turn_kernel,
        out_shape=jax.ShapeDtypeStruct((loc * block, feat_width), F32),
        in_specs=[WHOLE, WHOLE, WHOLE],
        out_specs=WHOLE,
        compiler_params=params(8),
        cost_estimate=cost(loc * block * feat_width * feat_width * 2, 2 * MIB),
        name="turn",
    )(mine, across, beside)


def swap(x, axis, bit):
    return lax.ppermute(x, axis, [(i, i ^ bit) for i in range(lax.axis_size(axis))])


def shards(
    features,
    weight_self,
    weight_neigh,
    cotangent,
    inner_rows,
    inner_cols,
    inner_values,
    send_blocks,
    outer_rows,
    outer_values,
    live_count,
):
    peers = lax.axis_size("dom")
    feat_width = features.shape[1]
    inner_a, outer_a, targets = inner_values[0], outer_values[0], send_blocks[0]
    block = inner_a.shape[-1]

    outgoing = gather_halves(features, targets, block)
    own = lax.all_to_all(outgoing, "dom", split_axis=0, concat_axis=0, tiled=True)
    total = inner_sums(inner_rows, inner_cols, features, inner_a)
    other = swap(own, "grp", 1)
    layer_out, grads, send_n, keep_n, send_s, keep_s = layer(
        outer_rows, live_count, own, other, outer_a, total, features, cotangent, weight_self, weight_neigh
    )
    got_n = swap(send_n, "grp", 1)
    came_n = swap((keep_n[0].astype(F32) + got_n[0].astype(F32)).astype(BF16), "grp", 2)
    got_s = swap(send_s, "grp", 1)
    came_s = swap((keep_s[0].astype(F32) + got_s[0].astype(F32)).astype(BF16), "grp", 2)
    scaled, payload = outer_back(outer_rows, live_count, keep_n, got_n, came_n, outer_a, peers)
    returned = lax.all_to_all(payload, "dom", split_axis=0, concat_axis=0, tiled=True)
    bit = peers // 2
    while bit:
        grads = grads.astype(BF16)
        grads = grads.astype(F32) + swap(grads, "dom", bit).astype(F32)
        bit //= 2
    partial = inner_back(inner_rows, inner_cols, scaled, keep_s, got_s, came_s, inner_a)
    mine = add_returned(targets, returned, partial)
    across = swap(mine, "grp", 2)
    beside = swap(jnp.stack([mine, across]), "grp", 1)
    feature_grad = turn(mine, across, beside, feat_width)
    return layer_out, feature_grad, grads[:feat_width], grads[feat_width:]


def solution(mesh):
    placed = (
        P("dom", None),
        P(None, "grp"),
        P(None, "grp"),
        P("dom", "grp"),
        P("dom", None),
        P("dom", None),
        P("dom", None, None, None),
        P("dom", None, None),
        P("dom", None),
        P("dom", None, None, None),
        P("dom", None),
    )
    return jax.shard_map(
        shards,
        mesh=mesh,
        in_specs=placed,
        out_specs=(P("dom", "grp"), P("dom", None), P(None, "grp"), P(None, "grp")),
        check_vma=False,
    )
```

```python
import functools

import jax
import jax.numpy as jnp
from jax import lax
from jax.experimental import pallas as pl
from jax.experimental.pallas import tpu as pltpu
from jax.sharding import PartitionSpec as P

F32 = jnp.float32
BF16 = jnp.bfloat16
MIB = 1 << 20
GROUP = 8
ROWS_LAST = (((1,), (1,)), ((), ()))
ROWS_FIRST = (((0,), (0,)), ((), ()))
WHOLE = pl.BlockSpec(memory_space=pltpu.VMEM)
SCALARS = pl.BlockSpec(memory_space=pltpu.SMEM)
ANYWHERE = pl.BlockSpec(memory_space=pl.ANY)


def dot(a, b):
    return jnp.dot(a, b, preferred_element_type=F32)


def params(mib):
    return pltpu.CompilerParams(vmem_limit_bytes=int(mib * MIB))


def cost(flops, moved):
    return pl.CostEstimate(flops=int(flops), bytes_accessed=int(moved), transcendentals=0)


def gather_kernel(half, targets, feat, out, sem):
    slots, _, peers = targets.shape
    block = half * 2
    mine = lax.axis_index("grp") % 2
    for p in range(peers):
        for s in range(slots):
            start = pl.multiple_of(targets[s, 0, p] * block + mine * half, half)
            pltpu.make_async_copy(feat.at[pl.ds(start, half)], out.at[p, s], sem).start()
    pltpu.make_async_copy(out, out, sem).wait()


def gather_halves(features, targets, block):
    slots, _, peers = targets.shape
    return pl.pallas_call(
        functools.partial(gather_kernel, block // 2),
        out_shape=jax.ShapeDtypeStruct((peers, slots, block // 2, features.shape[1]), BF16),
        in_specs=[SCALARS, ANYWHERE],
        out_specs=WHOLE,
        scratch_shapes=[pltpu.SemaphoreType.DMA],
        compiler_params=params(2 + 6 * peers * slots * block * features.shape[1] / MIB),
        name="gather_halves",
    )(targets, features)


def inner_kernel(rows, cols, feat, a, total, wide):
    step = pl.program_id(0)
    loc, block, width = total.shape
    feat_width = width // 2

    @pl.when(step == 0)
    def _():
        x = feat[...].reshape(loc, block, feat_width)
        wide[:, :, :feat_width] = x
        wide[:, :, feat_width:] = jnp.ones((loc, block, feat_width), BF16)
        total[:, :, :feat_width] = x.astype(F32)
        total[:, :, feat_width:] = jnp.ones((loc, block, feat_width), F32)

    count = a.shape[0]
    products = [dot(a[k], wide[cols[0, step * count + k]]) for k in range(count)]
    for k in range(count):
        total[rows[0, step * count + k]] += products[k]


def inner_sums(rows, cols, features, values):
    count, block, _ = values.shape
    nodes, feat_width = features.shape
    loc = nodes // block
    return pl.pallas_call(
        inner_kernel,
        out_shape=jax.ShapeDtypeStruct((loc, block, 2 * feat_width), F32),
        grid=(count // GROUP,),
        in_specs=[
            SCALARS,
            SCALARS,
            pl.BlockSpec((nodes, feat_width), lambda i: (0, 0)),
            pl.BlockSpec((GROUP, block, block), lambda i: (i, 0, 0)),
        ],
        out_specs=pl.BlockSpec((loc, block, 2 * feat_width), lambda i: (0, 0, 0)),
        scratch_shapes=[pltpu.VMEM((loc, block, 2 * feat_width), BF16)],
        compiler_params=params(16),
        cost_estimate=cost(count * block * block * feat_width * 4, 6 * MIB),
        name="inner_sums",
    )(rows, cols, features, values)


def layer_kernel(
    chunk_blocks,
    outer_rows, live, own, other, outer, total, feat, cot, w_self, w_neigh,
    layer_out, grads, send_n, keep_n, send_s, keep_s,
    x_wide, a_all, far, weights, turned, grad_sum, sems,
):
    step = pl.program_id(0)
    peers, slots, half, feat_width = own.shape
    count, block, _ = a_all.shape
    loc = far.shape[0]
    group = lax.axis_size("grp")
    part = feat_width // group
    me = lax.axis_index("grp")

    @pl.when(step == 0)
    def _():
        mine = me % 2
        copies = [
            pltpu.make_async_copy(
                own, x_wide.at[:, :, pl.ds(pl.multiple_of(mine * half, half), half), pl.ds(0, feat_width)], sems.at[0]
            ),
            pltpu.make_async_copy(
                other,
                x_wide.at[:, :, pl.ds(pl.multiple_of((1 - mine) * half, half), half), pl.ds(0, feat_width)],
                sems.at[1],
            ),
            pltpu.make_async_copy(outer, a_all, sems.at[2]),
        ]
        for copy in copies:
            copy.start()
        x_wide[:, :, :, feat_width:] = jnp.ones((peers, slots, block, feat_width), BF16)
        far[...] = jnp.zeros_like(far)
        grad_sum[...] = jnp.zeros_like(grad_sum)
        weights[:feat_width] = w_self[...]
        weights[feat_width:] = w_neigh[...]
        for place, away in enumerate((3, 1, 2, 0)):
            start = pl.multiple_of((me ^ away) * part, part)
            turned[pl.ds(place * part, part)] = w_self[pl.ds(start, part)]
            turned[pl.ds(feat_width + place * part, part)] = w_neigh[pl.ds(start, part)]
        for copy in copies:
            copy.wait()

        def some(g, _):
            products = []
            for k in range(GROUP):
                n = g * GROUP + k
                products.append(dot(a_all[n], x_wide[n // slots, n % slots]))
            for k in range(GROUP):
                n = g * GROUP + k
                alive = (n % slots < live[0, n // slots]).astype(F32)
                far[outer_rows[0, n]] += products[k] * alive
            return 0

        lax.fori_loop(0, count // GROUP, some, 0)

    rows = chunk_blocks * block
    here = (total[...] + far[pl.ds(step * chunk_blocks, chunk_blocks)]).reshape(rows, 2 * feat_width)
    over = 1.0 / here[:, feat_width:]
    agg = (here[:, :feat_width] * over).astype(BF16)
    both = jnp.concatenate([feat[...], agg], axis=1)
    pre = dot(both, weights[...])
    sig = 0.5 * jnp.tanh(0.5 * pre) + 0.5
    smooth = pre * sig
    layer_out[...] = smooth.astype(BF16)
    grad_pre = (cot[...].astype(F32) * (sig + smooth * (1.0 - sig))).astype(BF16)
    grad_sum[...] += lax.dot_general(both, grad_pre, ROWS_FIRST, preferred_element_type=F32)
    self_t = lax.dot_general(turned[:feat_width], grad_pre, ROWS_LAST, preferred_element_type=F32).astype(BF16)
    neigh = lax.dot_general(grad_pre, turned[feat_width:], ROWS_LAST, preferred_element_type=F32)
    neigh = (neigh * over).astype(BF16)
    eye = lax.broadcasted_iota(jnp.int32, (feat_width, feat_width), 0) == lax.broadcasted_iota(
        jnp.int32, (feat_width, feat_width), 1
    )
    neigh_t = lax.dot_general(eye.astype(BF16), neigh, ROWS_LAST, preferred_element_type=F32).astype(BF16)
    for b in range(chunk_blocks):
        lanes = slice(b * block, (b + 1) * block)
        for y in range(2):
            send_n[y, b] = neigh_t[y * part : (y + 1) * part, lanes]
            keep_n[y, b] = neigh_t[(2 + y) * part : (3 + y) * part, lanes]
            send_s[y, b] = self_t[y * part : (y + 1) * part, lanes]
            keep_s[y, b] = self_t[(2 + y) * part : (3 + y) * part, lanes]

    @pl.when(step == pl.num_programs(0) - 1)
    def _():
        grads[...] = grad_sum[...].astype(BF16)


def layer(outer_rows, live, own, other, outer, total, features, cotangent, w_self, w_neigh):
    nodes, feat_width = features.shape
    hidden = cotangent.shape[1]
    loc, block, _ = total.shape
    peers, slots, half, _ = own.shape
    count = outer.shape[0]
    chunk = 4
    rows = chunk * block
    part = feat_width // lax.axis_size("grp")
    piece = jax.ShapeDtypeStruct((2, loc, part, block), BF16)
    piece_spec = pl.BlockSpec((2, chunk, part, block), lambda i: (0, i, 0, 0))
    far_bytes = count * block * (block + 2 * feat_width) * 2
    return pl.pallas_call(
        functools.partial(layer_kernel, chunk),
        out_shape=(
            jax.ShapeDtypeStruct((nodes, hidden), BF16),
            jax.ShapeDtypeStruct((2 * feat_width, hidden), BF16),
            piece, piece, piece, piece,
        ),
        grid=(loc // chunk,),
        in_specs=[
            SCALARS, SCALARS, ANYWHERE, ANYWHERE, ANYWHERE,
            pl.BlockSpec((chunk, block, 2 * feat_width), lambda i: (i, 0, 0)),
            pl.BlockSpec((rows, feat_width), lambda i: (i, 0)),
            pl.BlockSpec((rows, hidden), lambda i: (i, 0)),
            pl.BlockSpec((feat_width, hidden), lambda i: (0, 0)),
            pl.BlockSpec((feat_width, hidden), lambda i: (0, 0)),
        ],
        out_specs=(
            pl.BlockSpec((rows, hidden), lambda i: (i, 0)),
            pl.BlockSpec((2 * feat_width, hidden), lambda i: (0, 0)),
            piece_spec, piece_spec, piece_spec, piece_spec,
        ),
        scratch_shapes=[
            pltpu.VMEM((peers, slots, block, 2 * feat_width), BF16),
            pltpu.VMEM((count, block, block), BF16),
            pltpu.VMEM((loc, block, 2 * feat_width), F32),
            pltpu.VMEM((2 * feat_width, hidden), BF16),
            pltpu.VMEM((2 * feat_width, hidden), BF16),
            pltpu.VMEM((2 * feat_width, hidden), F32),
            pltpu.SemaphoreType.DMA((3,)),
        ],
        compiler_params=params(20 + far_bytes / MIB),
        cost_estimate=cost(1.2e9, 8 * MIB),
        name="layer",
    )(outer_rows, live, own, other, outer, total, features, cotangent, w_self, w_neigh)


def outer_back_kernel(outer_rows, live, keep, got, came, outer, scaled, payload):
    peers, slots, part, block = payload.shape
    scaled[...] = (keep[1].astype(F32) + got[1].astype(F32) + came[...].astype(F32)).astype(BF16)

    def some(g, _):
        products = []
        for k in range(GROUP):
            n = g * GROUP + k
            products.append(dot(scaled[outer_rows[0, n]], outer[n]))
        for k in range(GROUP):
            n = g * GROUP + k
            alive = (n % slots < live[0, n // slots]).astype(F32)
            payload[n // slots, n % slots] = (products[k] * alive).astype(BF16)
        return 0

    lax.fori_loop(0, outer.shape[0] // GROUP, some, 0)


def outer_back(outer_rows, live, keep, got, came, outer, peers):
    loc, part, block = came.shape
    count = outer.shape[0]
    return pl.pallas_call(
        outer_back_kernel,
        out_shape=(
            jax.ShapeDtypeStruct((loc, part, block), BF16),
            jax.ShapeDtypeStruct((peers, count // peers, part, block), BF16),
        ),
        in_specs=[SCALARS, SCALARS, WHOLE, WHOLE, WHOLE, WHOLE],
        out_specs=(WHOLE, WHOLE),
        compiler_params=params(8 + count * block * (block + part) * 2 / MIB),
        cost_estimate=cost(count * block * block * part * 2, 2 * MIB),
        name="outer_back",
    )(outer_rows, live, keep, got, came, outer)


def inner_back_kernel(rows, cols, scaled, keep, got, came, a, total):
    step = pl.program_id(0)

    @pl.when(step == 0)
    def _():
        total[...] = (
            keep[1].astype(F32) + got[1].astype(F32) + came[...].astype(F32) + scaled[...].astype(F32)
        )

    count = a.shape[0]
    products = [dot(scaled[rows[0, step * count + k]], a[k]) for k in range(count)]
    for k in range(count):
        total[cols[0, step * count + k]] += products[k]


def inner_back(rows, cols, scaled, keep, got, came, values):
    count, block, _ = values.shape
    loc, part, _ = scaled.shape
    zero3 = lambda i: (0, 0, 0)
    zero4 = lambda i: (0, 0, 0, 0)
    group = 2 * GROUP
    return pl.pallas_call(
        inner_back_kernel,
        out_shape=jax.ShapeDtypeStruct((loc, part, block), F32),
        grid=(count // group,),
        in_specs=[
            SCALARS,
            SCALARS,
            pl.BlockSpec(scaled.shape, zero3),
            pl.BlockSpec(keep.shape, zero4),
            pl.BlockSpec(got.shape, zero4),
            pl.BlockSpec(came.shape, zero3),
            pl.BlockSpec((group, block, block), lambda i: (i, 0, 0)),
        ],
        out_specs=pl.BlockSpec((loc, part, block), zero3),
        compiler_params=params(8),
        cost_estimate=cost(count * block * block * part * 2, 3 * MIB),
        name="inner_back",
    )(rows, cols, scaled, keep, got, came, values)


def add_returned_kernel(targets, returned, total, out, summed):
    peers, slots, _, _ = returned.shape
    summed[...] = total[...]

    def some(q, _):
        for s in range(slots):
            summed[targets[s, 0, q]] += returned[q, s].astype(F32)
        return 0

    lax.fori_loop(0, peers, some, 0)
    out[...] = summed[...].astype(BF16)


def add_returned(targets, returned, total):
    return pl.pallas_call(
        add_returned_kernel,
        out_shape=jax.ShapeDtypeStruct(total.shape, BF16),
        in_specs=[SCALARS, WHOLE, WHOLE],
        out_specs=WHOLE,
        scratch_shapes=[pltpu.VMEM(total.shape, F32)],
        compiler_params=params(8 + returned.size * 2 / MIB),
        cost_estimate=cost(total.size * 8, 2 * MIB),
        name="add_returned",
    )(targets, returned, total)


def turn_kernel(mine, across, beside, out):
    loc, part, block = mine.shape
    me = lax.axis_index("grp")
    feat_width = out.shape[1]
    row = lax.broadcasted_iota(jnp.int32, (feat_width, feat_width), 0)
    lane = lax.broadcasted_iota(jnp.int32, (feat_width, feat_width), 1)
    stacked = row // part
    away = jnp.where(stacked == 1, 2, jnp.where(stacked == 2, 1, stacked))
    order = (((me ^ away) * part + row % part) == lane).astype(BF16)
    for b in range(loc):
        stack = jnp.concatenate([mine[b], across[b], beside[0, b], beside[1, b]], axis=0)
        out[b * block : (b + 1) * block] = lax.dot_general(stack, order, ROWS_FIRST, preferred_element_type=F32)


def turn(mine, across, beside, feat_width):
    loc, part, block = mine.shape
    return pl.pallas_call(
        turn_kernel,
        out_shape=jax.ShapeDtypeStruct((loc * block, feat_width), F32),
        in_specs=[WHOLE, WHOLE, WHOLE],
        out_specs=WHOLE,
        compiler_params=params(8),
        cost_estimate=cost(loc * block * feat_width * feat_width * 2, 2 * MIB),
        name="turn",
    )(mine, across, beside)


def swap(x, axis, bit):
    return lax.ppermute(x, axis, [(i, i ^ bit) for i in range(lax.axis_size(axis))])


def shards(
    features,
    weight_self,
    weight_neigh,
    cotangent,
    inner_rows,
    inner_cols,
    inner_values,
    send_blocks,
    outer_rows,
    outer_values,
    live_count,
):
    peers = lax.axis_size("dom")
    feat_width = features.shape[1]
    inner_a, outer_a = inner_values[0], outer_values[0]
    targets = send_blocks.transpose(2, 0, 1)
    block = inner_a.shape[-1]

    outgoing = gather_halves(features, targets, block)
    own = lax.all_to_all(outgoing, "dom", split_axis=0, concat_axis=0, tiled=True)
    own, total = lax.optimization_barrier((own, inner_sums(inner_rows, inner_cols, features, inner_a)))
    other = swap(own, "grp", 1)
    layer_out, grads, send_n, keep_n, send_s, keep_s = layer(
        outer_rows, live_count, own, other, outer_a, total, features, cotangent, weight_self, weight_neigh
    )
    got_n = swap(send_n, "grp", 1)
    came_n = swap((keep_n[0].astype(F32) + got_n[0].astype(F32)).astype(BF16), "grp", 2)
    got_s = swap(send_s, "grp", 1)
    came_s = swap((keep_s[0].astype(F32) + got_s[0].astype(F32)).astype(BF16), "grp", 2)
    scaled, payload = outer_back(outer_rows, live_count, keep_n, got_n, came_n, outer_a, peers)
    returned = lax.all_to_all(payload, "dom", split_axis=0, concat_axis=0, tiled=True)
    bit = 1
    while bit < peers:
        grads = grads.astype(BF16)
        grads = grads.astype(F32) + swap(grads, "dom", bit).astype(F32)
        bit *= 2
    partial = inner_back(inner_rows, inner_cols, scaled, keep_s, got_s, came_s, inner_a)
    mine = add_returned(targets, returned, partial)
    across = swap(mine, "grp", 2)
    beside = swap(jnp.stack([mine, across]), "grp", 1)
    feature_grad = turn(mine, across, beside, feat_width)
    return layer_out, feature_grad, grads[:feat_width], grads[feat_width:]


def solution(mesh):
    placed = (
        P("dom", None),
        P(None, "grp"),
        P(None, "grp"),
        P("dom", "grp"),
        P("dom", None),
        P("dom", None),
        P("dom", None, None, None),
        P("dom", None, None),
        P("dom", None),
        P("dom", None, None, None),
        P("dom", None),
    )
    return jax.shard_map(
        shards,
        mesh=mesh,
        in_specs=placed,
        out_specs=(P("dom", "grp"), P("dom", None), P(None, "grp"), P(None, "grp")),
        check_vma=False,
    )
```

```python
import functools

import jax
import jax.numpy as jnp
from jax import lax
from jax.experimental import pallas as pl
from jax.experimental.pallas import tpu as pltpu
from jax.sharding import PartitionSpec as P

F32 = jnp.float32
BF16 = jnp.bfloat16
MIB = 1 << 20
GROUP = 8
ROWS_LAST = (((1,), (1,)), ((), ()))
ROWS_FIRST = (((0,), (0,)), ((), ()))
WHOLE = pl.BlockSpec(memory_space=pltpu.VMEM)
SCALARS = pl.BlockSpec(memory_space=pltpu.SMEM)
FAR = pl.BlockSpec(memory_space=pltpu.HBM)


def dot(a, b):
    return jnp.dot(a, b, preferred_element_type=F32)


def far(*arrays):
    return [pltpu.with_memory_space_constraint(x, pltpu.HBM) for x in arrays]


def params(mib):
    return pltpu.CompilerParams(vmem_limit_bytes=int(mib * MIB))


def cost(flops, moved):
    return pl.CostEstimate(flops=int(flops), bytes_accessed=int(moved), transcendentals=0)


def gather_kernel(half, targets_far, feat_far, out, targets, feat, sems):
    fetches = [
        pltpu.make_async_copy(targets_far, targets, sems.at[0]),
        pltpu.make_async_copy(feat_far, feat, sems.at[1]),
    ]
    for fetch in fetches:
        fetch.start()
    for fetch in fetches:
        fetch.wait()
    slots, _, peers = targets.shape
    block = half * 2
    mine = lax.axis_index("grp") % 2
    for p in range(peers):
        for s in range(slots):
            start = pl.multiple_of(targets[s, 0, p] * block + mine * half, half)
            pltpu.make_async_copy(feat.at[pl.ds(start, half)], out.at[p, s], sems.at[2]).start()
    pltpu.make_async_copy(out, out, sems.at[2]).wait()


def gather_halves(features, targets, block):
    slots, _, peers = targets.shape
    return pl.pallas_call(
        functools.partial(gather_kernel, block // 2),
        out_shape=jax.ShapeDtypeStruct((peers, slots, block // 2, features.shape[1]), BF16),
        in_specs=[FAR, FAR],
        out_specs=FAR,
        scratch_shapes=[
            pltpu.SMEM(targets.shape, jnp.int32),
            pltpu.VMEM(features.shape, BF16),
            pltpu.SemaphoreType.DMA((3,)),
        ],
        compiler_params=params(4),
        name="gather_halves",
    )(*far(targets, features))


def inner_kernel(rows, cols, feat, a, total, wide):
    step = pl.program_id(0)
    loc, block, width = total.shape
    feat_width = width // 2

    @pl.when(step == 0)
    def _():
        x = feat[...].reshape(loc, block, feat_width)
        wide[:, :, :feat_width] = x
        wide[:, :, feat_width:] = jnp.ones((loc, block, feat_width), BF16)
        total[:, :, :feat_width] = x.astype(F32)
        total[:, :, feat_width:] = jnp.ones((loc, block, feat_width), F32)

    count = a.shape[0]
    products = [dot(a[k], wide[cols[0, step * count + k]]) for k in range(count)]
    for k in range(count):
        total[rows[0, step * count + k]] += products[k]


def inner_sums(rows, cols, features, values):
    count, block, _ = values.shape
    nodes, feat_width = features.shape
    loc = nodes // block
    return pl.pallas_call(
        inner_kernel,
        out_shape=jax.ShapeDtypeStruct((loc, block, 2 * feat_width), F32),
        grid=(count // GROUP,),
        in_specs=[
            SCALARS,
            SCALARS,
            pl.BlockSpec((nodes, feat_width), lambda i: (0, 0)),
            pl.BlockSpec((GROUP, block, block), lambda i: (i, 0, 0)),
        ],
        out_specs=pl.BlockSpec((loc, block, 2 * feat_width), lambda i: (0, 0, 0)),
        scratch_shapes=[pltpu.VMEM((loc, block, 2 * feat_width), BF16)],
        compiler_params=params(16),
        cost_estimate=cost(count * block * block * feat_width * 4, 6 * MIB),
        name="inner_sums",
    )(*far(rows, cols, features, values))


def layer_kernel(
    chunk_blocks,
    outer_rows_far, live_far, own, other, outer_far, total_in, feat_far, cot_far, w_self_far, w_neigh_far,
    layer_out, grads, send_n, keep_n, send_s, keep_s, total,
    outer_rows, live, outer, feat, cot, w_self, w_neigh, smooth, weights, turned, grad_sum, sems, chunk_sems, out_sems,
):
    del total_in
    peers, slots, half, feat_width = own.shape
    count, block, _ = outer.shape
    loc = total.shape[0]
    chunks = loc // chunk_blocks
    rows = chunk_blocks * block
    part = feat_width // lax.axis_size("grp")
    me = lax.axis_index("grp")
    mine = me % 2

    def place(chunk):
        return pl.ds(chunk * rows, rows)

    first = [
        pltpu.make_async_copy(outer_rows_far, outer_rows, sems.at[0]),
        pltpu.make_async_copy(live_far, live, sems.at[1]),
        pltpu.make_async_copy(outer_far, outer, sems.at[2]),
    ]
    second = [
        pltpu.make_async_copy(w_self_far, w_self, sems.at[3]),
        pltpu.make_async_copy(w_neigh_far, w_neigh, sems.at[4]),
    ]
    for c in range(chunks):
        second.append(pltpu.make_async_copy(feat_far.at[place(c)], feat.at[place(c)], chunk_sems.at[0, c]))
        second.append(pltpu.make_async_copy(cot_far.at[place(c)], cot.at[place(c)], chunk_sems.at[1, c]))
    for copy in first + second:
        copy.start()
    ones = jnp.ones((block, feat_width), BF16)
    for copy in first:
        copy.wait()

    def some(g, _):
        products = []
        for k in range(GROUP):
            n = g * GROUP + k
            near, away = own[n // slots, n % slots], other[n // slots, n % slots]
            x = jnp.concatenate([jnp.where(mine == 0, near, away), jnp.where(mine == 0, away, near)], axis=0)
            products.append(dot(outer[n], jnp.concatenate([x, ones], axis=1)))
        for k in range(GROUP):
            n = g * GROUP + k
            alive = (n % slots < live[0, n // slots]).astype(F32)
            total[outer_rows[0, n]] += products[k] * alive
        return 0

    lax.fori_loop(0, count // GROUP, some, 0)
    for copy in second:
        copy.wait()
    weights[:feat_width] = w_self[...] * 0.5
    weights[feat_width:] = w_neigh[...] * 0.5
    for spot, away in enumerate((3, 1, 2, 0)):
        start = pl.multiple_of((me ^ away) * part, part)
        turned[pl.ds(spot * part, part)] = w_self[pl.ds(start, part)] * 0.5
        turned[pl.ds(feat_width + spot * part, part)] = w_neigh[pl.ds(start, part)] * 0.5
    eye = lax.broadcasted_iota(jnp.int32, (feat_width, feat_width), 0) == lax.broadcasted_iota(
        jnp.int32, (feat_width, feat_width), 1
    )
    eye = eye.astype(BF16)
    leaving = []
    for c in range(chunks):
        here = total[pl.ds(c * chunk_blocks, chunk_blocks)].reshape(rows, 2 * feat_width)
        over = 1.0 / here[:, feat_width:]
        agg = (here[:, :feat_width] * over).astype(BF16)
        both = jnp.concatenate([feat[place(c)], agg], axis=1)
        pre = dot(both, weights[...])
        bent = jnp.tanh(pre)
        twice = 1.0 + bent
        silu = pre * twice
        smooth[place(c)] = silu.astype(BF16)
        leaving.append(pltpu.make_async_copy(smooth.at[place(c)], layer_out.at[place(c)], out_sems.at[c]))
        leaving[-1].start()
        grad_pre = (cot[place(c)].astype(F32) * (twice + silu * (1.0 - bent))).astype(BF16)
        grown = lax.dot_general(both, grad_pre, ROWS_FIRST, preferred_element_type=F32)
        if c == 0:
            grad_sum[...] = grown
        elif c < chunks - 1:
            grad_sum[...] += grown
        else:
            grads[...] = (0.5 * (grad_sum[...] + grown)).astype(BF16)
        self_t = lax.dot_general(turned[:feat_width], grad_pre, ROWS_LAST, preferred_element_type=F32).astype(BF16)
        neigh = lax.dot_general(grad_pre, turned[feat_width:], ROWS_LAST, preferred_element_type=F32)
        neigh = (neigh * over).astype(BF16)
        neigh_t = lax.dot_general(eye, neigh, ROWS_LAST, preferred_element_type=F32).astype(BF16)
        for b in range(chunk_blocks):
            lanes = slice(b * block, (b + 1) * block)
            at = c * chunk_blocks + b
            for y in range(2):
                send_n[y, at] = neigh_t[y * part : (y + 1) * part, lanes]
                keep_n[y, at] = neigh_t[(2 + y) * part : (3 + y) * part, lanes]
                send_s[y, at] = self_t[y * part : (y + 1) * part, lanes]
                keep_s[y, at] = self_t[(2 + y) * part : (3 + y) * part, lanes]
    for copy in leaving:
        copy.wait()


def layer(outer_rows, live, own, other, outer, total, features, cotangent, w_self, w_neigh):
    nodes, feat_width = features.shape
    hidden = cotangent.shape[1]
    loc, block, _ = total.shape
    count = outer.shape[0]
    chunk = 4
    part = feat_width // lax.axis_size("grp")
    piece = jax.ShapeDtypeStruct((2, loc, part, block), BF16)
    grads = (2 * feat_width, hidden)
    boundary_bytes = 2 * count * block * (block + 2 * feat_width)
    return pl.pallas_call(
        functools.partial(layer_kernel, chunk),
        out_shape=(
            jax.ShapeDtypeStruct((nodes, hidden), BF16),
            jax.ShapeDtypeStruct(grads, BF16),
            piece, piece, piece, piece,
            jax.ShapeDtypeStruct(total.shape, F32),
        ),
        in_specs=[FAR, FAR, WHOLE, WHOLE, FAR, WHOLE, FAR, FAR, FAR, FAR],
        out_specs=(FAR, WHOLE, WHOLE, WHOLE, WHOLE, WHOLE, WHOLE),
        input_output_aliases={5: 6},
        scratch_shapes=[
            pltpu.SMEM(outer_rows.shape, jnp.int32),
            pltpu.SMEM(live.shape, jnp.int32),
            pltpu.VMEM(outer.shape, BF16),
            pltpu.VMEM(features.shape, BF16),
            pltpu.VMEM(cotangent.shape, BF16),
            pltpu.VMEM(w_self.shape, BF16),
            pltpu.VMEM(w_neigh.shape, BF16),
            pltpu.VMEM(cotangent.shape, BF16),
            pltpu.VMEM(grads, BF16),
            pltpu.VMEM(grads, BF16),
            pltpu.VMEM(grads, F32),
            pltpu.SemaphoreType.DMA((5,)),
            pltpu.SemaphoreType.DMA((2, loc // chunk)),
            pltpu.SemaphoreType.DMA((loc // chunk,)),
        ],
        compiler_params=params(20 + boundary_bytes / MIB),
        cost_estimate=cost(1.2e9, 8 * MIB),
        name="layer",
    )(
        *far(outer_rows, live), own, other, *far(outer), total, *far(features, cotangent, w_self, w_neigh)
    )[:6]


def outer_back_kernel(outer_rows, live, keep, got, came, keep_s, got_s, outer, scaled, base, payload):
    peers, slots, part, block = payload.shape
    near = (keep[1].astype(F32) + got[1].astype(F32) + came[...].astype(F32)).astype(BF16)
    scaled[...] = near
    base[...] = near.astype(F32) + keep_s[1].astype(F32) + got_s[1].astype(F32)

    def some(g, _):
        products = []
        for k in range(GROUP):
            n = g * GROUP + k
            products.append(dot(scaled[outer_rows[0, n]], outer[n]))
        for k in range(GROUP):
            n = g * GROUP + k
            alive = (n % slots < live[0, n // slots]).astype(F32)
            payload[n // slots, n % slots] = (products[k] * alive).astype(BF16)
        return 0

    lax.fori_loop(0, outer.shape[0] // GROUP, some, 0)


def outer_back(outer_rows, live, keep, got, came, keep_s, got_s, outer, peers):
    loc, part, block = came.shape
    count = outer.shape[0]
    return pl.pallas_call(
        outer_back_kernel,
        out_shape=(
            jax.ShapeDtypeStruct((loc, part, block), BF16),
            jax.ShapeDtypeStruct((loc, part, block), F32),
            jax.ShapeDtypeStruct((peers, count // peers, part, block), BF16),
        ),
        in_specs=[SCALARS, SCALARS] + [WHOLE] * 6,
        out_specs=(WHOLE, WHOLE, WHOLE),
        compiler_params=params(8 + count * block * (block + part) * 2 / MIB),
        cost_estimate=cost(count * block * block * part * 2, 2 * MIB),
        name="outer_back",
    )(*far(outer_rows, live), keep, got, came, keep_s, got_s, outer)


def inner_back_kernel(rows, cols, scaled, base, came, a, total):
    step = pl.program_id(0)

    @pl.when(step == 0)
    def _():
        total[...] = base[...] + came[...].astype(F32)

    count = a.shape[0]
    products = [dot(scaled[rows[0, step * count + k]], a[k]) for k in range(count)]
    for k in range(count):
        total[cols[0, step * count + k]] += products[k]


def inner_back(rows, cols, scaled, base, came, values):
    count, block, _ = values.shape
    group = 2 * GROUP
    piece = pl.BlockSpec(scaled.shape, lambda i: (0, 0, 0))
    return pl.pallas_call(
        inner_back_kernel,
        out_shape=jax.ShapeDtypeStruct(base.shape, F32),
        grid=(count // group,),
        in_specs=[
            SCALARS,
            SCALARS,
            piece,
            piece,
            piece,
            pl.BlockSpec((group, block, block), lambda i: (i, 0, 0)),
        ],
        out_specs=piece,
        compiler_params=params(8),
        cost_estimate=cost(count * block * block * scaled.shape[1] * 2, 3 * MIB),
        name="inner_back",
    )(*far(rows, cols), scaled, base, came, *far(values))


def add_returned_kernel(targets, returned, total, out, summed):
    peers, slots, _, _ = returned.shape
    summed[...] = total[...]

    def some(q, _):
        for s in range(slots):
            summed[targets[s, 0, q]] += returned[q, s].astype(F32)
        return 0

    lax.fori_loop(0, peers, some, 0)
    out[...] = summed[...].astype(BF16)


def add_returned(targets, returned, total):
    return pl.pallas_call(
        add_returned_kernel,
        out_shape=jax.ShapeDtypeStruct(total.shape, BF16),
        in_specs=[SCALARS, WHOLE, WHOLE],
        out_specs=WHOLE,
        scratch_shapes=[pltpu.VMEM(total.shape, F32)],
        compiler_params=params(8 + returned.size * 2 / MIB),
        cost_estimate=cost(total.size * 8, 2 * MIB),
        name="add_returned",
    )(*far(targets), returned, total)


def pair_sum_kernel(a, b, out):
    out[...] = (a[...].astype(F32) + b[...].astype(F32)).astype(BF16)


def pair_sum(a, b):
    return pl.pallas_call(
        pair_sum_kernel,
        out_shape=jax.ShapeDtypeStruct(a.shape, BF16),
        in_specs=[WHOLE, WHOLE],
        out_specs=WHOLE,
        compiler_params=params(4),
        cost_estimate=cost(a.size * 2, a.size * 6),
        name="pair_sum",
    )(a, b)


def finish_kernel(mine, across, beside, opposite, grads, grads_came, out, self_grad, neigh_grad):
    loc, part, block = mine.shape
    me = lax.axis_index("grp")
    feat_width = out.shape[1]
    self_grad[...] = grads[:feat_width].astype(F32) + grads_came[:feat_width].astype(F32)
    neigh_grad[...] = grads[feat_width:].astype(F32) + grads_came[feat_width:].astype(F32)
    row = lax.broadcasted_iota(jnp.int32, (feat_width, feat_width), 0)
    lane = lax.broadcasted_iota(jnp.int32, (feat_width, feat_width), 1)
    stacked = row // part
    away = jnp.where(stacked == 1, 2, jnp.where(stacked == 2, 1, stacked))
    order = (((me ^ away) * part + row % part) == lane).astype(BF16)
    for b in range(loc):
        stack = jnp.concatenate([mine[b], across[b], beside[b], opposite[b]], axis=0)
        out[b * block : (b + 1) * block] = lax.dot_general(stack, order, ROWS_FIRST, preferred_element_type=F32)


def finish(mine, across, beside, opposite, grads, grads_came):
    loc, part, block = mine.shape
    feat_width = grads.shape[0] // 2
    weight = jax.ShapeDtypeStruct((feat_width, grads.shape[1]), F32)
    return pl.pallas_call(
        finish_kernel,
        out_shape=(jax.ShapeDtypeStruct((loc * block, feat_width), F32), weight, weight),
        in_specs=[WHOLE] * 6,
        out_specs=(WHOLE, WHOLE, WHOLE),
        compiler_params=params(8),
        cost_estimate=cost(loc * block * feat_width * feat_width * 2, 2 * MIB),
        name="finish",
    )(mine, across, beside, opposite, grads, grads_came)


def swap(x, axis, bit):
    return lax.ppermute(x, axis, [(i, i ^ bit) for i in range(lax.axis_size(axis))])


def shards(
    features,
    weight_self,
    weight_neigh,
    cotangent,
    inner_rows,
    inner_cols,
    inner_values,
    send_blocks,
    outer_rows,
    outer_values,
    live_count,
):
    peers = lax.axis_size("dom")
    feat_width = features.shape[1]
    inner_a, outer_a = inner_values[0], outer_values[0]
    targets = send_blocks.transpose(2, 0, 1)
    block = inner_a.shape[-1]

    outgoing = gather_halves(features, targets, block)
    own = lax.all_to_all(outgoing, "dom", split_axis=0, concat_axis=0, tiled=True)
    own, total = lax.optimization_barrier((own, inner_sums(inner_rows, inner_cols, features, inner_a)))
    other = swap(own, "grp", 1)
    layer_out, grads, send_n, keep_n, send_s, keep_s = layer(
        outer_rows, live_count, own, other, outer_a, total, features, cotangent, weight_self, weight_neigh
    )
    got_n = swap(send_n, "grp", 1)
    came_n = swap((keep_n[0].astype(F32) + got_n[0].astype(F32)).astype(BF16), "grp", 2)
    got_s = swap(send_s, "grp", 1)
    came_s = swap((keep_s[0].astype(F32) + got_s[0].astype(F32)).astype(BF16), "grp", 2)
    scaled, base, payload = outer_back(
        outer_rows, live_count, keep_n, got_n, came_n, keep_s, got_s, outer_a, peers
    )
    returned = lax.all_to_all(payload, "dom", split_axis=0, concat_axis=0, tiled=True)
    bit = peers // 2
    while bit > 2:
        grads = pair_sum(grads, swap(grads, "dom", bit))
        bit //= 2
    base, grads = lax.optimization_barrier((base, grads))
    partial = inner_back(inner_rows, inner_cols, scaled, base, came_s, inner_a)
    partial, grads = lax.optimization_barrier((partial, pair_sum(grads, swap(grads, "dom", 2))))
    mine = add_returned(targets, returned, partial)
    across = swap(mine, "grp", 2)
    beside = swap(mine, "grp", 1)
    opposite = swap(across, "grp", 1)
    feature_grad, self_grad, neigh_grad = finish(mine, across, beside, opposite, grads, swap(grads, "dom", 1))
    return layer_out, feature_grad, self_grad, neigh_grad


def solution(mesh):
    placed = (
        P("dom", None),
        P(None, "grp"),
        P(None, "grp"),
        P("dom", "grp"),
        P("dom", None),
        P("dom", None),
        P("dom", None, None, None),
        P("dom", None, None),
        P("dom", None),
        P("dom", None, None, None),
        P("dom", None),
    )
    return jax.shard_map(
        shards,
        mesh=mesh,
        in_specs=placed,
        out_specs=(P("dom", "grp"), P("dom", None), P(None, "grp"), P(None, "grp")),
        check_vma=False,
    )
```

```python
import functools

import jax
import jax.numpy as jnp
from jax import lax
from jax.experimental import pallas as pl
from jax.experimental.pallas import tpu as pltpu
from jax.sharding import PartitionSpec as P

F32 = jnp.float32
BF16 = jnp.bfloat16
MIB = 1 << 20
GROUP = 8
ROWS_LAST = (((1,), (1,)), ((), ()))
ROWS_FIRST = (((0,), (0,)), ((), ()))
WHOLE = pl.BlockSpec(memory_space=pltpu.VMEM)
SCALARS = pl.BlockSpec(memory_space=pltpu.SMEM)
FAR = pl.BlockSpec(memory_space=pltpu.HBM)


def dot(a, b):
    return jnp.dot(a, b, preferred_element_type=F32)


def far(*arrays):
    return [pltpu.with_memory_space_constraint(x, pltpu.HBM) for x in arrays]


def params(mib):
    return pltpu.CompilerParams(vmem_limit_bytes=int(mib * MIB))


def cost(flops, moved):
    return pl.CostEstimate(flops=int(flops), bytes_accessed=int(moved), transcendentals=0)


def gather_kernel(half, targets_far, feat_far, out, targets, feat, sems):
    fetches = [
        pltpu.make_async_copy(targets_far, targets, sems.at[0]),
        pltpu.make_async_copy(feat_far, feat, sems.at[1]),
    ]
    for fetch in fetches:
        fetch.start()
    for fetch in fetches:
        fetch.wait()
    slots, _, peers = targets.shape
    block = half * 2
    mine = lax.axis_index("grp") % 2
    for p in range(peers):
        for s in range(slots):
            start = pl.multiple_of(targets[s, 0, p] * block + mine * half, half)
            pltpu.make_async_copy(feat.at[pl.ds(start, half)], out.at[p, s], sems.at[2]).start()
    pltpu.make_async_copy(out, out, sems.at[2]).wait()


def gather_halves(features, targets, block):
    slots, _, peers = targets.shape
    return pl.pallas_call(
        functools.partial(gather_kernel, block // 2),
        out_shape=jax.ShapeDtypeStruct((peers, slots, block // 2, features.shape[1]), BF16),
        in_specs=[FAR, FAR],
        out_specs=FAR,
        scratch_shapes=[
            pltpu.SMEM(targets.shape, jnp.int32),
            pltpu.VMEM(features.shape, BF16),
            pltpu.SemaphoreType.DMA((3,)),
        ],
        compiler_params=params(4),
        name="gather_halves",
    )(*far(targets, features))


def stage_kernel(
    rows_far, cols_far, outer_rows_far, live_far, targets_far, feat_far, inner_far, outer_far,
    rows, cols, outer_rows, live, targets, total, over, outer,
    feat, inner, wide, sems, inner_sems,
):
    loc, block, feat_width = total.shape
    count, outer_count = inner.shape[0], outer.shape[0]
    slots, _, peers = targets.shape
    scalars = [
        pltpu.make_async_copy(source, place, sems.at[k])
        for k, (source, place) in enumerate((
            (rows_far, rows), (cols_far, cols), (outer_rows_far, outer_rows), (live_far, live), (targets_far, targets),
        ))
    ]
    tables = [
        pltpu.make_async_copy(source, place, sems.at[5 + k])
        for k, (source, place) in enumerate((
            (feat_far, feat), (outer_far, outer),
        ))
    ]
    groups = count // GROUP
    blocks = [
        pltpu.make_async_copy(
            inner_far.at[pl.ds(g * GROUP, GROUP)], inner.at[pl.ds(g * GROUP, GROUP)], inner_sems.at[g]
        )
        for g in range(groups)
    ]
    for copy in scalars + tables[:1] + blocks + tables[1:]:
        copy.start()
    for copy in scalars + tables[:1]:
        copy.wait()
    x = feat[...].reshape(loc, block, feat_width)
    wide[:, :, :feat_width] = x
    wide[:, :, feat_width:] = jnp.ones((loc, block, feat_width), BF16)
    total[...] = x.astype(F32)
    over[...] = jnp.ones((loc, block, feat_width), F32)
    for g in range(groups):
        blocks[g].wait()
        products = [dot(inner[g * GROUP + k], wide[cols[0, g * GROUP + k]]) for k in range(GROUP)]
        for k in range(GROUP):
            r = rows[0, g * GROUP + k]
            total[r] += products[k][:, :feat_width]
            over[r] += products[k][:, feat_width:]
    for copy in tables[1:]:
        copy.wait()

    def some(g, _):
        ones = jnp.ones((block, feat_width), BF16)
        products = [dot(outer[g * GROUP + k], ones) for k in range(GROUP)]
        for k in range(GROUP):
            n = g * GROUP + k
            alive = (n % slots < live[0, n // slots]).astype(F32)
            over[outer_rows[0, n]] += products[k] * alive
        return 0

    lax.fori_loop(0, outer_count // GROUP, some, 0)
    over[...] = 1.0 / over[...]


def stage(rows, cols, outer_rows, live, targets, features, inner, outer):
    count, block, _ = inner.shape
    nodes, feat_width = features.shape
    loc = nodes // block
    scalars = (rows, cols, outer_rows, live, targets)
    sums = (loc, block, feat_width)
    return pl.pallas_call(
        stage_kernel,
        out_shape=tuple(pltpu.SMEM(x.shape, jnp.int32) for x in scalars)
        + (pltpu.VMEM(sums, F32), pltpu.VMEM(sums, F32), pltpu.VMEM(outer.shape, BF16)),
        in_specs=[FAR] * 8,
        out_specs=(SCALARS,) * 5 + (WHOLE,) * 3,
        scratch_shapes=[
            pltpu.VMEM(features.shape, BF16),
            pltpu.VMEM(inner.shape, BF16),
            pltpu.VMEM((loc, block, 2 * feat_width), BF16),
            pltpu.SemaphoreType.DMA((7,)),
            pltpu.SemaphoreType.DMA((count // GROUP,)),
        ],
        compiler_params=params(12 + outer.size * 2 / MIB),
        cost_estimate=cost(count * block * block * feat_width * 4, 6 * MIB),
        name="stage",
    )(*far(*scalars, features, inner, outer))


def layer_kernel(
    chunk_blocks,
    outer_rows, live, own, other, outer, total_in, over_all, feat_far, cot_far, self_far, neigh_far,
    layer_out, grads, send_n, keep_n, send_s, keep_s, total,
    feat, cot, w_self, w_neigh, smooth, weights, turned, grad_sum, sems, out_sems,
):
    del total_in
    peers, slots, half, feat_width = own.shape
    count, block, _ = outer.shape
    loc = total.shape[0]
    chunks = loc // chunk_blocks
    rows = chunk_blocks * block
    part = feat_width // lax.axis_size("grp")
    me = lax.axis_index("grp")
    mine = me % 2
    fetches = [
        pltpu.make_async_copy(source, place, sems.at[k])
        for k, (source, place) in enumerate((
            (self_far, w_self), (neigh_far, w_neigh), (feat_far, feat), (cot_far, cot),
        ))
    ]
    for fetch in fetches:
        fetch.start()

    def some(g, _):
        products = []
        for k in range(GROUP):
            n = g * GROUP + k
            near, away = own[n // slots, n % slots], other[n // slots, n % slots]
            x = jnp.concatenate([jnp.where(mine == 0, near, away), jnp.where(mine == 0, away, near)], axis=0)
            products.append(dot(outer[n], x))
        for k in range(GROUP):
            n = g * GROUP + k
            alive = (n % slots < live[0, n // slots]).astype(F32)
            total[outer_rows[0, n]] += products[k] * alive
        return 0

    lax.fori_loop(0, count // GROUP, some, 0)
    for fetch in fetches:
        fetch.wait()
    weights[:feat_width] = w_self[...] * 0.5
    weights[feat_width:] = w_neigh[...] * 0.5
    for spot, away in enumerate((3, 1, 2, 0)):
        start = pl.multiple_of((me ^ away) * part, part)
        turned[pl.ds(spot * part, part)] = w_self[pl.ds(start, part)] * 0.5
        turned[pl.ds(feat_width + spot * part, part)] = w_neigh[pl.ds(start, part)] * 0.5
    eye = lax.broadcasted_iota(jnp.int32, (feat_width, feat_width), 0) == lax.broadcasted_iota(
        jnp.int32, (feat_width, feat_width), 1
    )
    eye = eye.astype(BF16)
    leaving = []
    for c in range(chunks):
        place = pl.ds(c * rows, rows)
        here = pl.ds(c * chunk_blocks, chunk_blocks)
        over = over_all[here].reshape(rows, feat_width)
        agg = (total[here].reshape(rows, feat_width) * over).astype(BF16)
        both = jnp.concatenate([feat[place], agg], axis=1)
        pre = dot(both, weights[...])
        bent = jnp.tanh(pre)
        twice = 1.0 + bent
        silu = pre * twice
        smooth[place] = silu.astype(BF16)
        leaving.append(pltpu.make_async_copy(smooth.at[place], layer_out.at[place], out_sems.at[c]))
        leaving[-1].start()
        grad_pre = (cot[place].astype(F32) * (twice + silu * (1.0 - bent))).astype(BF16)
        grown = lax.dot_general(both, grad_pre, ROWS_FIRST, preferred_element_type=F32)
        if c == 0:
            grad_sum[...] = grown
        elif c < chunks - 1:
            grad_sum[...] += grown
        else:
            grads[...] = (0.5 * (grad_sum[...] + grown)).astype(BF16)
        self_t = lax.dot_general(turned[:feat_width], grad_pre, ROWS_LAST, preferred_element_type=F32).astype(BF16)
        neigh = lax.dot_general(grad_pre, turned[feat_width:], ROWS_LAST, preferred_element_type=F32)
        neigh = (neigh * over).astype(BF16)
        neigh_t = lax.dot_general(eye, neigh, ROWS_LAST, preferred_element_type=F32).astype(BF16)
        for b in range(chunk_blocks):
            lanes = slice(b * block, (b + 1) * block)
            at = c * chunk_blocks + b
            for y in range(2):
                send_n[y, at] = neigh_t[y * part : (y + 1) * part, lanes]
                keep_n[y, at] = neigh_t[(2 + y) * part : (3 + y) * part, lanes]
                send_s[y, at] = self_t[y * part : (y + 1) * part, lanes]
                keep_s[y, at] = self_t[(2 + y) * part : (3 + y) * part, lanes]
    for copy in leaving:
        copy.wait()


def layer(outer_rows, live, own, other, outer, total, over, features, cotangent, w_self, w_neigh):
    feat_width = features.shape[1]
    loc, block, _ = total.shape
    chunk = 4
    grads = (2 * feat_width, cotangent.shape[1])
    part = feat_width // lax.axis_size("grp")
    piece = pltpu.VMEM((2, loc, part, block), BF16)
    return pl.pallas_call(
        functools.partial(layer_kernel, chunk),
        out_shape=(
            jax.ShapeDtypeStruct(cotangent.shape, BF16),
            pltpu.VMEM(grads, BF16),
            piece, piece, piece, piece,
            pltpu.VMEM(total.shape, F32),
        ),
        in_specs=[SCALARS] * 2 + [WHOLE] * 5 + [FAR] * 4,
        out_specs=(FAR,) + (WHOLE,) * 6,
        input_output_aliases={5: 6},
        scratch_shapes=[
            pltpu.VMEM(features.shape, BF16),
            pltpu.VMEM(cotangent.shape, BF16),
            pltpu.VMEM(w_self.shape, BF16),
            pltpu.VMEM(w_neigh.shape, BF16),
            pltpu.VMEM(cotangent.shape, BF16),
            pltpu.VMEM(grads, BF16),
            pltpu.VMEM(grads, BF16),
            pltpu.VMEM(grads, F32),
            pltpu.SemaphoreType.DMA((4,)),
            pltpu.SemaphoreType.DMA((loc // chunk,)),
        ],
        compiler_params=params(16 + 4 * own.size * 2 / MIB),
        cost_estimate=cost(1.2e9, 8 * MIB),
        name="layer",
    )(outer_rows, live, own, other, outer, total, over, *far(features, cotangent, w_self, w_neigh))[:6]


def outer_back_kernel(outer_rows, live, keep, got, came, keep_s, got_s, outer, scaled, base, payload):
    peers, slots, part, block = payload.shape
    near = (keep[1].astype(F32) + got[1].astype(F32) + came[...].astype(F32)).astype(BF16)
    scaled[...] = near
    base[...] = near.astype(F32) + keep_s[1].astype(F32) + got_s[1].astype(F32)

    def some(g, _):
        products = []
        for k in range(GROUP):
            n = g * GROUP + k
            products.append(dot(scaled[outer_rows[0, n]], outer[n]))
        for k in range(GROUP):
            n = g * GROUP + k
            alive = (n % slots < live[0, n // slots]).astype(F32)
            payload[n // slots, n % slots] = (products[k] * alive).astype(BF16)
        return 0

    lax.fori_loop(0, outer.shape[0] // GROUP, some, 0)


def outer_back(outer_rows, live, keep, got, came, keep_s, got_s, outer, peers):
    loc, part, block = came.shape
    count = outer.shape[0]
    return pl.pallas_call(
        outer_back_kernel,
        out_shape=(
            pltpu.VMEM((loc, part, block), BF16),
            pltpu.VMEM((loc, part, block), F32),
            jax.ShapeDtypeStruct((peers, count // peers, part, block), BF16),
        ),
        in_specs=[SCALARS, SCALARS] + [WHOLE] * 6,
        out_specs=(WHOLE, WHOLE, WHOLE),
        compiler_params=params(8 + count * block * (block + part) * 2 / MIB),
        cost_estimate=cost(count * block * block * part * 2, 2 * MIB),
        name="outer_back",
    )(outer_rows, live, keep, got, came, keep_s, got_s, outer)


def inner_back_kernel(rows, cols, scaled, base, inner_far, grads, grads_came, total, grads_out, inner, sems):
    groups = inner.shape[0] // GROUP
    blocks = [
        pltpu.make_async_copy(inner_far.at[pl.ds(g * GROUP, GROUP)], inner.at[pl.ds(g * GROUP, GROUP)], sems.at[g])
        for g in range(groups)
    ]
    for copy in blocks:
        copy.start()
    total[...] = base[...]
    grads_out[...] = (grads[...].astype(F32) + grads_came[...].astype(F32)).astype(BF16)
    for g in range(groups):
        blocks[g].wait()
        products = [dot(scaled[rows[0, g * GROUP + k]], inner[g * GROUP + k]) for k in range(GROUP)]
        for k in range(GROUP):
            total[cols[0, g * GROUP + k]] += products[k]


def inner_back(rows, cols, scaled, base, inner, grads, grads_came):
    count, block, _ = inner.shape
    return pl.pallas_call(
        inner_back_kernel,
        out_shape=(pltpu.VMEM(base.shape, F32), pltpu.VMEM(grads.shape, BF16)),
        in_specs=[SCALARS, SCALARS, WHOLE, WHOLE, FAR, WHOLE, WHOLE],
        out_specs=(WHOLE, WHOLE),
        scratch_shapes=[pltpu.VMEM(inner.shape, BF16), pltpu.SemaphoreType.DMA((count // GROUP,))],
        compiler_params=params(8),
        cost_estimate=cost(count * block * block * scaled.shape[1] * 2, 3 * MIB),
        name="inner_back",
    )(rows, cols, scaled, base, *far(inner), grads, grads_came)


def add_returned_kernel(targets, returned, came, total, out, summed):
    peers, slots, _, _ = returned.shape
    summed[...] = total[...] + came[...].astype(F32)

    def some(q, _):
        for s in range(slots):
            summed[targets[s, 0, q]] += returned[q, s].astype(F32)
        return 0

    lax.fori_loop(0, peers, some, 0)
    out[...] = summed[...].astype(BF16)


def add_returned(targets, returned, came, total):
    return pl.pallas_call(
        add_returned_kernel,
        out_shape=pltpu.VMEM(total.shape, BF16),
        in_specs=[SCALARS, WHOLE, WHOLE, WHOLE],
        out_specs=WHOLE,
        scratch_shapes=[pltpu.VMEM(total.shape, F32)],
        compiler_params=params(8 + returned.size * 2 / MIB),
        cost_estimate=cost(total.size * 8, 2 * MIB),
        name="add_returned",
    )(targets, returned, came, total)


def pair_sum_kernel(a, b, out):
    out[...] = (a[...].astype(F32) + b[...].astype(F32)).astype(BF16)


def pair_sum(a, b):
    return pl.pallas_call(
        pair_sum_kernel,
        out_shape=jax.ShapeDtypeStruct(a.shape, BF16),
        in_specs=[WHOLE, WHOLE],
        out_specs=WHOLE,
        compiler_params=params(4),
        cost_estimate=cost(a.size * 2, a.size * 6),
        name="pair_sum",
    )(a, b)


def finish_kernel(mine, across, beside, opposite, grads, grads_came, out, self_out, neigh_out, turned, summed, sems):
    loc, part, block = mine.shape
    me = lax.axis_index("grp")
    feat_width = turned.shape[1]
    summed[...] = grads[...].astype(F32) + grads_came[...].astype(F32)
    copies = [
        pltpu.make_async_copy(summed.at[pl.ds(0, feat_width)], self_out, sems.at[0]),
        pltpu.make_async_copy(summed.at[pl.ds(feat_width, feat_width)], neigh_out, sems.at[1]),
    ]
    for copy in copies:
        copy.start()
    row = lax.broadcasted_iota(jnp.int32, (feat_width, feat_width), 0)
    lane = lax.broadcasted_iota(jnp.int32, (feat_width, feat_width), 1)
    stacked = row // part
    away = jnp.where(stacked == 1, 2, jnp.where(stacked == 2, 1, stacked))
    order = (((me ^ away) * part + row % part) == lane).astype(BF16)
    step = loc // 4
    for c in range(4):
        for b in range(c * step, (c + 1) * step):
            stack = jnp.concatenate([mine[b], across[b], beside[b], opposite[b]], axis=0)
            turned[b * block : (b + 1) * block] = lax.dot_general(stack, order, ROWS_FIRST, preferred_element_type=F32)
        place = pl.ds(c * step * block, step * block)
        copies.append(pltpu.make_async_copy(turned.at[place], out.at[place], sems.at[2 + c]))
        copies[-1].start()
    for copy in copies:
        copy.wait()


def finish(mine, across, beside, opposite, grads, grads_came):
    loc, part, block = mine.shape
    feat_width = grads.shape[0] // 2
    weight = jax.ShapeDtypeStruct((feat_width, grads.shape[1]), F32)
    return pl.pallas_call(
        finish_kernel,
        out_shape=(jax.ShapeDtypeStruct((loc * block, feat_width), F32), weight, weight),
        in_specs=[WHOLE] * 6,
        out_specs=(FAR, FAR, FAR),
        scratch_shapes=[
            pltpu.VMEM((loc * block, feat_width), F32),
            pltpu.VMEM(grads.shape, F32),
            pltpu.SemaphoreType.DMA((6,)),
        ],
        compiler_params=params(8),
        cost_estimate=cost(loc * block * feat_width * feat_width * 2, 2 * MIB),
        name="finish",
    )(mine, across, beside, opposite, grads, grads_came)


def swap(x, axis, bit):
    return lax.ppermute(x, axis, [(i, i ^ bit) for i in range(lax.axis_size(axis))])


def shards(
    features,
    weight_self,
    weight_neigh,
    cotangent,
    inner_rows,
    inner_cols,
    inner_values,
    send_blocks,
    outer_rows,
    outer_values,
    live_count,
):
    peers = lax.axis_size("dom")
    feat_width = features.shape[1]
    inner_a, outer_a = inner_values[0], outer_values[0]
    targets = send_blocks.transpose(2, 0, 1)
    block = inner_a.shape[-1]

    outgoing = gather_halves(features, targets, block)
    own = lax.all_to_all(outgoing, "dom", split_axis=0, concat_axis=0, tiled=True)
    rows, cols, outer_rows, live, targets, total, over, outer_a = stage(
        inner_rows, inner_cols, outer_rows, live_count, targets, features, inner_a, outer_a
    )
    own, total = lax.optimization_barrier((own, total))
    other = swap(own, "grp", 1)
    layer_out, grads, send_n, keep_n, send_s, keep_s = layer(
        outer_rows, live, own, other, outer_a, total, over, features, cotangent, weight_self, weight_neigh
    )
    got_n = swap(send_n, "grp", 1)
    came_n = swap((keep_n[0].astype(F32) + got_n[0].astype(F32)).astype(BF16), "grp", 2)
    got_s = swap(send_s, "grp", 1)
    came_s = swap((keep_s[0].astype(F32) + got_s[0].astype(F32)).astype(BF16), "grp", 2)
    scaled, base, payload = outer_back(outer_rows, live, keep_n, got_n, came_n, keep_s, got_s, outer_a, peers)
    returned = lax.all_to_all(payload, "dom", split_axis=0, concat_axis=0, tiled=True)
    bit = peers // 2
    while bit > 4:
        grads = pair_sum(grads, swap(grads, "dom", bit))
        bit //= 2
    partial, grads = inner_back(rows, cols, scaled, base, inner_a, grads, swap(grads, "dom", 4))
    grads = pair_sum(grads, swap(grads, "dom", 2))
    mine = add_returned(targets, returned, came_s, partial)
    across = swap(mine, "grp", 2)
    beside = swap(mine, "grp", 1)
    opposite = swap(across, "grp", 1)
    feature_grad, self_grad, neigh_grad = finish(mine, across, beside, opposite, grads, swap(grads, "dom", 1))
    return layer_out, feature_grad, self_grad, neigh_grad


def solution(mesh):
    placed = (
        P("dom", None),
        P(None, "grp"),
        P(None, "grp"),
        P("dom", "grp"),
        P("dom", None),
        P("dom", None),
        P("dom", None, None, None),
        P("dom", None, None),
        P("dom", None),
        P("dom", None, None, None),
        P("dom", None),
    )
    return jax.shard_map(
        shards,
        mesh=mesh,
        in_specs=placed,
        out_specs=(P("dom", "grp"), P("dom", None), P(None, "grp"), P(None, "grp")),
        check_vma=False,
    )
```

```python
import functools

import jax
import jax.numpy as jnp
from jax import lax
from jax.experimental import pallas as pl
from jax.experimental.pallas import tpu as pltpu
from jax.sharding import PartitionSpec as P

F32 = jnp.float32
BF16 = jnp.bfloat16
MIB = 1 << 20
GROUP = 8
ROWS_LAST = (((1,), (1,)), ((), ()))
ROWS_FIRST = (((0,), (0,)), ((), ()))
WHOLE = pl.BlockSpec(memory_space=pltpu.VMEM)
SCALARS = pl.BlockSpec(memory_space=pltpu.SMEM)
FAR = pl.BlockSpec(memory_space=pltpu.HBM)


def dot(a, b):
    return jnp.dot(a, b, preferred_element_type=F32)


def far(*arrays):
    return [pltpu.with_memory_space_constraint(x, pltpu.HBM) for x in arrays]


def params(mib):
    return pltpu.CompilerParams(vmem_limit_bytes=int(mib * MIB))


def cost(flops, moved):
    return pl.CostEstimate(flops=int(flops), bytes_accessed=int(moved), transcendentals=0)


def gather_kernel(half, targets_far, feat_far, out, targets, feat, sems):
    fetches = [
        pltpu.make_async_copy(targets_far, targets, sems.at[0]),
        pltpu.make_async_copy(feat_far, feat, sems.at[1]),
    ]
    for fetch in fetches:
        fetch.start()
    for fetch in fetches:
        fetch.wait()
    slots, _, peers = targets.shape
    block = half * 2
    mine = lax.axis_index("grp") % 2
    for p in range(peers):
        for s in range(slots):
            start = pl.multiple_of(targets[s, 0, p] * block + mine * half, half)
            pltpu.make_async_copy(feat.at[pl.ds(start, half)], out.at[p, s], sems.at[2]).start()
    pltpu.make_async_copy(out, out, sems.at[2]).wait()


def gather_halves(features, targets, block):
    slots, _, peers = targets.shape
    return pl.pallas_call(
        functools.partial(gather_kernel, block // 2),
        out_shape=jax.ShapeDtypeStruct((peers, slots, block // 2, features.shape[1]), BF16),
        in_specs=[FAR, FAR],
        out_specs=FAR,
        scratch_shapes=[
            pltpu.SMEM(targets.shape, jnp.int32),
            pltpu.VMEM(features.shape, BF16),
            pltpu.SemaphoreType.DMA((3,)),
        ],
        compiler_params=params(4),
        name="gather_halves",
    )(*far(targets, features))


def stage_kernel(
    rows_far, cols_far, outer_rows_far, live_far, targets_far, feat_far, inner_far, outer_far,
    rows, cols, outer_rows, live, targets, total, over, over_rows,
    feat, inner, outer, wide, degree_rows, sems, inner_sems,
):
    loc, block, feat_width = total.shape
    count, outer_count = inner.shape[0], outer.shape[0]
    slots, _, peers = targets.shape
    scalars = [
        pltpu.make_async_copy(source, place, sems.at[k])
        for k, (source, place) in enumerate((
            (rows_far, rows), (cols_far, cols), (outer_rows_far, outer_rows), (live_far, live), (targets_far, targets),
        ))
    ]
    tables = [
        pltpu.make_async_copy(source, place, sems.at[5 + k])
        for k, (source, place) in enumerate((
            (feat_far, feat), (outer_far, outer),
        ))
    ]
    groups = count // GROUP
    blocks = [
        pltpu.make_async_copy(
            inner_far.at[pl.ds(g * GROUP, GROUP)], inner.at[pl.ds(g * GROUP, GROUP)], inner_sems.at[g]
        )
        for g in range(groups)
    ]
    for copy in scalars + tables[:1] + blocks + tables[1:]:
        copy.start()
    for copy in scalars + tables[:1]:
        copy.wait()
    x = feat[...].reshape(loc, block, feat_width)
    wide[:, :, :feat_width] = x
    wide[:, :, feat_width:] = jnp.ones((loc, block, feat_width), BF16)
    total[...] = x.astype(F32)
    over[...] = jnp.ones((loc, block, feat_width), F32)
    degree_rows[...] = jnp.ones(degree_rows.shape, F32)
    few = jnp.ones((degree_rows.shape[1], block), BF16)
    for g in range(groups):
        blocks[g].wait()
        products = [dot(inner[g * GROUP + k], wide[cols[0, g * GROUP + k]]) for k in range(GROUP)]
        flat = [
            lax.dot_general(few, inner[g * GROUP + k], ROWS_LAST, preferred_element_type=F32) for k in range(GROUP)
        ]
        for k in range(GROUP):
            r = rows[0, g * GROUP + k]
            total[r] += products[k][:, :feat_width]
            over[r] += products[k][:, feat_width:]
            degree_rows[r] += flat[k]
    for copy in tables[1:]:
        copy.wait()

    def some(g, _):
        ones = jnp.ones((block, feat_width), BF16)
        products = [dot(outer[g * GROUP + k], ones) for k in range(GROUP)]
        flat = [
            lax.dot_general(few, outer[g * GROUP + k], ROWS_LAST, preferred_element_type=F32) for k in range(GROUP)
        ]
        for k in range(GROUP):
            n = g * GROUP + k
            alive = (n % slots < live[0, n // slots]).astype(F32)
            over[outer_rows[0, n]] += products[k] * alive
            degree_rows[outer_rows[0, n]] += flat[k] * alive
        return 0

    lax.fori_loop(0, outer_count // GROUP, some, 0)
    over[...] = 1.0 / over[...]
    over_rows[...] = 1.0 / degree_rows[...]


def stage(rows, cols, outer_rows, live, targets, features, inner, outer):
    count, block, _ = inner.shape
    nodes, feat_width = features.shape
    loc = nodes // block
    scalars = (rows, cols, outer_rows, live, targets)
    sums = (loc, block, feat_width)
    return pl.pallas_call(
        stage_kernel,
        out_shape=tuple(pltpu.SMEM(x.shape, jnp.int32) for x in scalars)
        + (pltpu.VMEM(sums, F32), pltpu.VMEM(sums, F32), pltpu.VMEM((loc, 8, block), F32)),
        in_specs=[FAR] * 8,
        out_specs=(SCALARS,) * 5 + (WHOLE,) * 3,
        scratch_shapes=[
            pltpu.VMEM(features.shape, BF16),
            pltpu.VMEM(inner.shape, BF16),
            pltpu.VMEM(outer.shape, BF16),
            pltpu.VMEM((loc, block, 2 * feat_width), BF16),
            pltpu.VMEM((loc, 8, block), F32),
            pltpu.SemaphoreType.DMA((7,)),
            pltpu.SemaphoreType.DMA((count // GROUP,)),
        ],
        compiler_params=params(12 + outer.size * 2 / MIB),
        cost_estimate=cost(count * block * block * feat_width * 4, 6 * MIB),
        name="stage",
    )(*far(*scalars, features, inner, outer))


def fetch_kernel(
    outer_far, feat_far, cot_far, self_far, neigh_far, outer, feat, cot, weights, turned, w_self, w_neigh, sems
):
    feat_width = feat.shape[1]
    part = feat_width // lax.axis_size("grp")
    me = lax.axis_index("grp")
    fetches = [
        pltpu.make_async_copy(source, place, sems.at[k])
        for k, (source, place) in enumerate((
            (self_far, w_self), (neigh_far, w_neigh), (outer_far, outer), (feat_far, feat), (cot_far, cot),
        ))
    ]
    for fetch in fetches:
        fetch.start()
    for fetch in fetches[:2]:
        fetch.wait()
    weights[:feat_width] = w_self[...] * 0.5
    weights[feat_width:] = w_neigh[...] * 0.5
    for spot, away in enumerate((3, 1, 2, 0)):
        start = pl.multiple_of((me ^ away) * part, part)
        turned[pl.ds(spot * part, part)] = w_self[pl.ds(start, part)] * 0.5
        turned[pl.ds(feat_width + spot * part, part)] = w_neigh[pl.ds(start, part)] * 0.5
    for fetch in fetches[2:]:
        fetch.wait()


def fetch(outer, features, cotangent, w_self, w_neigh):
    both = (2 * features.shape[1], w_self.shape[1])
    return pl.pallas_call(
        fetch_kernel,
        out_shape=tuple(pltpu.VMEM(shape, BF16) for shape in (outer.shape, features.shape, cotangent.shape, both, both)),
        in_specs=[FAR] * 5,
        out_specs=(WHOLE,) * 5,
        scratch_shapes=[
            pltpu.VMEM(w_self.shape, BF16),
            pltpu.VMEM(w_neigh.shape, BF16),
            pltpu.SemaphoreType.DMA((5,)),
        ],
        compiler_params=params(8 + outer.size * 2 / MIB),
        cost_estimate=cost(1e6, 3 * MIB),
        name="fetch",
    )(*far(outer, features, cotangent, w_self, w_neigh))


def layer_kernel(
    chunk_blocks,
    outer_rows, live, own, other, outer, total_in, over_all, over_rows, feat, cot, weights, turned,
    layer_out, grads, send_n, keep_n, send_s, keep_s, total,
    smooth, grad_sum, out_sems,
):
    del total_in
    peers, slots, half, feat_width = own.shape
    count, block, _ = outer.shape
    loc = total.shape[0]
    chunks = loc // chunk_blocks
    rows = chunk_blocks * block
    part = feat_width // lax.axis_size("grp")
    mine = lax.axis_index("grp") % 2

    def some(g, _):
        products = []
        for k in range(GROUP):
            n = g * GROUP + k
            near, away = own[n // slots, n % slots], other[n // slots, n % slots]
            x = jnp.concatenate([jnp.where(mine == 0, near, away), jnp.where(mine == 0, away, near)], axis=0)
            products.append(dot(outer[n], x))
        for k in range(GROUP):
            n = g * GROUP + k
            alive = (n % slots < live[0, n // slots]).astype(F32)
            total[outer_rows[0, n]] += products[k] * alive
        return 0

    lax.fori_loop(0, count // GROUP, some, 0)
    leaving = []
    for c in range(chunks):
        place = pl.ds(c * rows, rows)
        here = pl.ds(c * chunk_blocks, chunk_blocks)
        over = over_all[here].reshape(rows, feat_width)
        agg = (total[here].reshape(rows, feat_width) * over).astype(BF16)
        both = jnp.concatenate([feat[place], agg], axis=1)
        pre = dot(both, weights[...])
        bent = jnp.tanh(pre)
        twice = 1.0 + bent
        silu = pre * twice
        smooth[place] = silu.astype(BF16)
        leaving.append(pltpu.make_async_copy(smooth.at[place], layer_out.at[place], out_sems.at[c]))
        leaving[-1].start()
        grad_pre = (cot[place].astype(F32) * (twice + silu * (1.0 - bent))).astype(BF16)
        grown = lax.dot_general(both, grad_pre, ROWS_FIRST, preferred_element_type=F32)
        if c == 0:
            grad_sum[...] = grown
        elif c < chunks - 1:
            grad_sum[...] += grown
        else:
            grads[...] = (0.5 * (grad_sum[...] + grown)).astype(BF16)
        back = lax.dot_general(turned[...], grad_pre, ROWS_LAST, preferred_element_type=F32)
        for b in range(chunk_blocks):
            at = c * chunk_blocks + b
            lanes = slice(b * block, (b + 1) * block)
            self_t = back[:feat_width, lanes].astype(BF16)
            neigh_t = (back[feat_width:, lanes] * over_rows[at, :1]).astype(BF16)
            for y in range(2):
                send_n[y, at] = neigh_t[y * part : (y + 1) * part]
                keep_n[y, at] = neigh_t[(2 + y) * part : (3 + y) * part]
                send_s[y, at] = self_t[y * part : (y + 1) * part]
                keep_s[y, at] = self_t[(2 + y) * part : (3 + y) * part]
    for copy in leaving:
        copy.wait()


def layer(outer_rows, live, own, other, outer, total, over, over_rows, features, cotangent, weights, turned):
    feat_width = features.shape[1]
    loc, block, _ = total.shape
    chunk = 4
    grads = weights.shape
    part = feat_width // lax.axis_size("grp")
    piece = pltpu.VMEM((2, loc, part, block), BF16)
    return pl.pallas_call(
        functools.partial(layer_kernel, chunk),
        out_shape=(
            jax.ShapeDtypeStruct(cotangent.shape, BF16),
            pltpu.VMEM(grads, BF16),
            piece, piece, piece, piece,
            pltpu.VMEM(total.shape, F32),
        ),
        in_specs=[SCALARS] * 2 + [WHOLE] * 10,
        out_specs=(FAR,) + (WHOLE,) * 6,
        input_output_aliases={5: 6},
        scratch_shapes=[
            pltpu.VMEM(cotangent.shape, BF16),
            pltpu.VMEM(grads, F32),
            pltpu.SemaphoreType.DMA((loc // chunk,)),
        ],
        compiler_params=params(16 + 4 * own.size * 2 / MIB),
        cost_estimate=cost(1.2e9, 8 * MIB),
        name="layer",
    )(outer_rows, live, own, other, outer, total, over, over_rows, features, cotangent, weights, turned)[:6]


def outer_back_kernel(outer_rows, live, keep, got, came, keep_s, got_s, outer, scaled, base, payload):
    peers, slots, part, block = payload.shape
    near = (keep[1].astype(F32) + got[1].astype(F32) + came[...].astype(F32)).astype(BF16)
    scaled[...] = near
    base[...] = near.astype(F32) + keep_s[1].astype(F32) + got_s[1].astype(F32)

    def some(g, _):
        products = []
        for k in range(GROUP):
            n = g * GROUP + k
            products.append(dot(scaled[outer_rows[0, n]], outer[n]))
        for k in range(GROUP):
            n = g * GROUP + k
            alive = (n % slots < live[0, n // slots]).astype(F32)
            payload[n // slots, n % slots] = (products[k] * alive).astype(BF16)
        return 0

    lax.fori_loop(0, outer.shape[0] // GROUP, some, 0)


def outer_back(outer_rows, live, keep, got, came, keep_s, got_s, outer, peers):
    loc, part, block = came.shape
    count = outer.shape[0]
    return pl.pallas_call(
        outer_back_kernel,
        out_shape=(
            pltpu.VMEM((loc, part, block), BF16),
            pltpu.VMEM((loc, part, block), F32),
            jax.ShapeDtypeStruct((peers, count // peers, part, block), BF16),
        ),
        in_specs=[SCALARS, SCALARS] + [WHOLE] * 6,
        out_specs=(WHOLE, WHOLE, WHOLE),
        compiler_params=params(8 + count * block * (block + part) * 2 / MIB),
        cost_estimate=cost(count * block * block * part * 2, 2 * MIB),
        name="outer_back",
    )(outer_rows, live, keep, got, came, keep_s, got_s, outer)


def inner_back_kernel(rows, cols, scaled, base, inner_far, came, total, inner, sems):
    groups = inner.shape[0] // GROUP
    blocks = [
        pltpu.make_async_copy(inner_far.at[pl.ds(g * GROUP, GROUP)], inner.at[pl.ds(g * GROUP, GROUP)], sems.at[g])
        for g in range(groups)
    ]
    for copy in blocks:
        copy.start()
    total[...] = base[...] + came[...].astype(F32)
    for g in range(groups):
        blocks[g].wait()
        products = [dot(scaled[rows[0, g * GROUP + k]], inner[g * GROUP + k]) for k in range(GROUP)]
        for k in range(GROUP):
            total[cols[0, g * GROUP + k]] += products[k]


def inner_back(rows, cols, scaled, base, inner, came):
    count, block, _ = inner.shape
    return pl.pallas_call(
        inner_back_kernel,
        out_shape=pltpu.VMEM(base.shape, F32),
        in_specs=[SCALARS, SCALARS, WHOLE, WHOLE, FAR, WHOLE],
        out_specs=WHOLE,
        scratch_shapes=[pltpu.VMEM(inner.shape, BF16), pltpu.SemaphoreType.DMA((count // GROUP,))],
        compiler_params=params(8),
        cost_estimate=cost(count * block * block * scaled.shape[1] * 2, 3 * MIB),
        name="inner_back",
    )(rows, cols, scaled, base, *far(inner), came)


def add_returned_kernel(targets, returned, total, out, summed):
    peers, slots, _, _ = returned.shape
    summed[...] = total[...]

    def some(q, _):
        for s in range(slots):
            summed[targets[s, 0, q]] += returned[q, s].astype(F32)
        return 0

    lax.fori_loop(0, peers, some, 0)
    out[...] = summed[...].astype(BF16)


def add_returned(targets, returned, total):
    return pl.pallas_call(
        add_returned_kernel,
        out_shape=pltpu.VMEM(total.shape, BF16),
        in_specs=[SCALARS, WHOLE, WHOLE],
        out_specs=WHOLE,
        scratch_shapes=[pltpu.VMEM(total.shape, F32)],
        compiler_params=params(8 + returned.size * 2 / MIB),
        cost_estimate=cost(total.size * 8, 2 * MIB),
        name="add_returned",
    )(targets, returned, total)


def pair_sum_kernel(a, b, out):
    out[...] = (a[...].astype(F32) + b[...].astype(F32)).astype(BF16)


def pair_sum(a, b):
    return pl.pallas_call(
        pair_sum_kernel,
        out_shape=jax.ShapeDtypeStruct(a.shape, BF16),
        in_specs=[WHOLE, WHOLE],
        out_specs=WHOLE,
        compiler_params=params(4),
        cost_estimate=cost(a.size * 2, a.size * 6),
        name="pair_sum",
    )(a, b)


def finish_kernel(mine, across, beside, opposite, grads, grads_came, out, self_out, neigh_out, turned, summed, sems):
    loc, part, block = mine.shape
    me = lax.axis_index("grp")
    feat_width = turned.shape[1]
    summed[...] = grads[...].astype(F32) + grads_came[...].astype(F32)
    copies = [
        pltpu.make_async_copy(summed.at[pl.ds(0, feat_width)], self_out, sems.at[0]),
        pltpu.make_async_copy(summed.at[pl.ds(feat_width, feat_width)], neigh_out, sems.at[1]),
    ]
    for copy in copies:
        copy.start()
    row = lax.broadcasted_iota(jnp.int32, (feat_width, feat_width), 0)
    lane = lax.broadcasted_iota(jnp.int32, (feat_width, feat_width), 1)
    stacked = row // part
    away = jnp.where(stacked == 1, 2, jnp.where(stacked == 2, 1, stacked))
    order = (((me ^ away) * part + row % part) == lane).astype(BF16)
    step = loc // 4
    for c in range(4):
        for b in range(c * step, (c + 1) * step):
            stack = jnp.concatenate([mine[b], across[b], beside[b], opposite[b]], axis=0)
            turned[b * block : (b + 1) * block] = lax.dot_general(stack, order, ROWS_FIRST, preferred_element_type=F32)
        place = pl.ds(c * step * block, step * block)
        copies.append(pltpu.make_async_copy(turned.at[place], out.at[place], sems.at[2 + c]))
        copies[-1].start()
    for copy in copies:
        copy.wait()


def finish(mine, across, beside, opposite, grads, grads_came):
    loc, part, block = mine.shape
    feat_width = grads.shape[0] // 2
    weight = jax.ShapeDtypeStruct((feat_width, grads.shape[1]), F32)
    return pl.pallas_call(
        finish_kernel,
        out_shape=(jax.ShapeDtypeStruct((loc * block, feat_width), F32), weight, weight),
        in_specs=[WHOLE] * 6,
        out_specs=(FAR, FAR, FAR),
        scratch_shapes=[
            pltpu.VMEM((loc * block, feat_width), F32),
            pltpu.VMEM(grads.shape, F32),
            pltpu.SemaphoreType.DMA((6,)),
        ],
        compiler_params=params(8),
        cost_estimate=cost(loc * block * feat_width * feat_width * 2, 2 * MIB),
        name="finish",
    )(mine, across, beside, opposite, grads, grads_came)


def swap(x, axis, bit):
    return lax.ppermute(x, axis, [(i, i ^ bit) for i in range(lax.axis_size(axis))])


def shards(
    features,
    weight_self,
    weight_neigh,
    cotangent,
    inner_rows,
    inner_cols,
    inner_values,
    send_blocks,
    outer_rows,
    outer_values,
    live_count,
):
    peers = lax.axis_size("dom")
    feat_width = features.shape[1]
    inner_a, outer_a = inner_values[0], outer_values[0]
    targets = send_blocks.transpose(2, 0, 1)
    block = inner_a.shape[-1]

    outgoing = gather_halves(features, targets, block)
    own = lax.all_to_all(outgoing, "dom", split_axis=0, concat_axis=0, tiled=True)
    rows, cols, outer_rows, live, targets, total, over, over_rows = stage(
        inner_rows, inner_cols, outer_rows, live_count, targets, features, inner_a, outer_a
    )
    own, total, outer_a = lax.optimization_barrier((own, total, outer_a))
    other = swap(own, "grp", 1)
    outer_a, features, cotangent, weights, turned = fetch(outer_a, features, cotangent, weight_self, weight_neigh)
    layer_out, grads, send_n, keep_n, send_s, keep_s = layer(
        outer_rows, live, own, other, outer_a, total, over, over_rows, features, cotangent, weights, turned
    )
    got_n = swap(send_n, "grp", 1)
    came_n = swap((keep_n[0].astype(F32) + got_n[0].astype(F32)).astype(BF16), "grp", 2)
    got_s = swap(send_s, "grp", 1)
    came_s = swap((keep_s[0].astype(F32) + got_s[0].astype(F32)).astype(BF16), "grp", 2)
    scaled, base, payload = outer_back(outer_rows, live, keep_n, got_n, came_n, keep_s, got_s, outer_a, peers)
    returned = lax.all_to_all(payload, "dom", split_axis=0, concat_axis=0, tiled=True)
    bit = peers // 2
    while bit > 2:
        grads = pair_sum(grads, swap(grads, "dom", bit))
        bit //= 2
    base, grads = lax.optimization_barrier((base, grads))
    partial = inner_back(rows, cols, scaled, base, inner_a, came_s)
    grads = pair_sum(grads, swap(grads, "dom", 2))
    mine = add_returned(targets, returned, partial)
    across = swap(mine, "grp", 2)
    beside = swap(mine, "grp", 1)
    opposite = swap(across, "grp", 1)
    feature_grad, self_grad, neigh_grad = finish(mine, across, beside, opposite, grads, swap(grads, "dom", 1))
    return layer_out, feature_grad, self_grad, neigh_grad


def solution(mesh):
    placed = (
        P("dom", None),
        P(None, "grp"),
        P(None, "grp"),
        P("dom", "grp"),
        P("dom", None),
        P("dom", None),
        P("dom", None, None, None),
        P("dom", None, None),
        P("dom", None),
        P("dom", None, None, None),
        P("dom", None),
    )
    return jax.shard_map(
        shards,
        mesh=mesh,
        in_specs=placed,
        out_specs=(P("dom", "grp"), P("dom", None), P(None, "grp"), P(None, "grp")),
        check_vma=False,
    )
```

```python
import functools

import jax
import jax.numpy as jnp
from jax import lax
from jax.experimental import pallas as pl
from jax.experimental.pallas import tpu as pltpu
from jax.sharding import PartitionSpec as P

F32 = jnp.float32
BF16 = jnp.bfloat16
MIB = 1 << 20
GROUP = 8
ROWS_LAST = (((1,), (1,)), ((), ()))
ROWS_FIRST = (((0,), (0,)), ((), ()))
WHOLE = pl.BlockSpec(memory_space=pltpu.VMEM)
SCALARS = pl.BlockSpec(memory_space=pltpu.SMEM)
FAR = pl.BlockSpec(memory_space=pltpu.HBM)


def dot(a, b):
    return jnp.dot(a, b, preferred_element_type=F32)


def far(*arrays):
    return [pltpu.with_memory_space_constraint(x, pltpu.HBM) for x in arrays]


def group_of(count, slots):
    return slots * max(k for k in range(1, 9) if count // slots % k == 0)


def for_groups(count, body):
    if count == 1:
        body(0, 0)
    else:
        lax.fori_loop(0, count, body, 0)


def params(mib):
    return pltpu.CompilerParams(vmem_limit_bytes=int(mib * MIB))


def cost(flops, moved):
    return pl.CostEstimate(flops=int(flops), bytes_accessed=int(moved), transcendentals=0)


def gather_kernel(targets_far, feat_far, out, targets, feat, outgoing, sems, out_sem):
    pieces = sems.shape[0] - 1
    step = feat.shape[0] // pieces
    mine = lax.axis_index("grp") % 2
    fetches = [pltpu.make_async_copy(targets_far, targets, sems.at[pieces])]
    for k in range(pieces):
        place = pl.ds(k * step, step)
        fetches.append(pltpu.make_async_copy(feat_far.at[place, pl.ds(mine, 1)], feat.at[place], sems.at[k]))
    for fetch in fetches:
        fetch.start()
    for fetch in fetches:
        fetch.wait()
    slots, _, peers = targets.shape
    for p in range(peers):
        for s in range(slots):
            outgoing[p, s] = feat[targets[s, 0, p], 0]
        pltpu.make_async_copy(outgoing.at[p], out.at[p], out_sem).start()
    pltpu.make_async_copy(outgoing, out, out_sem).wait()


def gather_halves(features, targets, block):
    nodes, feat_width = features.shape
    loc, half = nodes // block, block // 2
    slots, _, peers = targets.shape
    return pl.pallas_call(
        gather_kernel,
        out_shape=jax.ShapeDtypeStruct((peers, slots, half, feat_width), BF16),
        in_specs=[FAR, FAR],
        out_specs=FAR,
        scratch_shapes=[
            pltpu.SMEM(targets.shape, jnp.int32),
            pltpu.VMEM((loc, 1, half, feat_width), BF16),
            pltpu.VMEM((peers, slots, half, feat_width), BF16),
            pltpu.SemaphoreType.DMA((5,)),
            pltpu.SemaphoreType.DMA,
        ],
        compiler_params=params(4 + 2 * peers * slots * half * feat_width / MIB),
        name="gather_halves",
    )(*far(targets, features.reshape(loc, 2, half, feat_width)))


def stage_kernel(
    rows_far, cols_far, outer_rows_far, live_far, targets_far, feat_far, inner_far, outer_far,
    rows, cols, outer_rows, live, targets, total, over, over_rows,
    feat, inner, outer, wide, degree_rows, sems, inner_sems,
):
    loc, block, feat_width = total.shape
    count, outer_count = inner.shape[0], outer.shape[0]
    slots, _, peers = targets.shape
    scalars = [
        pltpu.make_async_copy(source, place, sems.at[k])
        for k, (source, place) in enumerate((
            (rows_far, rows), (cols_far, cols), (outer_rows_far, outer_rows), (live_far, live), (targets_far, targets),
        ))
    ]
    tables = [
        pltpu.make_async_copy(source, place, sems.at[5 + k])
        for k, (source, place) in enumerate((
            (feat_far, feat), (outer_far, outer),
        ))
    ]
    groups = count // GROUP
    blocks = [
        pltpu.make_async_copy(
            inner_far.at[pl.ds(g * GROUP, GROUP)], inner.at[pl.ds(g * GROUP, GROUP)], inner_sems.at[g]
        )
        for g in range(groups)
    ]
    for copy in scalars + tables[:1] + blocks + tables[1:]:
        copy.start()
    for copy in scalars + tables[:1]:
        copy.wait()
    x = feat[...].reshape(loc, block, feat_width)
    wide[:, :, :feat_width] = x
    wide[:, :, feat_width:] = jnp.ones((loc, block, feat_width), BF16)
    total[...] = x.astype(F32)
    over[...] = jnp.ones((loc, block, feat_width), F32)
    degree_rows[...] = jnp.ones(degree_rows.shape, F32)
    few = jnp.ones((degree_rows.shape[1], block), BF16)
    for g in range(groups):
        blocks[g].wait()
        products = [dot(inner[g * GROUP + k], wide[cols[0, g * GROUP + k]]) for k in range(GROUP)]
        flat = [
            lax.dot_general(few, inner[g * GROUP + k], ROWS_LAST, preferred_element_type=F32) for k in range(GROUP)
        ]
        for k in range(GROUP):
            r = rows[0, g * GROUP + k]
            total[r] += products[k][:, :feat_width]
            over[r] += products[k][:, feat_width:]
            degree_rows[r] += flat[k]
    for copy in tables[1:]:
        copy.wait()

    def some(g, _):
        ones = jnp.ones((block, feat_width), BF16)
        products = [dot(outer[g * GROUP + k], ones) for k in range(GROUP)]
        flat = [
            lax.dot_general(few, outer[g * GROUP + k], ROWS_LAST, preferred_element_type=F32) for k in range(GROUP)
        ]
        for k in range(GROUP):
            n = g * GROUP + k
            alive = (n % slots < live[0, n // slots]).astype(F32)
            over[outer_rows[0, n]] += products[k] * alive
            degree_rows[outer_rows[0, n]] += flat[k] * alive
        return 0

    lax.fori_loop(0, outer_count // GROUP, some, 0)
    over[...] = 1.0 / over[...]
    over_rows[...] = 1.0 / degree_rows[...]


def stage(rows, cols, outer_rows, live, targets, features, inner, outer):
    count, block, _ = inner.shape
    nodes, feat_width = features.shape
    loc = nodes // block
    scalars = (rows, cols, outer_rows, live, targets)
    sums = (loc, block, feat_width)
    return pl.pallas_call(
        stage_kernel,
        out_shape=tuple(pltpu.SMEM(x.shape, jnp.int32) for x in scalars)
        + (pltpu.VMEM(sums, F32), pltpu.VMEM(sums, F32), pltpu.VMEM((loc, 8, block), F32)),
        in_specs=[FAR] * 8,
        out_specs=(SCALARS,) * 5 + (WHOLE,) * 3,
        scratch_shapes=[
            pltpu.VMEM(features.shape, BF16),
            pltpu.VMEM(inner.shape, BF16),
            pltpu.VMEM(outer.shape, BF16),
            pltpu.VMEM((loc, block, 2 * feat_width), BF16),
            pltpu.VMEM((loc, 8, block), F32),
            pltpu.SemaphoreType.DMA((7,)),
            pltpu.SemaphoreType.DMA((count // GROUP,)),
        ],
        compiler_params=params(12 + outer.size * 2 / MIB),
        cost_estimate=cost(count * block * block * feat_width * 4, 6 * MIB),
        name="stage",
    )(*far(*scalars, features, inner, outer))


def fetch_kernel(
    outer_far, feat_far, cot_far, self_far, neigh_far, outer, feat, cot, weights, turned, w_self, w_neigh, sems
):
    feat_width = feat.shape[1]
    part = feat_width // lax.axis_size("grp")
    me = lax.axis_index("grp")
    fetches = [
        pltpu.make_async_copy(source, place, sems.at[k])
        for k, (source, place) in enumerate((
            (self_far, w_self), (neigh_far, w_neigh), (outer_far, outer), (feat_far, feat), (cot_far, cot),
        ))
    ]
    for fetch in fetches:
        fetch.start()
    for fetch in fetches[:2]:
        fetch.wait()
    weights[:feat_width] = w_self[...] * 0.5
    weights[feat_width:] = w_neigh[...] * 0.5
    for spot, away in enumerate((3, 1, 2, 0)):
        start = pl.multiple_of((me ^ away) * part, part)
        turned[pl.ds(spot * part, part)] = w_self[pl.ds(start, part)] * 0.5
        turned[pl.ds(feat_width + spot * part, part)] = w_neigh[pl.ds(start, part)] * 0.5
    for fetch in fetches[2:]:
        fetch.wait()


def fetch(outer, features, cotangent, w_self, w_neigh):
    both = (2 * features.shape[1], w_self.shape[1])
    return pl.pallas_call(
        fetch_kernel,
        out_shape=tuple(pltpu.VMEM(shape, BF16) for shape in (outer.shape, features.shape, cotangent.shape, both, both)),
        in_specs=[FAR] * 5,
        out_specs=(WHOLE,) * 5,
        scratch_shapes=[
            pltpu.VMEM(w_self.shape, BF16),
            pltpu.VMEM(w_neigh.shape, BF16),
            pltpu.SemaphoreType.DMA((5,)),
        ],
        compiler_params=params(8 + outer.size * 2 / MIB),
        cost_estimate=cost(1e6, 3 * MIB),
        name="fetch",
    )(*far(outer, features, cotangent, w_self, w_neigh))


def layer_kernel(
    chunk_blocks,
    outer_rows, live, own, other, outer, total_in, over_all, over_rows, feat, cot, weights, turned,
    smooth, grad_pre_all, both_all, send_n, keep_n, send_s, keep_s, total,
):
    del total_in
    peers, slots, half, feat_width = own.shape
    count, block, _ = outer.shape
    loc = total.shape[0]
    chunks = loc // chunk_blocks
    rows = chunk_blocks * block
    part = feat_width // lax.axis_size("grp")
    mine = lax.axis_index("grp") % 2
    group = group_of(count, slots)

    def some(g, _):
        products = []
        for k in range(group):
            n = g * group + k
            near, away = own[n // slots, n % slots], other[n // slots, n % slots]
            x = jnp.concatenate([jnp.where(mine == 0, near, away), jnp.where(mine == 0, away, near)], axis=0)
            products.append(dot(outer[n], x))
        for k in range(group):
            n = g * group + k
            alive = (n % slots < live[0, n // slots]).astype(F32)
            total[outer_rows[0, n]] += products[k] * alive
        return 0

    for_groups(count // group, some)
    for c in range(chunks):
        place = pl.ds(c * rows, rows)
        here = pl.ds(c * chunk_blocks, chunk_blocks)
        over = over_all[here].reshape(rows, feat_width)
        agg = (total[here].reshape(rows, feat_width) * over).astype(BF16)
        both = jnp.concatenate([feat[place], agg], axis=1)
        pre = dot(both, weights[...])
        bent = jnp.tanh(pre)
        twice = 1.0 + bent
        silu = pre * twice
        smooth[place] = silu.astype(BF16)
        grad_pre = (cot[place].astype(F32) * (twice + silu * (1.0 - bent))).astype(BF16)
        grad_pre_all[place] = grad_pre
        both_all[place] = both
        back = lax.dot_general(turned[...], grad_pre, ROWS_LAST, preferred_element_type=F32)
        for b in range(chunk_blocks):
            at = c * chunk_blocks + b
            lanes = slice(b * block, (b + 1) * block)
            self_t = back[:feat_width, lanes].astype(BF16)
            neigh_t = (back[feat_width:, lanes] * over_rows[at, :1]).astype(BF16)
            for y in range(2):
                send_n[y, at] = neigh_t[y * part : (y + 1) * part]
                keep_n[y, at] = neigh_t[(2 + y) * part : (3 + y) * part]
                send_s[y, at] = self_t[y * part : (y + 1) * part]
                keep_s[y, at] = self_t[(2 + y) * part : (3 + y) * part]


def layer(outer_rows, live, own, other, outer, total, over, over_rows, features, cotangent, weights, turned):
    feat_width = features.shape[1]
    loc, block, _ = total.shape
    chunk = 4
    part = feat_width // lax.axis_size("grp")
    piece = pltpu.VMEM((2, loc, part, block), BF16)
    return pl.pallas_call(
        functools.partial(layer_kernel, chunk),
        out_shape=(
            pltpu.VMEM(cotangent.shape, BF16),
            pltpu.VMEM(cotangent.shape, BF16),
            pltpu.VMEM((cotangent.shape[0], 2 * feat_width), BF16),
            piece, piece, piece, piece,
            pltpu.VMEM(total.shape, F32),
        ),
        in_specs=[SCALARS] * 2 + [WHOLE] * 10,
        out_specs=(WHOLE,) * 8,
        input_output_aliases={5: 7},
        compiler_params=params(16 + 4 * own.size * 2 / MIB),
        cost_estimate=cost(1.2e9, 8 * MIB),
        name="layer",
    )(outer_rows, live, own, other, outer, total, over, over_rows, features, cotangent, weights, turned)[:7]


def weight_grads_kernel(smooth, grad_pre, both, layer_out, grads, sems):
    pieces = sems.shape[0]
    rows = smooth.shape[0] // pieces
    copies = [
        pltpu.make_async_copy(smooth.at[pl.ds(c * rows, rows)], layer_out.at[pl.ds(c * rows, rows)], sems.at[c])
        for c in range(pieces)
    ]
    for copy in copies:
        copy.start()
    grown = lax.dot_general(both[...], grad_pre[...], ROWS_FIRST, preferred_element_type=F32)
    grads[...] = (0.5 * grown).astype(BF16)
    for copy in copies:
        copy.wait()


def weight_grads(smooth, grad_pre, both):
    return pl.pallas_call(
        weight_grads_kernel,
        out_shape=(
            jax.ShapeDtypeStruct(smooth.shape, BF16),
            pltpu.VMEM((both.shape[1], grad_pre.shape[1]), BF16),
        ),
        in_specs=[WHOLE] * 3,
        out_specs=(FAR, WHOLE),
        scratch_shapes=[pltpu.SemaphoreType.DMA((4,))],
        compiler_params=params(12),
        cost_estimate=cost(2 * grad_pre.size * both.shape[1], 4 * MIB),
        name="weight_grads",
    )(smooth, grad_pre, both)


def outer_back_kernel(
    outer_rows, live, keep, got, came, keep_s, got_s, outer, scaled, base, payload_far, payload, sem
):
    peers, slots, part, block = payload.shape
    near = (keep[1].astype(F32) + got[1].astype(F32) + came[...].astype(F32)).astype(BF16)
    scaled[...] = near
    base[...] = near.astype(F32) + keep_s[1].astype(F32) + got_s[1].astype(F32)
    group = group_of(outer.shape[0], slots)

    def some(g, _):
        products = []
        for k in range(group):
            n = g * group + k
            products.append(dot(scaled[outer_rows[0, n]], outer[n]))
        for k in range(group):
            n = g * group + k
            alive = (n % slots < live[0, n // slots]).astype(F32)
            p = n // slots
            payload[p, n % slots] = (products[k] * alive).astype(BF16)
            if k % slots == slots - 1:
                pltpu.make_async_copy(payload.at[p], payload_far.at[p], sem).start()
        return 0

    for_groups(outer.shape[0] // group, some)
    pltpu.make_async_copy(payload, payload_far, sem).wait()


def outer_back(outer_rows, live, keep, got, came, keep_s, got_s, outer, peers):
    loc, part, block = came.shape
    count = outer.shape[0]
    return pl.pallas_call(
        outer_back_kernel,
        out_shape=(
            pltpu.VMEM((loc, part, block), BF16),
            pltpu.VMEM((loc, part, block), F32),
            jax.ShapeDtypeStruct((peers, count // peers, part, block), BF16),
        ),
        in_specs=[SCALARS, SCALARS] + [WHOLE] * 6,
        out_specs=(WHOLE, WHOLE, FAR),
        scratch_shapes=[pltpu.VMEM((peers, count // peers, part, block), BF16), pltpu.SemaphoreType.DMA],
        compiler_params=params(8 + count * block * (block + part) * 2 / MIB),
        cost_estimate=cost(count * block * block * part * 2, 2 * MIB),
        name="outer_back",
    )(outer_rows, live, keep, got, came, keep_s, got_s, outer)


def fetch_inner_kernel(inner_far, inner, sems):
    copies = [
        pltpu.make_async_copy(inner_far.at[pl.ds(g * GROUP, GROUP)], inner.at[pl.ds(g * GROUP, GROUP)], sems.at[g])
        for g in range(sems.shape[0])
    ]
    for copy in copies:
        copy.start()
    for copy in copies:
        copy.wait()


def fetch_inner(inner):
    return pl.pallas_call(
        fetch_inner_kernel,
        out_shape=pltpu.VMEM(inner.shape, BF16),
        in_specs=[FAR],
        out_specs=WHOLE,
        scratch_shapes=[pltpu.SemaphoreType.DMA((inner.shape[0] // GROUP,))],
        compiler_params=params(4),
        cost_estimate=cost(1e6, 2 * MIB),
        name="fetch_inner",
    )(*far(inner))


def inner_back_kernel(rows, cols, scaled, base, inner, came, total):
    total[...] = base[...] + came[...].astype(F32)
    for g in range(inner.shape[0] // GROUP):
        products = [dot(scaled[rows[0, g * GROUP + k]], inner[g * GROUP + k]) for k in range(GROUP)]
        for k in range(GROUP):
            total[cols[0, g * GROUP + k]] += products[k]


def inner_back(rows, cols, scaled, base, inner, came):
    count, block, _ = inner.shape
    return pl.pallas_call(
        inner_back_kernel,
        out_shape=pltpu.VMEM(base.shape, F32),
        in_specs=[SCALARS, SCALARS, WHOLE, WHOLE, WHOLE, WHOLE],
        out_specs=WHOLE,
        compiler_params=params(8),
        cost_estimate=cost(count * block * block * scaled.shape[1] * 2, 3 * MIB),
        name="inner_back",
    )(rows, cols, scaled, base, inner, came)


def add_returned_kernel(targets, returned, total, out, summed):
    peers, slots, _, _ = returned.shape
    summed[...] = total[...]

    def some(q, _):
        for s in range(slots):
            summed[targets[s, 0, q]] += returned[q, s].astype(F32)
        return 0

    lax.fori_loop(0, peers, some, 0)
    out[...] = summed[...].astype(BF16)


def add_returned(targets, returned, total):
    return pl.pallas_call(
        add_returned_kernel,
        out_shape=pltpu.VMEM(total.shape, BF16),
        in_specs=[SCALARS, WHOLE, WHOLE],
        out_specs=WHOLE,
        scratch_shapes=[pltpu.VMEM(total.shape, F32)],
        compiler_params=params(8 + returned.size * 2 / MIB),
        cost_estimate=cost(total.size * 8, 2 * MIB),
        name="add_returned",
    )(targets, returned, total)


def pair_sum_kernel(a, b, out):
    out[...] = (a[...].astype(F32) + b[...].astype(F32)).astype(BF16)


def pair_sum(a, b):
    return pl.pallas_call(
        pair_sum_kernel,
        out_shape=jax.ShapeDtypeStruct(a.shape, BF16),
        in_specs=[WHOLE, WHOLE],
        out_specs=WHOLE,
        compiler_params=params(4),
        cost_estimate=cost(a.size * 2, a.size * 6),
        name="pair_sum",
    )(a, b)


def finish_kernel(mine, across, beside, opposite, grads, grads_came, out, self_out, neigh_out, turned, summed, sems):
    loc, part, block = mine.shape
    me = lax.axis_index("grp")
    feat_width = turned.shape[1]
    summed[...] = grads[...].astype(F32) + grads_came[...].astype(F32)
    copies = [
        pltpu.make_async_copy(summed.at[pl.ds(0, feat_width)], self_out, sems.at[0]),
        pltpu.make_async_copy(summed.at[pl.ds(feat_width, feat_width)], neigh_out, sems.at[1]),
    ]
    for copy in copies:
        copy.start()
    row = lax.broadcasted_iota(jnp.int32, (feat_width, feat_width), 0)
    lane = lax.broadcasted_iota(jnp.int32, (feat_width, feat_width), 1)
    stacked = row // part
    away = jnp.where(stacked == 1, 2, jnp.where(stacked == 2, 1, stacked))
    order = (((me ^ away) * part + row % part) == lane).astype(BF16)
    step = loc // 4
    for c in range(4):
        for b in range(c * step, (c + 1) * step):
            stack = jnp.concatenate([mine[b], across[b], beside[b], opposite[b]], axis=0)
            turned[b * block : (b + 1) * block] = lax.dot_general(stack, order, ROWS_FIRST, preferred_element_type=F32)
        place = pl.ds(c * step * block, step * block)
        copies.append(pltpu.make_async_copy(turned.at[place], out.at[place], sems.at[2 + c]))
        copies[-1].start()
    for copy in copies:
        copy.wait()


def finish(mine, across, beside, opposite, grads, grads_came):
    loc, part, block = mine.shape
    feat_width = grads.shape[0] // 2
    weight = jax.ShapeDtypeStruct((feat_width, grads.shape[1]), F32)
    return pl.pallas_call(
        finish_kernel,
        out_shape=(jax.ShapeDtypeStruct((loc * block, feat_width), F32), weight, weight),
        in_specs=[WHOLE] * 6,
        out_specs=(FAR, FAR, FAR),
        scratch_shapes=[
            pltpu.VMEM((loc * block, feat_width), F32),
            pltpu.VMEM(grads.shape, F32),
            pltpu.SemaphoreType.DMA((6,)),
        ],
        compiler_params=params(8),
        cost_estimate=cost(loc * block * feat_width * feat_width * 2, 2 * MIB),
        name="finish",
    )(mine, across, beside, opposite, grads, grads_came)


def swap(x, axis, bit):
    return lax.ppermute(x, axis, [(i, i ^ bit) for i in range(lax.axis_size(axis))])


def shards(
    features,
    weight_self,
    weight_neigh,
    cotangent,
    inner_rows,
    inner_cols,
    inner_values,
    send_blocks,
    outer_rows,
    outer_values,
    live_count,
):
    peers = lax.axis_size("dom")
    feat_width = features.shape[1]
    inner_a, outer_a = inner_values[0], outer_values[0]
    targets = send_blocks.transpose(2, 0, 1)
    block = inner_a.shape[-1]

    outgoing = gather_halves(features, targets, block)
    own = lax.all_to_all(outgoing, "dom", split_axis=0, concat_axis=0, tiled=True)
    rows, cols, outer_rows, live, targets, total, over, over_rows = stage(
        inner_rows, inner_cols, outer_rows, live_count, targets, features, inner_a, outer_a
    )
    own, total, outer_a = lax.optimization_barrier((own, total, outer_a))
    other = swap(own, "grp", 1)
    outer_a, features, cotangent, weights, turned = fetch(outer_a, features, cotangent, weight_self, weight_neigh)
    smooth, grad_pre, both, send_n, keep_n, send_s, keep_s = layer(
        outer_rows, live, own, other, outer_a, total, over, over_rows, features, cotangent, weights, turned
    )
    layer_out, grads = weight_grads(smooth, grad_pre, both)
    got_n = swap(send_n, "grp", 1)
    got_n, grads = lax.optimization_barrier((got_n, grads))
    pass_n, inner_a = lax.optimization_barrier(
        ((keep_n[0].astype(F32) + got_n[0].astype(F32)).astype(BF16), inner_a)
    )
    came_n, inner_a = lax.optimization_barrier((swap(pass_n, "grp", 2), fetch_inner(inner_a)))
    got_s = swap(send_s, "grp", 1)
    came_s = swap((keep_s[0].astype(F32) + got_s[0].astype(F32)).astype(BF16), "grp", 2)
    scaled, base, payload = outer_back(outer_rows, live, keep_n, got_n, came_n, keep_s, got_s, outer_a, peers)
    returned = lax.all_to_all(payload, "dom", split_axis=0, concat_axis=0, tiled=True)
    bit = peers // 2
    while bit > 2:
        grads = pair_sum(grads, swap(grads, "dom", bit))
        bit //= 2
    base, grads = lax.optimization_barrier((base, grads))
    partial = inner_back(rows, cols, scaled, base, inner_a, came_s)
    grads = pair_sum(grads, swap(grads, "dom", 1))
    mine = add_returned(targets, returned, partial)
    across = swap(mine, "grp", 2)
    beside = swap(mine, "grp", 1)
    opposite = swap(across, "grp", 1)
    feature_grad, self_grad, neigh_grad = finish(mine, across, beside, opposite, grads, swap(grads, "dom", 2))
    return layer_out, feature_grad, self_grad, neigh_grad


def solution(mesh):
    placed = (
        P("dom", None),
        P(None, "grp"),
        P(None, "grp"),
        P("dom", "grp"),
        P("dom", None),
        P("dom", None),
        P("dom", None, None, None),
        P("dom", None, None),
        P("dom", None),
        P("dom", None, None, None),
        P("dom", None),
    )
    return jax.shard_map(
        shards,
        mesh=mesh,
        in_specs=placed,
        out_specs=(P("dom", "grp"), P("dom", None), P(None, "grp"), P(None, "grp")),
        check_vma=False,
    )
```

```python
import functools

import jax
import jax.numpy as jnp
from jax import lax
from jax.experimental import pallas as pl
from jax.experimental.pallas import tpu as pltpu
from jax.sharding import PartitionSpec as P

F32 = jnp.float32
BF16 = jnp.bfloat16
MIB = 1 << 20
GROUP = 8
ROWS_LAST = (((1,), (1,)), ((), ()))
ROWS_FIRST = (((0,), (0,)), ((), ()))
WHOLE = pl.BlockSpec(memory_space=pltpu.VMEM)
SCALARS = pl.BlockSpec(memory_space=pltpu.SMEM)
FAR = pl.BlockSpec(memory_space=pltpu.HBM)


def dot(a, b):
    return jnp.dot(a, b, preferred_element_type=F32)


def far(*arrays):
    return [pltpu.with_memory_space_constraint(x, pltpu.HBM) for x in arrays]


OUT_ORDER = (5, 7, 1, 4, 6, 3, 0, 2)
BACK_ORDER = (5, 7, 1, 4, 6, 3, 0, 2)


def order_of(order, peers):
    return order if len(order) == peers else tuple((j + peers // 2) % peers for j in range(peers))


def peer_at(order, j):
    return order[j] if isinstance(j, int) else lax.rem(j + len(order) // 2, len(order))


def exchange(x, order):
    return lax.all_to_all(x, "dom", split_axis=0, concat_axis=0, tiled=True, axis_index_groups=[list(order)])


def for_places(peers, body):
    together = max(k for k in range(1, 9) if peers % k == 0)
    if together == peers:
        body(range(peers))
    else:

        def some(g, _):
            body([g * together + k for k in range(together)])
            return 0

        lax.fori_loop(0, peers // together, some, 0)


def params(mib):
    return pltpu.CompilerParams(vmem_limit_bytes=int(mib * MIB))


def cost(flops, moved):
    return pl.CostEstimate(flops=int(flops), bytes_accessed=int(moved), transcendentals=0)


def gather_kernel(order, targets_far, feat_far, out, targets, feat, outgoing, sems, out_sem):
    pieces = sems.shape[0] - 1
    step = feat.shape[0] // pieces
    mine = lax.axis_index("grp") % 2
    fetches = [pltpu.make_async_copy(targets_far, targets, sems.at[pieces])]
    for k in range(pieces):
        place = pl.ds(k * step, step)
        fetches.append(pltpu.make_async_copy(feat_far.at[place, pl.ds(mine, 1)], feat.at[place], sems.at[k]))
    for fetch in fetches:
        fetch.start()
    for fetch in fetches:
        fetch.wait()
    slots = targets.shape[0]
    for j, p in enumerate(order):
        for s in range(slots):
            outgoing[j, s] = feat[targets[s, 0, p], 0]
        pltpu.make_async_copy(outgoing.at[j], out.at[j], out_sem).start()
    pltpu.make_async_copy(outgoing, out, out_sem).wait()


def gather_halves(features, targets, block, order):
    nodes, feat_width = features.shape
    loc, half = nodes // block, block // 2
    slots, _, peers = targets.shape
    return pl.pallas_call(
        functools.partial(gather_kernel, order),
        out_shape=jax.ShapeDtypeStruct((peers, slots, half, feat_width), BF16),
        in_specs=[FAR, FAR],
        out_specs=FAR,
        scratch_shapes=[
            pltpu.SMEM(targets.shape, jnp.int32),
            pltpu.VMEM((loc, 1, half, feat_width), BF16),
            pltpu.VMEM((peers, slots, half, feat_width), BF16),
            pltpu.SemaphoreType.DMA((5,)),
            pltpu.SemaphoreType.DMA,
        ],
        compiler_params=params(4 + 2 * peers * slots * half * feat_width / MIB),
        name="gather_halves",
    )(*far(targets, features.reshape(loc, 2, half, feat_width)))


def stage_kernel(
    rows_far, cols_far, outer_rows_far, live_far, targets_far, feat_far, inner_far, outer_far,
    rows, cols, outer_rows, live, targets, total, over, over_rows,
    feat, inner, outer, wide, degree_rows, sems, inner_sems,
):
    loc, block, feat_width = total.shape
    count, outer_count = inner.shape[0], outer.shape[0]
    slots, _, peers = targets.shape
    scalars = [
        pltpu.make_async_copy(source, place, sems.at[k])
        for k, (source, place) in enumerate((
            (rows_far, rows), (cols_far, cols), (outer_rows_far, outer_rows), (live_far, live), (targets_far, targets),
        ))
    ]
    tables = [
        pltpu.make_async_copy(source, place, sems.at[5 + k])
        for k, (source, place) in enumerate((
            (feat_far, feat), (outer_far, outer),
        ))
    ]
    groups = count // GROUP
    blocks = [
        pltpu.make_async_copy(
            inner_far.at[pl.ds(g * GROUP, GROUP)], inner.at[pl.ds(g * GROUP, GROUP)], inner_sems.at[g]
        )
        for g in range(groups)
    ]
    for copy in scalars + tables[:1] + blocks + tables[1:]:
        copy.start()
    for copy in scalars + tables[:1]:
        copy.wait()
    x = feat[...].reshape(loc, block, feat_width)
    wide[:, :, :feat_width] = x
    wide[:, :, feat_width:] = jnp.ones((loc, block, feat_width), BF16)
    total[...] = x.astype(F32)
    over[...] = jnp.ones((loc, block, feat_width), F32)
    degree_rows[...] = jnp.ones(degree_rows.shape, F32)
    few = jnp.ones((degree_rows.shape[1], block), BF16)
    for g in range(groups):
        blocks[g].wait()
        products = [dot(inner[g * GROUP + k], wide[cols[0, g * GROUP + k]]) for k in range(GROUP)]
        flat = [
            lax.dot_general(few, inner[g * GROUP + k], ROWS_LAST, preferred_element_type=F32) for k in range(GROUP)
        ]
        for k in range(GROUP):
            r = rows[0, g * GROUP + k]
            total[r] += products[k][:, :feat_width]
            over[r] += products[k][:, feat_width:]
            degree_rows[r] += flat[k]
    for copy in tables[1:]:
        copy.wait()

    def some(g, _):
        ones = jnp.ones((block, feat_width), BF16)
        products = [dot(outer[g * GROUP + k], ones) for k in range(GROUP)]
        flat = [
            lax.dot_general(few, outer[g * GROUP + k], ROWS_LAST, preferred_element_type=F32) for k in range(GROUP)
        ]
        for k in range(GROUP):
            n = g * GROUP + k
            alive = (n % slots < live[0, n // slots]).astype(F32)
            over[outer_rows[0, n]] += products[k] * alive
            degree_rows[outer_rows[0, n]] += flat[k] * alive
        return 0

    lax.fori_loop(0, outer_count // GROUP, some, 0)
    over[...] = 1.0 / over[...]
    over_rows[...] = 1.0 / degree_rows[...]


def stage(rows, cols, outer_rows, live, targets, features, inner, outer):
    count, block, _ = inner.shape
    nodes, feat_width = features.shape
    loc = nodes // block
    scalars = (rows, cols, outer_rows, live, targets)
    sums = (loc, block, feat_width)
    return pl.pallas_call(
        stage_kernel,
        out_shape=tuple(pltpu.SMEM(x.shape, jnp.int32) for x in scalars)
        + (pltpu.VMEM(sums, F32), pltpu.VMEM(sums, F32), pltpu.VMEM((loc, 8, block), F32)),
        in_specs=[FAR] * 8,
        out_specs=(SCALARS,) * 5 + (WHOLE,) * 3,
        scratch_shapes=[
            pltpu.VMEM(features.shape, BF16),
            pltpu.VMEM(inner.shape, BF16),
            pltpu.VMEM(outer.shape, BF16),
            pltpu.VMEM((loc, block, 2 * feat_width), BF16),
            pltpu.VMEM((loc, 8, block), F32),
            pltpu.SemaphoreType.DMA((7,)),
            pltpu.SemaphoreType.DMA((count // GROUP,)),
        ],
        compiler_params=params(12 + outer.size * 2 / MIB),
        cost_estimate=cost(count * block * block * feat_width * 4, 6 * MIB),
        name="stage",
    )(*far(*scalars, features, inner, outer))


def fetch_kernel(
    outer_far, feat_far, cot_far, self_far, neigh_far, outer, feat, cot, weights, turned, w_self, w_neigh, sems
):
    feat_width = feat.shape[1]
    part = feat_width // lax.axis_size("grp")
    me = lax.axis_index("grp")
    fetches = [
        pltpu.make_async_copy(source, place, sems.at[k])
        for k, (source, place) in enumerate((
            (self_far, w_self), (neigh_far, w_neigh), (outer_far, outer), (feat_far, feat), (cot_far, cot),
        ))
    ]
    for fetch in fetches:
        fetch.start()
    for fetch in fetches[:2]:
        fetch.wait()
    weights[:feat_width] = w_self[...] * 0.5
    weights[feat_width:] = w_neigh[...] * 0.5
    for spot, away in enumerate((3, 1, 2, 0)):
        start = pl.multiple_of((me ^ away) * part, part)
        turned[pl.ds(spot * part, part)] = w_self[pl.ds(start, part)] * 0.5
        turned[pl.ds(feat_width + spot * part, part)] = w_neigh[pl.ds(start, part)] * 0.5
    for fetch in fetches[2:]:
        fetch.wait()


def fetch(outer, features, cotangent, w_self, w_neigh):
    both = (2 * features.shape[1], w_self.shape[1])
    return pl.pallas_call(
        fetch_kernel,
        out_shape=tuple(pltpu.VMEM(shape, BF16) for shape in (outer.shape, features.shape, cotangent.shape, both, both)),
        in_specs=[FAR] * 5,
        out_specs=(WHOLE,) * 5,
        scratch_shapes=[
            pltpu.VMEM(w_self.shape, BF16),
            pltpu.VMEM(w_neigh.shape, BF16),
            pltpu.SemaphoreType.DMA((5,)),
        ],
        compiler_params=params(8 + outer.size * 2 / MIB),
        cost_estimate=cost(1e6, 3 * MIB),
        name="fetch",
    )(*far(outer, features, cotangent, w_self, w_neigh))


def layer_kernel(
    chunk_blocks, order,
    outer_rows, live, own, other, outer, total_in, over_all, over_rows, feat, cot, weights, turned,
    smooth, grad_pre_all, both_all, send_n, keep_n, send_s, keep_s, total,
):
    del total_in
    peers, slots, half, feat_width = own.shape
    count, block, _ = outer.shape
    loc = total.shape[0]
    chunks = loc // chunk_blocks
    rows = chunk_blocks * block
    part = feat_width // lax.axis_size("grp")
    mine = lax.axis_index("grp") % 2

    def some(places):
        blocks = [(j, k, peer_at(order, j) * slots + k) for j in places for k in range(slots)]
        products = []
        for j, k, n in blocks:
            near, away = own[j, k], other[j, k]
            x = jnp.concatenate([jnp.where(mine == 0, near, away), jnp.where(mine == 0, away, near)], axis=0)
            products.append(dot(outer[n], x))
        for (j, k, n), product in zip(blocks, products):
            alive = (k < live[0, peer_at(order, j)]).astype(F32)
            total[outer_rows[0, n]] += product * alive

    for_places(peers, some)
    for c in range(chunks):
        place = pl.ds(c * rows, rows)
        here = pl.ds(c * chunk_blocks, chunk_blocks)
        over = over_all[here].reshape(rows, feat_width)
        agg = (total[here].reshape(rows, feat_width) * over).astype(BF16)
        both = jnp.concatenate([feat[place], agg], axis=1)
        pre = dot(both, weights[...])
        bent = jnp.tanh(pre)
        twice = 1.0 + bent
        silu = pre * twice
        smooth[place] = silu.astype(BF16)
        grad_pre = (cot[place].astype(F32) * (twice + silu * (1.0 - bent))).astype(BF16)
        grad_pre_all[place] = grad_pre
        both_all[place] = both
        back = lax.dot_general(turned[...], grad_pre, ROWS_LAST, preferred_element_type=F32)
        for b in range(chunk_blocks):
            at = c * chunk_blocks + b
            lanes = slice(b * block, (b + 1) * block)
            self_t = back[:feat_width, lanes].astype(BF16)
            neigh_t = (back[feat_width:, lanes] * over_rows[at, :1]).astype(BF16)
            for y in range(2):
                send_n[y, at] = neigh_t[y * part : (y + 1) * part]
                keep_n[y, at] = neigh_t[(2 + y) * part : (3 + y) * part]
                send_s[y, at] = self_t[y * part : (y + 1) * part]
                keep_s[y, at] = self_t[(2 + y) * part : (3 + y) * part]


def layer(outer_rows, live, own, other, outer, total, over, over_rows, features, cotangent, weights, turned, order):
    feat_width = features.shape[1]
    loc, block, _ = total.shape
    chunk = 4
    part = feat_width // lax.axis_size("grp")
    piece = pltpu.VMEM((2, loc, part, block), BF16)
    return pl.pallas_call(
        functools.partial(layer_kernel, chunk, order),
        out_shape=(
            pltpu.VMEM(cotangent.shape, BF16),
            pltpu.VMEM(cotangent.shape, BF16),
            pltpu.VMEM((cotangent.shape[0], 2 * feat_width), BF16),
            piece, piece, piece, piece,
            pltpu.VMEM(total.shape, F32),
        ),
        in_specs=[SCALARS] * 2 + [WHOLE] * 10,
        out_specs=(WHOLE,) * 8,
        input_output_aliases={5: 7},
        compiler_params=params(16 + 4 * own.size * 2 / MIB),
        cost_estimate=cost(1.2e9, 8 * MIB),
        name="layer",
    )(outer_rows, live, own, other, outer, total, over, over_rows, features, cotangent, weights, turned)[:7]


def weight_grads_kernel(smooth, grad_pre, both, layer_out, grads, sems):
    pieces = sems.shape[0]
    rows = smooth.shape[0] // pieces
    copies = [
        pltpu.make_async_copy(smooth.at[pl.ds(c * rows, rows)], layer_out.at[pl.ds(c * rows, rows)], sems.at[c])
        for c in range(pieces)
    ]
    for copy in copies:
        copy.start()
    grown = lax.dot_general(both[...], grad_pre[...], ROWS_FIRST, preferred_element_type=F32)
    grads[...] = (0.5 * grown).astype(BF16)
    for copy in copies:
        copy.wait()


def weight_grads(smooth, grad_pre, both):
    return pl.pallas_call(
        weight_grads_kernel,
        out_shape=(
            jax.ShapeDtypeStruct(smooth.shape, BF16),
            pltpu.VMEM((both.shape[1], grad_pre.shape[1]), BF16),
        ),
        in_specs=[WHOLE] * 3,
        out_specs=(FAR, WHOLE),
        scratch_shapes=[pltpu.SemaphoreType.DMA((4,))],
        compiler_params=params(12),
        cost_estimate=cost(2 * grad_pre.size * both.shape[1], 4 * MIB),
        name="weight_grads",
    )(smooth, grad_pre, both)


def outer_back_kernel(
    order, outer_rows, live, keep, got, came, keep_s, got_s, outer, scaled, base, payload_far, payload, sem
):
    peers, slots, part, block = payload.shape
    near = (keep[1].astype(F32) + got[1].astype(F32) + came[...].astype(F32)).astype(BF16)
    scaled[...] = near
    base[...] = near.astype(F32) + keep_s[1].astype(F32) + got_s[1].astype(F32)

    def some(places):
        blocks = [(j, k, peer_at(order, j) * slots + k) for j in places for k in range(slots)]
        products = [dot(scaled[outer_rows[0, n]], outer[n]) for _, _, n in blocks]
        for (j, k, n), product in zip(blocks, products):
            alive = (k < live[0, peer_at(order, j)]).astype(F32)
            payload[j, k] = (product * alive).astype(BF16)
            if k == slots - 1:
                pltpu.make_async_copy(payload.at[j], payload_far.at[j], sem).start()

    for_places(peers, some)
    pltpu.make_async_copy(payload, payload_far, sem).wait()


def outer_back(outer_rows, live, keep, got, came, keep_s, got_s, outer, order):
    loc, part, block = came.shape
    count, peers = outer.shape[0], len(order)
    return pl.pallas_call(
        functools.partial(outer_back_kernel, order),
        out_shape=(
            pltpu.VMEM((loc, part, block), BF16),
            pltpu.VMEM((loc, part, block), F32),
            jax.ShapeDtypeStruct((peers, count // peers, part, block), BF16),
        ),
        in_specs=[SCALARS, SCALARS] + [WHOLE] * 6,
        out_specs=(WHOLE, WHOLE, FAR),
        scratch_shapes=[pltpu.VMEM((peers, count // peers, part, block), BF16), pltpu.SemaphoreType.DMA],
        compiler_params=params(8 + count * block * (block + part) * 2 / MIB),
        cost_estimate=cost(count * block * block * part * 2, 2 * MIB),
        name="outer_back",
    )(outer_rows, live, keep, got, came, keep_s, got_s, outer)


def inner_back_kernel(rows, cols, scaled, base, inner_far, total, inner, sems):
    groups = inner.shape[0] // GROUP
    blocks = [
        pltpu.make_async_copy(inner_far.at[pl.ds(g * GROUP, GROUP)], inner.at[pl.ds(g * GROUP, GROUP)], sems.at[g])
        for g in range(groups)
    ]
    for copy in blocks:
        copy.start()
    total[...] = base[...]
    for g in range(groups):
        blocks[g].wait()
        products = [dot(scaled[rows[0, g * GROUP + k]], inner[g * GROUP + k]) for k in range(GROUP)]
        for k in range(GROUP):
            total[cols[0, g * GROUP + k]] += products[k]


def inner_back(rows, cols, scaled, base, inner):
    count, block, _ = inner.shape
    return pl.pallas_call(
        inner_back_kernel,
        out_shape=pltpu.VMEM(base.shape, F32),
        in_specs=[SCALARS, SCALARS, WHOLE, WHOLE, FAR],
        out_specs=WHOLE,
        scratch_shapes=[pltpu.VMEM(inner.shape, BF16), pltpu.SemaphoreType.DMA((count // GROUP,))],
        compiler_params=params(8),
        cost_estimate=cost(count * block * block * scaled.shape[1] * 2, 3 * MIB),
        name="inner_back",
    )(rows, cols, scaled, base, *far(inner))


def add_came_kernel(total, came, out):
    out[...] = total[...] + came[...].astype(F32)


def add_came(total, came):
    return pl.pallas_call(
        add_came_kernel,
        out_shape=pltpu.VMEM(total.shape, F32),
        in_specs=[WHOLE, WHOLE],
        out_specs=WHOLE,
        compiler_params=params(4),
        cost_estimate=cost(total.size, total.size * 10),
        name="add_came",
    )(total, came)


def add_returned_kernel(order, targets, returned, total, out, summed):
    peers, slots, _, _ = returned.shape
    summed[...] = total[...]

    def some(places):
        for j in places:
            for k in range(slots):
                summed[targets[k, 0, peer_at(order, j)]] += returned[j, k].astype(F32)

    for_places(peers, some)
    out[...] = summed[...].astype(BF16)


def add_returned(targets, returned, total, order):
    return pl.pallas_call(
        functools.partial(add_returned_kernel, order),
        out_shape=pltpu.VMEM(total.shape, BF16),
        in_specs=[SCALARS, WHOLE, WHOLE],
        out_specs=WHOLE,
        scratch_shapes=[pltpu.VMEM(total.shape, F32)],
        compiler_params=params(8 + returned.size * 2 / MIB),
        cost_estimate=cost(total.size * 8, 2 * MIB),
        name="add_returned",
    )(targets, returned, total)


def pair_sum_kernel(a, b, out):
    out[...] = (a[...].astype(F32) + b[...].astype(F32)).astype(BF16)


def pair_sum(a, b):
    return pl.pallas_call(
        pair_sum_kernel,
        out_shape=jax.ShapeDtypeStruct(a.shape, BF16),
        in_specs=[WHOLE, WHOLE],
        out_specs=WHOLE,
        compiler_params=params(4),
        cost_estimate=cost(a.size * 2, a.size * 6),
        name="pair_sum",
    )(a, b)


def finish_kernel(mine, across, beside, opposite, grads, grads_came, out, self_out, neigh_out, turned, summed, sems):
    loc, part, block = mine.shape
    me = lax.axis_index("grp")
    feat_width = turned.shape[1]
    summed[...] = grads[...].astype(F32) + grads_came[...].astype(F32)
    copies = [
        pltpu.make_async_copy(summed.at[pl.ds(0, feat_width)], self_out, sems.at[0]),
        pltpu.make_async_copy(summed.at[pl.ds(feat_width, feat_width)], neigh_out, sems.at[1]),
    ]
    for copy in copies:
        copy.start()
    row = lax.broadcasted_iota(jnp.int32, (feat_width, feat_width), 0)
    lane = lax.broadcasted_iota(jnp.int32, (feat_width, feat_width), 1)
    stacked = row // part
    away = jnp.where(stacked == 1, 2, jnp.where(stacked == 2, 1, stacked))
    order = (((me ^ away) * part + row % part) == lane).astype(BF16)
    step = loc // 4
    for c in range(4):
        for b in range(c * step, (c + 1) * step):
            stack = jnp.concatenate([mine[b], across[b], beside[b], opposite[b]], axis=0)
            turned[b * block : (b + 1) * block] = lax.dot_general(stack, order, ROWS_FIRST, preferred_element_type=F32)
        place = pl.ds(c * step * block, step * block)
        copies.append(pltpu.make_async_copy(turned.at[place], out.at[place], sems.at[2 + c]))
        copies[-1].start()
    for copy in copies:
        copy.wait()


def finish(mine, across, beside, opposite, grads, grads_came):
    loc, part, block = mine.shape
    feat_width = grads.shape[0] // 2
    weight = jax.ShapeDtypeStruct((feat_width, grads.shape[1]), F32)
    return pl.pallas_call(
        finish_kernel,
        out_shape=(jax.ShapeDtypeStruct((loc * block, feat_width), F32), weight, weight),
        in_specs=[WHOLE] * 6,
        out_specs=(FAR, FAR, FAR),
        scratch_shapes=[
            pltpu.VMEM((loc * block, feat_width), F32),
            pltpu.VMEM(grads.shape, F32),
            pltpu.SemaphoreType.DMA((6,)),
        ],
        compiler_params=params(8),
        cost_estimate=cost(loc * block * feat_width * feat_width * 2, 2 * MIB),
        name="finish",
    )(mine, across, beside, opposite, grads, grads_came)


def swap(x, axis, bit):
    return lax.ppermute(x, axis, [(i, i ^ bit) for i in range(lax.axis_size(axis))])


def shards(
    features,
    weight_self,
    weight_neigh,
    cotangent,
    inner_rows,
    inner_cols,
    inner_values,
    send_blocks,
    outer_rows,
    outer_values,
    live_count,
):
    peers = lax.axis_size("dom")
    feat_width = features.shape[1]
    inner_a, outer_a = inner_values[0], outer_values[0]
    targets = send_blocks.transpose(2, 0, 1)
    block = inner_a.shape[-1]

    out_order, back_order = order_of(OUT_ORDER, peers), order_of(BACK_ORDER, peers)
    own = exchange(gather_halves(features, targets, block, out_order), out_order)
    rows, cols, outer_rows, live, targets, total, over, over_rows = stage(
        inner_rows, inner_cols, outer_rows, live_count, targets, features, inner_a, outer_a
    )
    own, total, outer_a = lax.optimization_barrier((own, total, outer_a))
    other = swap(own, "grp", 1)
    outer_a, features, cotangent, weights, turned = fetch(outer_a, features, cotangent, weight_self, weight_neigh)
    smooth, grad_pre, both, send_n, keep_n, send_s, keep_s = layer(
        outer_rows, live, own, other, outer_a, total, over, over_rows, features, cotangent, weights, turned, out_order
    )
    layer_out, grads = weight_grads(smooth, grad_pre, both)
    got_n = swap(send_n, "grp", 1)
    got_n, grads = lax.optimization_barrier((got_n, grads))
    came_n = swap((keep_n[0].astype(F32) + got_n[0].astype(F32)).astype(BF16), "grp", 2)
    got_s = swap(send_s, "grp", 1)
    came_s = swap((keep_s[0].astype(F32) + got_s[0].astype(F32)).astype(BF16), "grp", 2)
    scaled, base, payload = outer_back(outer_rows, live, keep_n, got_n, came_n, keep_s, got_s, outer_a, back_order)
    returned = exchange(payload, back_order)
    bit = peers // 2
    while bit > 2:
        grads = pair_sum(grads, swap(grads, "dom", bit))
        bit //= 2
    base, grads = lax.optimization_barrier((base, grads))
    partial = add_came(inner_back(rows, cols, scaled, base, inner_a), came_s)
    grads = pair_sum(grads, swap(grads, "dom", 1))
    mine = add_returned(targets, returned, partial, back_order)
    across = swap(mine, "grp", 2)
    beside = swap(mine, "grp", 1)
    opposite = swap(across, "grp", 1)
    feature_grad, self_grad, neigh_grad = finish(mine, across, beside, opposite, grads, swap(grads, "dom", 2))
    return layer_out, feature_grad, self_grad, neigh_grad


def solution(mesh):
    placed = (
        P("dom", None),
        P(None, "grp"),
        P(None, "grp"),
        P("dom", "grp"),
        P("dom", None),
        P("dom", None),
        P("dom", None, None, None),
        P("dom", None, None),
        P("dom", None),
        P("dom", None, None, None),
        P("dom", None),
    )
    return jax.shard_map(
        shards,
        mesh=mesh,
        in_specs=placed,
        out_specs=(P("dom", "grp"), P("dom", None), P(None, "grp"), P(None, "grp")),
        check_vma=False,
    )
```

```python
import functools

import jax
import jax.numpy as jnp
from jax import lax
from jax.experimental import pallas as pl
from jax.experimental.pallas import tpu as pltpu
from jax.sharding import PartitionSpec as P

F32 = jnp.float32
BF16 = jnp.bfloat16
MIB = 1 << 20
GROUP = 8
ROWS_LAST = (((1,), (1,)), ((), ()))
ROWS_FIRST = (((0,), (0,)), ((), ()))
WHOLE = pl.BlockSpec(memory_space=pltpu.VMEM)
SCALARS = pl.BlockSpec(memory_space=pltpu.SMEM)
FAR = pl.BlockSpec(memory_space=pltpu.HBM)


def dot(a, b):
    return jnp.dot(a, b, preferred_element_type=F32)


def far(*arrays):
    return [pltpu.with_memory_space_constraint(x, pltpu.HBM) for x in arrays]


OUT_ORDER = (4, 7, 1, 5, 6, 3, 0, 2)
BACK_ORDER = (4, 2, 5, 3, 1, 0, 7, 6)


def order_of(order, peers):
    return order if len(order) == peers else tuple((j + peers // 2) % peers for j in range(peers))


def peer_at(order, j):
    return order[j] if isinstance(j, int) else lax.rem(j + len(order) // 2, len(order))


def exchange(x, order):
    return lax.all_to_all(x, "dom", split_axis=0, concat_axis=0, tiled=True, axis_index_groups=[list(order)])


def for_places(peers, body):
    together = max(k for k in range(1, 9) if peers % k == 0)
    if together == peers:
        body(range(peers))
    else:

        def some(g, _):
            body([g * together + k for k in range(together)])
            return 0

        lax.fori_loop(0, peers // together, some, 0)


def params(mib):
    return pltpu.CompilerParams(vmem_limit_bytes=int(mib * MIB))


def cost(flops, moved):
    return pl.CostEstimate(flops=int(flops), bytes_accessed=int(moved), transcendentals=0)


def gather_kernel(order, targets_far, feat_far, out, targets, feat, outgoing, sems, out_sem):
    pieces = sems.shape[0] - 1
    step = feat.shape[0] // pieces
    mine = lax.axis_index("grp") % 2
    fetches = [pltpu.make_async_copy(targets_far, targets, sems.at[pieces])]
    for k in range(pieces):
        place = pl.ds(k * step, step)
        fetches.append(pltpu.make_async_copy(feat_far.at[place, pl.ds(mine, 1)], feat.at[place], sems.at[k]))
    for fetch in fetches:
        fetch.start()
    for fetch in fetches:
        fetch.wait()
    slots = targets.shape[0]
    for j, p in enumerate(order):
        for s in range(slots):
            outgoing[j, s] = feat[targets[s, 0, p], 0]
        pltpu.make_async_copy(outgoing.at[j], out.at[j], out_sem).start()
    pltpu.make_async_copy(outgoing, out, out_sem).wait()


def gather_halves(features, targets, block, order):
    nodes, feat_width = features.shape
    loc, half = nodes // block, block // 2
    slots, _, peers = targets.shape
    return pl.pallas_call(
        functools.partial(gather_kernel, order),
        out_shape=jax.ShapeDtypeStruct((peers, slots, half, feat_width), BF16),
        in_specs=[FAR, FAR],
        out_specs=FAR,
        scratch_shapes=[
            pltpu.SMEM(targets.shape, jnp.int32),
            pltpu.VMEM((loc, 1, half, feat_width), BF16),
            pltpu.VMEM((peers, slots, half, feat_width), BF16),
            pltpu.SemaphoreType.DMA((5,)),
            pltpu.SemaphoreType.DMA,
        ],
        compiler_params=params(4 + 2 * peers * slots * half * feat_width / MIB),
        name="gather_halves",
    )(*far(targets, features.reshape(loc, 2, half, feat_width)))


def stage_kernel(
    rows_far, cols_far, outer_rows_far, live_far, targets_far, feat_far, inner_far, outer_far,
    rows, cols, outer_rows, live, targets, total, over, over_rows,
    feat, inner, outer, wide, degree_rows, sems, inner_sems,
):
    loc, block, feat_width = total.shape
    count, outer_count = inner.shape[0], outer.shape[0]
    slots, _, peers = targets.shape
    scalars = [
        pltpu.make_async_copy(source, place, sems.at[k])
        for k, (source, place) in enumerate((
            (rows_far, rows), (cols_far, cols), (outer_rows_far, outer_rows), (live_far, live), (targets_far, targets),
        ))
    ]
    tables = [
        pltpu.make_async_copy(source, place, sems.at[5 + k])
        for k, (source, place) in enumerate((
            (feat_far, feat), (outer_far, outer),
        ))
    ]
    groups = count // GROUP
    blocks = [
        pltpu.make_async_copy(
            inner_far.at[pl.ds(g * GROUP, GROUP)], inner.at[pl.ds(g * GROUP, GROUP)], inner_sems.at[g]
        )
        for g in range(groups)
    ]
    for copy in scalars + tables[:1] + blocks + tables[1:]:
        copy.start()
    for copy in scalars + tables[:1]:
        copy.wait()
    x = feat[...].reshape(loc, block, feat_width)
    wide[:, :, :feat_width] = x
    wide[:, :, feat_width:] = jnp.ones((loc, block, feat_width), BF16)
    total[...] = x.astype(F32)
    over[...] = jnp.ones((loc, block, feat_width), F32)
    degree_rows[...] = jnp.ones(degree_rows.shape, F32)
    few = jnp.ones((degree_rows.shape[1], block), BF16)
    for g in range(groups):
        blocks[g].wait()
        products = [dot(inner[g * GROUP + k], wide[cols[0, g * GROUP + k]]) for k in range(GROUP)]
        flat = [
            lax.dot_general(few, inner[g * GROUP + k], ROWS_LAST, preferred_element_type=F32) for k in range(GROUP)
        ]
        for k in range(GROUP):
            r = rows[0, g * GROUP + k]
            total[r] += products[k][:, :feat_width]
            over[r] += products[k][:, feat_width:]
            degree_rows[r] += flat[k]
    for copy in tables[1:]:
        copy.wait()

    def some(g, _):
        ones = jnp.ones((block, feat_width), BF16)
        products = [dot(outer[g * GROUP + k], ones) for k in range(GROUP)]
        flat = [
            lax.dot_general(few, outer[g * GROUP + k], ROWS_LAST, preferred_element_type=F32) for k in range(GROUP)
        ]
        for k in range(GROUP):
            n = g * GROUP + k
            alive = (n % slots < live[0, n // slots]).astype(F32)
            over[outer_rows[0, n]] += products[k] * alive
            degree_rows[outer_rows[0, n]] += flat[k] * alive
        return 0

    lax.fori_loop(0, outer_count // GROUP, some, 0)
    over[...] = 1.0 / over[...]
    over_rows[...] = 1.0 / degree_rows[...]


def stage(rows, cols, outer_rows, live, targets, features, inner, outer):
    count, block, _ = inner.shape
    nodes, feat_width = features.shape
    loc = nodes // block
    scalars = (rows, cols, outer_rows, live, targets)
    sums = (loc, block, feat_width)
    return pl.pallas_call(
        stage_kernel,
        out_shape=tuple(pltpu.SMEM(x.shape, jnp.int32) for x in scalars)
        + (pltpu.VMEM(sums, F32), pltpu.VMEM(sums, F32), pltpu.VMEM((loc, 8, block), F32)),
        in_specs=[FAR] * 8,
        out_specs=(SCALARS,) * 5 + (WHOLE,) * 3,
        scratch_shapes=[
            pltpu.VMEM(features.shape, BF16),
            pltpu.VMEM(inner.shape, BF16),
            pltpu.VMEM(outer.shape, BF16),
            pltpu.VMEM((loc, block, 2 * feat_width), BF16),
            pltpu.VMEM((loc, 8, block), F32),
            pltpu.SemaphoreType.DMA((7,)),
            pltpu.SemaphoreType.DMA((count // GROUP,)),
        ],
        compiler_params=params(12 + outer.size * 2 / MIB),
        cost_estimate=cost(count * block * block * feat_width * 4, 6 * MIB),
        name="stage",
    )(*far(*scalars, features, inner, outer))


def fetch_kernel(
    outer_far, feat_far, cot_far, self_far, neigh_far, outer, feat, cot, weights, turned, w_self, w_neigh, sems
):
    feat_width = feat.shape[1]
    part = feat_width // lax.axis_size("grp")
    me = lax.axis_index("grp")
    fetches = [
        pltpu.make_async_copy(source, place, sems.at[k])
        for k, (source, place) in enumerate((
            (self_far, w_self), (neigh_far, w_neigh), (outer_far, outer), (feat_far, feat), (cot_far, cot),
        ))
    ]
    for fetch in fetches:
        fetch.start()
    for fetch in fetches[:2]:
        fetch.wait()
    weights[:feat_width] = w_self[...] * 0.5
    weights[feat_width:] = w_neigh[...] * 0.5
    for spot, away in enumerate((3, 1, 2, 0)):
        start = pl.multiple_of((me ^ away) * part, part)
        turned[pl.ds(spot * part, part)] = w_self[pl.ds(start, part)] * 0.5
        turned[pl.ds(feat_width + spot * part, part)] = w_neigh[pl.ds(start, part)] * 0.5
    for fetch in fetches[2:]:
        fetch.wait()


def fetch(outer, features, cotangent, w_self, w_neigh):
    both = (2 * features.shape[1], w_self.shape[1])
    return pl.pallas_call(
        fetch_kernel,
        out_shape=tuple(pltpu.VMEM(shape, BF16) for shape in (outer.shape, features.shape, cotangent.shape, both, both)),
        in_specs=[FAR] * 5,
        out_specs=(WHOLE,) * 5,
        scratch_shapes=[
            pltpu.VMEM(w_self.shape, BF16),
            pltpu.VMEM(w_neigh.shape, BF16),
            pltpu.SemaphoreType.DMA((5,)),
        ],
        compiler_params=params(8 + outer.size * 2 / MIB),
        cost_estimate=cost(1e6, 3 * MIB),
        name="fetch",
    )(*far(outer, features, cotangent, w_self, w_neigh))


def layer_kernel(
    chunk_blocks, order,
    outer_rows, live, own, other, outer, total_in, over_all, over_rows, feat, cot, weights, turned,
    smooth, grad_pre_all, both_all, send_n, keep_n, send_s, keep_s, total,
):
    del total_in
    peers, slots, half, feat_width = own.shape
    count, block, _ = outer.shape
    loc = total.shape[0]
    chunks = loc // chunk_blocks
    rows = chunk_blocks * block
    part = feat_width // lax.axis_size("grp")
    mine = lax.axis_index("grp") % 2

    def some(places):
        blocks = [(j, k, peer_at(order, j) * slots + k) for j in places for k in range(slots)]
        products = []
        for j, k, n in blocks:
            near, away = own[j, k], other[j, k]
            x = jnp.concatenate([jnp.where(mine == 0, near, away), jnp.where(mine == 0, away, near)], axis=0)
            products.append(dot(outer[n], x))
        for (j, k, n), product in zip(blocks, products):
            alive = (k < live[0, peer_at(order, j)]).astype(F32)
            total[outer_rows[0, n]] += product * alive

    for_places(peers, some)
    for c in range(chunks):
        place = pl.ds(c * rows, rows)
        here = pl.ds(c * chunk_blocks, chunk_blocks)
        over = over_all[here].reshape(rows, feat_width)
        agg = (total[here].reshape(rows, feat_width) * over).astype(BF16)
        both = jnp.concatenate([feat[place], agg], axis=1)
        pre = dot(both, weights[...])
        bent = jnp.tanh(pre)
        twice = 1.0 + bent
        silu = pre * twice
        smooth[place] = silu.astype(BF16)
        grad_pre = (cot[place].astype(F32) * (twice + silu * (1.0 - bent))).astype(BF16)
        grad_pre_all[place] = grad_pre
        both_all[place] = both
        back = lax.dot_general(turned[...], grad_pre, ROWS_LAST, preferred_element_type=F32)
        for b in range(chunk_blocks):
            at = c * chunk_blocks + b
            lanes = slice(b * block, (b + 1) * block)
            self_t = back[:feat_width, lanes].astype(BF16)
            neigh_t = (back[feat_width:, lanes] * over_rows[at, :1]).astype(BF16)
            for y in range(2):
                send_n[y, at] = neigh_t[y * part : (y + 1) * part]
                keep_n[y, at] = neigh_t[(2 + y) * part : (3 + y) * part]
                send_s[y, at] = self_t[y * part : (y + 1) * part]
                keep_s[y, at] = self_t[(2 + y) * part : (3 + y) * part]


def layer(outer_rows, live, own, other, outer, total, over, over_rows, features, cotangent, weights, turned, order):
    feat_width = features.shape[1]
    loc, block, _ = total.shape
    chunk = 4
    part = feat_width // lax.axis_size("grp")
    piece = pltpu.VMEM((2, loc, part, block), BF16)
    return pl.pallas_call(
        functools.partial(layer_kernel, chunk, order),
        out_shape=(
            pltpu.VMEM(cotangent.shape, BF16),
            pltpu.VMEM(cotangent.shape, BF16),
            pltpu.VMEM((cotangent.shape[0], 2 * feat_width), BF16),
            piece, piece, piece, piece,
            pltpu.VMEM(total.shape, F32),
        ),
        in_specs=[SCALARS] * 2 + [WHOLE] * 10,
        out_specs=(WHOLE,) * 8,
        input_output_aliases={5: 7},
        compiler_params=params(16 + 4 * own.size * 2 / MIB),
        cost_estimate=cost(1.2e9, 8 * MIB),
        name="layer",
    )(outer_rows, live, own, other, outer, total, over, over_rows, features, cotangent, weights, turned)[:7]


def weight_grads_kernel(smooth, grad_pre, both, layer_out, grads, sems):
    pieces = sems.shape[0]
    rows = smooth.shape[0] // pieces
    copies = [
        pltpu.make_async_copy(smooth.at[pl.ds(c * rows, rows)], layer_out.at[pl.ds(c * rows, rows)], sems.at[c])
        for c in range(pieces)
    ]
    for copy in copies:
        copy.start()
    grown = lax.dot_general(both[...], grad_pre[...], ROWS_FIRST, preferred_element_type=F32)
    grads[...] = (0.5 * grown).astype(BF16)
    for copy in copies:
        copy.wait()


def weight_grads(smooth, grad_pre, both):
    return pl.pallas_call(
        weight_grads_kernel,
        out_shape=(
            jax.ShapeDtypeStruct(smooth.shape, BF16),
            pltpu.VMEM((both.shape[1], grad_pre.shape[1]), BF16),
        ),
        in_specs=[WHOLE] * 3,
        out_specs=(FAR, WHOLE),
        scratch_shapes=[pltpu.SemaphoreType.DMA((4,))],
        compiler_params=params(12),
        cost_estimate=cost(2 * grad_pre.size * both.shape[1], 4 * MIB),
        name="weight_grads",
    )(smooth, grad_pre, both)


def outer_back_kernel(
    order, outer_rows, live, keep, got, came, keep_s, got_s, outer, scaled, base, payload_far, payload, sem
):
    peers, slots, part, block = payload.shape
    near = (keep[1].astype(F32) + got[1].astype(F32) + came[...].astype(F32)).astype(BF16)
    scaled[...] = near
    base[...] = near.astype(F32) + keep_s[1].astype(F32) + got_s[1].astype(F32)

    def some(places):
        blocks = [(j, k, peer_at(order, j) * slots + k) for j in places for k in range(slots)]
        products = [dot(scaled[outer_rows[0, n]], outer[n]) for _, _, n in blocks]
        for (j, k, n), product in zip(blocks, products):
            alive = (k < live[0, peer_at(order, j)]).astype(F32)
            payload[j, k] = (product * alive).astype(BF16)
            if k == slots - 1:
                pltpu.make_async_copy(payload.at[j], payload_far.at[j], sem).start()

    for_places(peers, some)
    pltpu.make_async_copy(payload, payload_far, sem).wait()


def outer_back(outer_rows, live, keep, got, came, keep_s, got_s, outer, order):
    loc, part, block = came.shape
    count, peers = outer.shape[0], len(order)
    return pl.pallas_call(
        functools.partial(outer_back_kernel, order),
        out_shape=(
            pltpu.VMEM((loc, part, block), BF16),
            pltpu.VMEM((loc, part, block), F32),
            jax.ShapeDtypeStruct((peers, count // peers, part, block), BF16),
        ),
        in_specs=[SCALARS, SCALARS] + [WHOLE] * 6,
        out_specs=(WHOLE, WHOLE, FAR),
        scratch_shapes=[pltpu.VMEM((peers, count // peers, part, block), BF16), pltpu.SemaphoreType.DMA],
        compiler_params=params(8 + count * block * (block + part) * 2 / MIB),
        cost_estimate=cost(count * block * block * part * 2, 2 * MIB),
        name="outer_back",
    )(outer_rows, live, keep, got, came, keep_s, got_s, outer)


def inner_back_kernel(rows, cols, scaled, base, inner_far, total, inner, sems):
    groups = inner.shape[0] // GROUP
    blocks = [
        pltpu.make_async_copy(inner_far.at[pl.ds(g * GROUP, GROUP)], inner.at[pl.ds(g * GROUP, GROUP)], sems.at[g])
        for g in range(groups)
    ]
    for copy in blocks:
        copy.start()
    total[...] = base[...]
    for g in range(groups):
        blocks[g].wait()
        products = [dot(scaled[rows[0, g * GROUP + k]], inner[g * GROUP + k]) for k in range(GROUP)]
        for k in range(GROUP):
            total[cols[0, g * GROUP + k]] += products[k]


def inner_back(rows, cols, scaled, base, inner):
    count, block, _ = inner.shape
    return pl.pallas_call(
        inner_back_kernel,
        out_shape=pltpu.VMEM(base.shape, F32),
        in_specs=[SCALARS, SCALARS, WHOLE, WHOLE, FAR],
        out_specs=WHOLE,
        scratch_shapes=[pltpu.VMEM(inner.shape, BF16), pltpu.SemaphoreType.DMA((count // GROUP,))],
        compiler_params=params(8),
        cost_estimate=cost(count * block * block * scaled.shape[1] * 2, 3 * MIB),
        name="inner_back",
    )(rows, cols, scaled, base, *far(inner))


def add_came_kernel(total, came, out):
    out[...] = total[...] + came[...].astype(F32)


def add_came(total, came):
    return pl.pallas_call(
        add_came_kernel,
        out_shape=pltpu.VMEM(total.shape, F32),
        in_specs=[WHOLE, WHOLE],
        out_specs=WHOLE,
        compiler_params=params(4),
        cost_estimate=cost(total.size, total.size * 10),
        name="add_came",
    )(total, came)


def add_returned_kernel(order, targets, returned, total, out, summed):
    peers, slots, _, _ = returned.shape
    summed[...] = total[...]

    def some(places):
        for j in places:
            for k in range(slots):
                summed[targets[k, 0, peer_at(order, j)]] += returned[j, k].astype(F32)

    for_places(peers, some)
    out[...] = summed[...].astype(BF16)


def add_returned(targets, returned, total, order):
    return pl.pallas_call(
        functools.partial(add_returned_kernel, order),
        out_shape=pltpu.VMEM(total.shape, BF16),
        in_specs=[SCALARS, WHOLE, WHOLE],
        out_specs=WHOLE,
        scratch_shapes=[pltpu.VMEM(total.shape, F32)],
        compiler_params=params(8 + returned.size * 2 / MIB),
        cost_estimate=cost(total.size * 8, 2 * MIB),
        name="add_returned",
    )(targets, returned, total)


def pair_sum_kernel(a, b, out):
    out[...] = (a[...].astype(F32) + b[...].astype(F32)).astype(BF16)


def pair_sum(a, b):
    return pl.pallas_call(
        pair_sum_kernel,
        out_shape=jax.ShapeDtypeStruct(a.shape, BF16),
        in_specs=[WHOLE, WHOLE],
        out_specs=WHOLE,
        compiler_params=params(4),
        cost_estimate=cost(a.size * 2, a.size * 6),
        name="pair_sum",
    )(a, b)


def finish_kernel(mine, across, beside, opposite, grads, grads_came, out, self_out, neigh_out, turned, summed, sems):
    loc, part, block = mine.shape
    me = lax.axis_index("grp")
    feat_width = turned.shape[1]
    summed[...] = grads[...].astype(F32) + grads_came[...].astype(F32)
    copies = [
        pltpu.make_async_copy(summed.at[pl.ds(0, feat_width)], self_out, sems.at[0]),
        pltpu.make_async_copy(summed.at[pl.ds(feat_width, feat_width)], neigh_out, sems.at[1]),
    ]
    for copy in copies:
        copy.start()
    row = lax.broadcasted_iota(jnp.int32, (feat_width, feat_width), 0)
    lane = lax.broadcasted_iota(jnp.int32, (feat_width, feat_width), 1)
    stacked = row // part
    away = jnp.where(stacked == 1, 2, jnp.where(stacked == 2, 1, stacked))
    order = (((me ^ away) * part + row % part) == lane).astype(BF16)
    step = loc // 4
    for c in range(4):
        for b in range(c * step, (c + 1) * step):
            stack = jnp.concatenate([mine[b], across[b], beside[b], opposite[b]], axis=0)
            turned[b * block : (b + 1) * block] = lax.dot_general(stack, order, ROWS_FIRST, preferred_element_type=F32)
        place = pl.ds(c * step * block, step * block)
        copies.append(pltpu.make_async_copy(turned.at[place], out.at[place], sems.at[2 + c]))
        copies[-1].start()
    for copy in copies:
        copy.wait()


def finish(mine, across, beside, opposite, grads, grads_came):
    loc, part, block = mine.shape
    feat_width = grads.shape[0] // 2
    weight = jax.ShapeDtypeStruct((feat_width, grads.shape[1]), F32)
    return pl.pallas_call(
        finish_kernel,
        out_shape=(jax.ShapeDtypeStruct((loc * block, feat_width), F32), weight, weight),
        in_specs=[WHOLE] * 6,
        out_specs=(FAR, FAR, FAR),
        scratch_shapes=[
            pltpu.VMEM((loc * block, feat_width), F32),
            pltpu.VMEM(grads.shape, F32),
            pltpu.SemaphoreType.DMA((6,)),
        ],
        compiler_params=params(8),
        cost_estimate=cost(loc * block * feat_width * feat_width * 2, 2 * MIB),
        name="finish",
    )(mine, across, beside, opposite, grads, grads_came)


def swap(x, axis, bit):
    return lax.ppermute(x, axis, [(i, i ^ bit) for i in range(lax.axis_size(axis))])


def shards(
    features,
    weight_self,
    weight_neigh,
    cotangent,
    inner_rows,
    inner_cols,
    inner_values,
    send_blocks,
    outer_rows,
    outer_values,
    live_count,
):
    peers = lax.axis_size("dom")
    feat_width = features.shape[1]
    inner_a, outer_a = inner_values[0], outer_values[0]
    targets = send_blocks.transpose(2, 0, 1)
    block = inner_a.shape[-1]

    out_order, back_order = order_of(OUT_ORDER, peers), order_of(BACK_ORDER, peers)
    own = exchange(gather_halves(features, targets, block, out_order), out_order)
    rows, cols, outer_rows, live, targets, total, over, over_rows = stage(
        inner_rows, inner_cols, outer_rows, live_count, targets, features, inner_a, outer_a
    )
    own, total, outer_a = lax.optimization_barrier((own, total, outer_a))
    other = swap(own, "grp", 1)
    outer_a, features, cotangent, weights, turned = fetch(outer_a, features, cotangent, weight_self, weight_neigh)
    smooth, grad_pre, both, send_n, keep_n, send_s, keep_s = layer(
        outer_rows, live, own, other, outer_a, total, over, over_rows, features, cotangent, weights, turned, out_order
    )
    layer_out, grads = weight_grads(smooth, grad_pre, both)
    got_n = swap(send_n, "grp", 1)
    got_n, grads = lax.optimization_barrier((got_n, grads))
    came_n = swap((keep_n[0].astype(F32) + got_n[0].astype(F32)).astype(BF16), "grp", 2)
    got_s = swap(send_s, "grp", 1)
    came_s = swap((keep_s[0].astype(F32) + got_s[0].astype(F32)).astype(BF16), "grp", 2)
    scaled, base, payload = outer_back(outer_rows, live, keep_n, got_n, came_n, keep_s, got_s, outer_a, back_order)
    returned = exchange(payload, back_order)
    bit = peers // 2
    while bit > 2:
        came, came_s = lax.optimization_barrier((swap(grads, "dom", bit), came_s))
        grads = (grads.astype(F32) + came.astype(F32)).astype(BF16)
        bit //= 2
    base, grads = lax.optimization_barrier((base, grads))
    partial = add_came(inner_back(rows, cols, scaled, base, inner_a), came_s)
    grads = pair_sum(grads, swap(grads, "dom", 1))
    mine = add_returned(targets, returned, partial, back_order)
    across = swap(mine, "grp", 2)
    beside = swap(mine, "grp", 1)
    opposite = swap(across, "grp", 1)
    feature_grad, self_grad, neigh_grad = finish(mine, across, beside, opposite, grads, swap(grads, "dom", 2))
    return layer_out, feature_grad, self_grad, neigh_grad


def solution(mesh):
    placed = (
        P("dom", None),
        P(None, "grp"),
        P(None, "grp"),
        P("dom", "grp"),
        P("dom", None),
        P("dom", None),
        P("dom", None, None, None),
        P("dom", None, None),
        P("dom", None),
        P("dom", None, None, None),
        P("dom", None),
    )
    return jax.shard_map(
        shards,
        mesh=mesh,
        in_specs=placed,
        out_specs=(P("dom", "grp"), P("dom", None), P(None, "grp"), P(None, "grp")),
        check_vma=False,
    )
```

```python
import functools

import jax
import jax.numpy as jnp
from jax import lax
from jax.experimental import pallas as pl
from jax.experimental.pallas import tpu as pltpu
from jax.sharding import PartitionSpec as P

F32 = jnp.float32
BF16 = jnp.bfloat16
MIB = 1 << 20
GROUP = 16
OUTER_GROUP = 8
ROWS_LAST = (((1,), (1,)), ((), ()))
ROWS_FIRST = (((0,), (0,)), ((), ()))
WHOLE = pl.BlockSpec(memory_space=pltpu.VMEM)
SCALARS = pl.BlockSpec(memory_space=pltpu.SMEM)
FAR = pl.BlockSpec(memory_space=pltpu.HBM)


def dot(a, b):
    return jnp.dot(a, b, preferred_element_type=F32)


def far(*arrays):
    return [pltpu.with_memory_space_constraint(x, pltpu.HBM) for x in arrays]


OUT_ORDER = (4, 7, 3, 5, 2, 1, 0, 6)
BACK_ORDER = (4, 2, 5, 3, 1, 0, 7, 6)


def order_of(order, peers):
    return order if len(order) == peers else tuple((j + peers // 2) % peers for j in range(peers))


def peer_at(order, j):
    return order[j] if isinstance(j, int) else lax.rem(j + len(order) // 2, len(order))


def exchange(x, order):
    return lax.all_to_all(x, "dom", split_axis=0, concat_axis=0, tiled=True, axis_index_groups=[list(order)])


def for_places(peers, body):
    together = max(k for k in range(1, 9) if peers % k == 0)
    if together == peers:
        body(range(peers))
    else:

        def some(g, _):
            body([g * together + k for k in range(together)])
            return 0

        lax.fori_loop(0, peers // together, some, 0)


def params(mib):
    return pltpu.CompilerParams(vmem_limit_bytes=int(mib * MIB))


def cost(flops, moved):
    return pl.CostEstimate(flops=int(flops), bytes_accessed=int(moved), transcendentals=0)


def gather_kernel(order, targets_far, feat_far, out, targets, feat, outgoing, sems, out_sem):
    pieces = sems.shape[0] - 1
    step = feat.shape[0] // pieces
    mine = lax.axis_index("grp") % 2
    fetches = [pltpu.make_async_copy(targets_far, targets, sems.at[pieces])]
    for k in range(pieces):
        place = pl.ds(k * step, step)
        fetches.append(pltpu.make_async_copy(feat_far.at[place, pl.ds(mine, 1)], feat.at[place], sems.at[k]))
    for fetch in fetches:
        fetch.start()
    for fetch in fetches:
        fetch.wait()
    slots = targets.shape[0]
    for j, p in enumerate(order):
        for s in range(slots):
            outgoing[j, s] = feat[targets[s, 0, p], 0]
        pltpu.make_async_copy(outgoing.at[j], out.at[j], out_sem).start()
    pltpu.make_async_copy(outgoing, out, out_sem).wait()


def gather_halves(features, targets, block, order):
    nodes, feat_width = features.shape
    loc, half = nodes // block, block // 2
    slots, _, peers = targets.shape
    return pl.pallas_call(
        functools.partial(gather_kernel, order),
        out_shape=jax.ShapeDtypeStruct((peers, slots, half, feat_width), BF16),
        in_specs=[FAR, FAR],
        out_specs=FAR,
        scratch_shapes=[
            pltpu.SMEM(targets.shape, jnp.int32),
            pltpu.VMEM((loc, 1, half, feat_width), BF16),
            pltpu.VMEM((peers, slots, half, feat_width), BF16),
            pltpu.SemaphoreType.DMA((5,)),
            pltpu.SemaphoreType.DMA,
        ],
        compiler_params=params(4 + 2 * peers * slots * half * feat_width / MIB),
        name="gather_halves",
    )(*far(targets, features.reshape(loc, 2, half, feat_width)))


def stage_kernel(
    rows_far, cols_far, outer_rows_far, live_far, targets_far, feat_far, inner_far, outer_far,
    rows, cols, outer_rows, live, targets, total, over, over_rows,
    feat, inner, outer, wide, degree_rows, sems, inner_sems,
):
    loc, block, feat_width = total.shape
    count, outer_count = inner.shape[0], outer.shape[0]
    slots, _, peers = targets.shape
    scalars = [
        pltpu.make_async_copy(source, place, sems.at[k])
        for k, (source, place) in enumerate((
            (rows_far, rows), (cols_far, cols), (outer_rows_far, outer_rows), (live_far, live), (targets_far, targets),
        ))
    ]
    tables = [
        pltpu.make_async_copy(source, place, sems.at[5 + k])
        for k, (source, place) in enumerate((
            (feat_far, feat), (outer_far, outer),
        ))
    ]
    groups = count // GROUP
    blocks = [
        pltpu.make_async_copy(
            inner_far.at[pl.ds(g * GROUP, GROUP)], inner.at[pl.ds(g * GROUP, GROUP)], inner_sems.at[g]
        )
        for g in range(groups)
    ]
    for copy in scalars + tables[:1] + blocks + tables[1:]:
        copy.start()
    for copy in scalars + tables[:1]:
        copy.wait()
    x = feat[...].reshape(loc, block, feat_width)
    wide[:, :, :feat_width] = x
    wide[:, :, feat_width:] = jnp.ones((loc, block, feat_width), BF16)
    total[...] = x.astype(F32)
    over[...] = jnp.ones((loc, block, feat_width), F32)
    degree_rows[...] = jnp.ones(degree_rows.shape, F32)
    few = jnp.ones((degree_rows.shape[1], block), BF16)
    for g in range(groups):
        blocks[g].wait()
        products = [dot(inner[g * GROUP + k], wide[cols[0, g * GROUP + k]]) for k in range(GROUP)]
        flat = [
            lax.dot_general(few, inner[g * GROUP + k], ROWS_LAST, preferred_element_type=F32) for k in range(GROUP)
        ]
        for k in range(GROUP):
            r = rows[0, g * GROUP + k]
            total[r] += products[k][:, :feat_width]
            over[r] += products[k][:, feat_width:]
            degree_rows[r] += flat[k]
    for copy in tables[1:]:
        copy.wait()

    def some(g, _):
        ones = jnp.ones((block, feat_width), BF16)
        products = [dot(outer[g * OUTER_GROUP + k], ones) for k in range(OUTER_GROUP)]
        flat = [
            lax.dot_general(few, outer[g * OUTER_GROUP + k], ROWS_LAST, preferred_element_type=F32) for k in range(OUTER_GROUP)
        ]
        for k in range(OUTER_GROUP):
            n = g * OUTER_GROUP + k
            alive = (n % slots < live[0, n // slots]).astype(F32)
            over[outer_rows[0, n]] += products[k] * alive
            degree_rows[outer_rows[0, n]] += flat[k] * alive
        return 0

    lax.fori_loop(0, outer_count // OUTER_GROUP, some, 0)
    over[...] = 1.0 / over[...]
    over_rows[...] = 1.0 / degree_rows[...]


def stage(rows, cols, outer_rows, live, targets, features, inner, outer):
    count, block, _ = inner.shape
    nodes, feat_width = features.shape
    loc = nodes // block
    scalars = (rows, cols, outer_rows, live, targets)
    sums = (loc, block, feat_width)
    return pl.pallas_call(
        stage_kernel,
        out_shape=tuple(pltpu.SMEM(x.shape, jnp.int32) for x in scalars)
        + (pltpu.VMEM(sums, F32), pltpu.VMEM(sums, F32), pltpu.VMEM((loc, 8, block), F32)),
        in_specs=[FAR] * 8,
        out_specs=(SCALARS,) * 5 + (WHOLE,) * 3,
        scratch_shapes=[
            pltpu.VMEM(features.shape, BF16),
            pltpu.VMEM(inner.shape, BF16),
            pltpu.VMEM(outer.shape, BF16),
            pltpu.VMEM((loc, block, 2 * feat_width), BF16),
            pltpu.VMEM((loc, 8, block), F32),
            pltpu.SemaphoreType.DMA((7,)),
            pltpu.SemaphoreType.DMA((count // GROUP,)),
        ],
        compiler_params=params(12 + outer.size * 2 / MIB),
        cost_estimate=cost(count * block * block * feat_width * 4, 6 * MIB),
        name="stage",
    )(*far(*scalars, features, inner, outer))


def fetch_kernel(
    outer_far, feat_far, cot_far, self_far, neigh_far, outer, feat, cot, weights, turned, w_self, w_neigh, sems
):
    feat_width = feat.shape[1]
    part = feat_width // lax.axis_size("grp")
    me = lax.axis_index("grp")
    fetches = [
        pltpu.make_async_copy(source, place, sems.at[k])
        for k, (source, place) in enumerate((
            (self_far, w_self), (neigh_far, w_neigh), (outer_far, outer), (feat_far, feat), (cot_far, cot),
        ))
    ]
    for fetch in fetches:
        fetch.start()
    for fetch in fetches[:2]:
        fetch.wait()
    weights[:feat_width] = w_self[...] * 0.5
    weights[feat_width:] = w_neigh[...] * 0.5
    for spot, away in enumerate((3, 1, 2, 0)):
        start = pl.multiple_of((me ^ away) * part, part)
        turned[pl.ds(spot * part, part)] = w_self[pl.ds(start, part)] * 0.5
        turned[pl.ds(feat_width + spot * part, part)] = w_neigh[pl.ds(start, part)] * 0.5
    for fetch in fetches[2:]:
        fetch.wait()


def fetch(outer, features, cotangent, w_self, w_neigh):
    both = (2 * features.shape[1], w_self.shape[1])
    return pl.pallas_call(
        fetch_kernel,
        out_shape=tuple(pltpu.VMEM(shape, BF16) for shape in (outer.shape, features.shape, cotangent.shape, both, both)),
        in_specs=[FAR] * 5,
        out_specs=(WHOLE,) * 5,
        scratch_shapes=[
            pltpu.VMEM(w_self.shape, BF16),
            pltpu.VMEM(w_neigh.shape, BF16),
            pltpu.SemaphoreType.DMA((5,)),
        ],
        compiler_params=params(8 + outer.size * 2 / MIB),
        cost_estimate=cost(1e6, 3 * MIB),
        name="fetch",
    )(*far(outer, features, cotangent, w_self, w_neigh))


def layer_kernel(
    chunk_blocks, order,
    outer_rows, live, own, other, outer, total_in, over_all, over_rows, feat, cot, weights, turned,
    smooth, grad_pre_all, both_all, send_n, keep_n, send_s, keep_s, total,
):
    del total_in
    peers, slots, half, feat_width = own.shape
    count, block, _ = outer.shape
    loc = total.shape[0]
    chunks = loc // chunk_blocks
    rows = chunk_blocks * block
    part = feat_width // lax.axis_size("grp")
    mine = lax.axis_index("grp") % 2

    def some(places):
        blocks = [(j, k, peer_at(order, j) * slots + k) for j in places for k in range(slots)]
        products = []
        for j, k, n in blocks:
            near, away = own[j, k], other[j, k]
            x = jnp.concatenate([jnp.where(mine == 0, near, away), jnp.where(mine == 0, away, near)], axis=0)
            products.append(dot(outer[n], x))
        for (j, k, n), product in zip(blocks, products):
            alive = (k < live[0, peer_at(order, j)]).astype(F32)
            total[outer_rows[0, n]] += product * alive

    for_places(peers, some)
    for c in range(chunks):
        place = pl.ds(c * rows, rows)
        here = pl.ds(c * chunk_blocks, chunk_blocks)
        over = over_all[here].reshape(rows, feat_width)
        agg = (total[here].reshape(rows, feat_width) * over).astype(BF16)
        both = jnp.concatenate([feat[place], agg], axis=1)
        pre = dot(both, weights[...])
        bent = jnp.tanh(pre)
        twice = 1.0 + bent
        silu = pre * twice
        smooth[place] = silu.astype(BF16)
        grad_pre = (cot[place].astype(F32) * (twice + silu * (1.0 - bent))).astype(BF16)
        grad_pre_all[place] = grad_pre
        both_all[place] = both
        back = lax.dot_general(turned[...], grad_pre, ROWS_LAST, preferred_element_type=F32)
        for b in range(chunk_blocks):
            at = c * chunk_blocks + b
            lanes = slice(b * block, (b + 1) * block)
            self_t = back[:feat_width, lanes].astype(BF16)
            neigh_t = (back[feat_width:, lanes] * over_rows[at, :1]).astype(BF16)
            for y in range(2):
                send_n[y, at] = neigh_t[y * part : (y + 1) * part]
                keep_n[y, at] = neigh_t[(2 + y) * part : (3 + y) * part]
                send_s[y, at] = self_t[y * part : (y + 1) * part]
                keep_s[y, at] = self_t[(2 + y) * part : (3 + y) * part]


def layer(outer_rows, live, own, other, outer, total, over, over_rows, features, cotangent, weights, turned, order):
    feat_width = features.shape[1]
    loc, block, _ = total.shape
    chunk = 4
    part = feat_width // lax.axis_size("grp")
    piece = pltpu.VMEM((2, loc, part, block), BF16)
    return pl.pallas_call(
        functools.partial(layer_kernel, chunk, order),
        out_shape=(
            pltpu.VMEM(cotangent.shape, BF16),
            pltpu.VMEM(cotangent.shape, BF16),
            pltpu.VMEM((cotangent.shape[0], 2 * feat_width), BF16),
            piece, piece, piece, piece,
            pltpu.VMEM(total.shape, F32),
        ),
        in_specs=[SCALARS] * 2 + [WHOLE] * 10,
        out_specs=(WHOLE,) * 8,
        input_output_aliases={5: 7},
        compiler_params=params(16 + 4 * own.size * 2 / MIB),
        cost_estimate=cost(1.2e9, 8 * MIB),
        name="layer",
    )(outer_rows, live, own, other, outer, total, over, over_rows, features, cotangent, weights, turned)[:7]


def weight_grads_kernel(smooth, grad_pre, both, layer_out, grads, sems):
    pieces = sems.shape[0]
    rows = smooth.shape[0] // pieces
    copies = [
        pltpu.make_async_copy(smooth.at[pl.ds(c * rows, rows)], layer_out.at[pl.ds(c * rows, rows)], sems.at[c])
        for c in range(pieces)
    ]
    for copy in copies:
        copy.start()
    grown = lax.dot_general(both[...], grad_pre[...], ROWS_FIRST, preferred_element_type=F32)
    grads[...] = (0.5 * grown).astype(BF16)
    for copy in copies:
        copy.wait()


def weight_grads(smooth, grad_pre, both):
    return pl.pallas_call(
        weight_grads_kernel,
        out_shape=(
            jax.ShapeDtypeStruct(smooth.shape, BF16),
            pltpu.VMEM((both.shape[1], grad_pre.shape[1]), BF16),
        ),
        in_specs=[WHOLE] * 3,
        out_specs=(FAR, WHOLE),
        scratch_shapes=[pltpu.SemaphoreType.DMA((4,))],
        compiler_params=params(12),
        cost_estimate=cost(2 * grad_pre.size * both.shape[1], 4 * MIB),
        name="weight_grads",
    )(smooth, grad_pre, both)


def outer_back_kernel(
    order, outer_rows, live, keep, got, came, keep_s, got_s, outer, scaled, base, payload_far, payload, sem
):
    peers, slots, part, block = payload.shape
    near = (keep[1].astype(F32) + got[1].astype(F32) + came[...].astype(F32)).astype(BF16)
    scaled[...] = near
    base[...] = near.astype(F32) + keep_s[1].astype(F32) + got_s[1].astype(F32)

    def some(places):
        blocks = [(j, k, peer_at(order, j) * slots + k) for j in places for k in range(slots)]
        products = [dot(scaled[outer_rows[0, n]], outer[n]) for _, _, n in blocks]
        for (j, k, n), product in zip(blocks, products):
            alive = (k < live[0, peer_at(order, j)]).astype(F32)
            payload[j, k] = (product * alive).astype(BF16)
            if k == slots - 1:
                pltpu.make_async_copy(payload.at[j], payload_far.at[j], sem).start()

    for_places(peers, some)
    pltpu.make_async_copy(payload, payload_far, sem).wait()


def outer_back(outer_rows, live, keep, got, came, keep_s, got_s, outer, order):
    loc, part, block = came.shape
    count, peers = outer.shape[0], len(order)
    return pl.pallas_call(
        functools.partial(outer_back_kernel, order),
        out_shape=(
            pltpu.VMEM((loc, part, block), BF16),
            pltpu.VMEM((loc, part, block), F32),
            jax.ShapeDtypeStruct((peers, count // peers, part, block), BF16),
        ),
        in_specs=[SCALARS, SCALARS] + [WHOLE] * 6,
        out_specs=(WHOLE, WHOLE, FAR),
        scratch_shapes=[pltpu.VMEM((peers, count // peers, part, block), BF16), pltpu.SemaphoreType.DMA],
        compiler_params=params(8 + count * block * (block + part) * 2 / MIB),
        cost_estimate=cost(count * block * block * part * 2, 2 * MIB),
        name="outer_back",
    )(outer_rows, live, keep, got, came, keep_s, got_s, outer)


def inner_back_kernel(rows, cols, scaled, base, inner_far, total, inner, sems):
    groups = inner.shape[0] // GROUP
    blocks = [
        pltpu.make_async_copy(inner_far.at[pl.ds(g * GROUP, GROUP)], inner.at[pl.ds(g * GROUP, GROUP)], sems.at[g])
        for g in range(groups)
    ]
    for copy in blocks:
        copy.start()
    total[...] = base[...]
    for g in range(groups):
        blocks[g].wait()
        products = [dot(scaled[rows[0, g * GROUP + k]], inner[g * GROUP + k]) for k in range(GROUP)]
        for k in range(GROUP):
            total[cols[0, g * GROUP + k]] += products[k]


def inner_back(rows, cols, scaled, base, inner):
    count, block, _ = inner.shape
    return pl.pallas_call(
        inner_back_kernel,
        out_shape=pltpu.VMEM(base.shape, F32),
        in_specs=[SCALARS, SCALARS, WHOLE, WHOLE, FAR],
        out_specs=WHOLE,
        scratch_shapes=[pltpu.VMEM(inner.shape, BF16), pltpu.SemaphoreType.DMA((count // GROUP,))],
        compiler_params=params(8),
        cost_estimate=cost(count * block * block * scaled.shape[1] * 2, 3 * MIB),
        name="inner_back",
    )(rows, cols, scaled, base, *far(inner))


def add_came_kernel(total, came, out):
    out[...] = total[...] + came[...].astype(F32)


def add_came(total, came):
    return pl.pallas_call(
        add_came_kernel,
        out_shape=pltpu.VMEM(total.shape, F32),
        in_specs=[WHOLE, WHOLE],
        out_specs=WHOLE,
        compiler_params=params(4),
        cost_estimate=cost(total.size, total.size * 10),
        name="add_came",
    )(total, came)


def add_returned_kernel(order, targets, returned, total, out, summed):
    peers, slots, _, _ = returned.shape
    summed[...] = total[...]

    def some(places):
        for j in places:
            for k in range(slots):
                summed[targets[k, 0, peer_at(order, j)]] += returned[j, k].astype(F32)

    for_places(peers, some)
    out[...] = summed[...].astype(BF16)


def add_returned(targets, returned, total, order):
    return pl.pallas_call(
        functools.partial(add_returned_kernel, order),
        out_shape=pltpu.VMEM(total.shape, BF16),
        in_specs=[SCALARS, WHOLE, WHOLE],
        out_specs=WHOLE,
        scratch_shapes=[pltpu.VMEM(total.shape, F32)],
        compiler_params=params(8 + returned.size * 2 / MIB),
        cost_estimate=cost(total.size * 8, 2 * MIB),
        name="add_returned",
    )(targets, returned, total)


def pair_sum_kernel(a, b, out):
    out[...] = (a[...].astype(F32) + b[...].astype(F32)).astype(BF16)


def pair_sum(a, b):
    return pl.pallas_call(
        pair_sum_kernel,
        out_shape=jax.ShapeDtypeStruct(a.shape, BF16),
        in_specs=[WHOLE, WHOLE],
        out_specs=WHOLE,
        compiler_params=params(4),
        cost_estimate=cost(a.size * 2, a.size * 6),
        name="pair_sum",
    )(a, b)


def finish_kernel(mine, across, beside, opposite, grads, grads_came, out, self_out, neigh_out, turned, summed, sems):
    loc, part, block = mine.shape
    me = lax.axis_index("grp")
    feat_width = turned.shape[1]
    summed[...] = grads[...].astype(F32) + grads_came[...].astype(F32)
    copies = [
        pltpu.make_async_copy(summed.at[pl.ds(0, feat_width)], self_out, sems.at[0]),
        pltpu.make_async_copy(summed.at[pl.ds(feat_width, feat_width)], neigh_out, sems.at[1]),
    ]
    for copy in copies:
        copy.start()
    row = lax.broadcasted_iota(jnp.int32, (feat_width, feat_width), 0)
    lane = lax.broadcasted_iota(jnp.int32, (feat_width, feat_width), 1)
    stacked = row // part
    away = jnp.where(stacked == 1, 2, jnp.where(stacked == 2, 1, stacked))
    order = (((me ^ away) * part + row % part) == lane).astype(BF16)
    step = loc // 4
    for c in range(4):
        for b in range(c * step, (c + 1) * step):
            stack = jnp.concatenate([mine[b], across[b], beside[b], opposite[b]], axis=0)
            turned[b * block : (b + 1) * block] = lax.dot_general(stack, order, ROWS_FIRST, preferred_element_type=F32)
        place = pl.ds(c * step * block, step * block)
        copies.append(pltpu.make_async_copy(turned.at[place], out.at[place], sems.at[2 + c]))
        copies[-1].start()
    for copy in copies:
        copy.wait()


def finish(mine, across, beside, opposite, grads, grads_came):
    loc, part, block = mine.shape
    feat_width = grads.shape[0] // 2
    weight = jax.ShapeDtypeStruct((feat_width, grads.shape[1]), F32)
    return pl.pallas_call(
        finish_kernel,
        out_shape=(jax.ShapeDtypeStruct((loc * block, feat_width), F32), weight, weight),
        in_specs=[WHOLE] * 6,
        out_specs=(FAR, FAR, FAR),
        scratch_shapes=[
            pltpu.VMEM((loc * block, feat_width), F32),
            pltpu.VMEM(grads.shape, F32),
            pltpu.SemaphoreType.DMA((6,)),
        ],
        compiler_params=params(8),
        cost_estimate=cost(loc * block * feat_width * feat_width * 2, 2 * MIB),
        name="finish",
    )(mine, across, beside, opposite, grads, grads_came)


def swap(x, axis, bit):
    return lax.ppermute(x, axis, [(i, i ^ bit) for i in range(lax.axis_size(axis))])


def shards(
    features,
    weight_self,
    weight_neigh,
    cotangent,
    inner_rows,
    inner_cols,
    inner_values,
    send_blocks,
    outer_rows,
    outer_values,
    live_count,
):
    peers = lax.axis_size("dom")
    feat_width = features.shape[1]
    inner_a, outer_a = inner_values[0], outer_values[0]
    targets = send_blocks.transpose(2, 0, 1)
    block = inner_a.shape[-1]

    out_order, back_order = order_of(OUT_ORDER, peers), order_of(BACK_ORDER, peers)
    own = exchange(gather_halves(features, targets, block, out_order), out_order)
    rows, cols, outer_rows, live, targets, total, over, over_rows = stage(
        inner_rows, inner_cols, outer_rows, live_count, targets, features, inner_a, outer_a
    )
    own, total, outer_a = lax.optimization_barrier((own, total, outer_a))
    other = swap(own, "grp", 1)
    outer_a, features, cotangent, weights, turned = fetch(outer_a, features, cotangent, weight_self, weight_neigh)
    smooth, grad_pre, both, send_n, keep_n, send_s, keep_s = layer(
        outer_rows, live, own, other, outer_a, total, over, over_rows, features, cotangent, weights, turned, out_order
    )
    layer_out, grads = weight_grads(smooth, grad_pre, both)
    got_n = swap(send_n, "grp", 1)
    got_n, grads = lax.optimization_barrier((got_n, grads))
    came_n = swap((keep_n[0].astype(F32) + got_n[0].astype(F32)).astype(BF16), "grp", 2)
    got_s = swap(send_s, "grp", 1)
    came_s = swap((keep_s[0].astype(F32) + got_s[0].astype(F32)).astype(BF16), "grp", 2)
    scaled, base, payload = outer_back(outer_rows, live, keep_n, got_n, came_n, keep_s, got_s, outer_a, back_order)
    returned = exchange(payload, back_order)
    bit = peers // 2
    while bit > 2:
        came, came_s = lax.optimization_barrier((swap(grads, "dom", bit), came_s))
        grads = (grads.astype(F32) + came.astype(F32)).astype(BF16)
        bit //= 2
    base, grads = lax.optimization_barrier((base, grads))
    partial = add_came(inner_back(rows, cols, scaled, base, inner_a), came_s)
    grads = pair_sum(grads, swap(grads, "dom", 1))
    mine = add_returned(targets, returned, partial, back_order)
    across = swap(mine, "grp", 2)
    beside = swap(mine, "grp", 1)
    opposite = swap(across, "grp", 1)
    feature_grad, self_grad, neigh_grad = finish(mine, across, beside, opposite, grads, swap(grads, "dom", 2))
    return layer_out, feature_grad, self_grad, neigh_grad


def solution(mesh):
    placed = (
        P("dom", None),
        P(None, "grp"),
        P(None, "grp"),
        P("dom", "grp"),
        P("dom", None),
        P("dom", None),
        P("dom", None, None, None),
        P("dom", None, None),
        P("dom", None),
        P("dom", None, None, None),
        P("dom", None),
    )
    return jax.shard_map(
        shards,
        mesh=mesh,
        in_specs=placed,
        out_specs=(P("dom", "grp"), P("dom", None), P(None, "grp"), P(None, "grp")),
        check_vma=False,
    )
```

```python
import functools

import jax
import jax.numpy as jnp
from jax import lax
from jax.experimental import pallas as pl
from jax.experimental.pallas import tpu as pltpu
from jax.sharding import PartitionSpec as P

F32 = jnp.float32
BF16 = jnp.bfloat16
MIB = 1 << 20
GROUP = 16
OUTER_GROUP = 8
ROWS_LAST = (((1,), (1,)), ((), ()))
ROWS_FIRST = (((0,), (0,)), ((), ()))
WHOLE = pl.BlockSpec(memory_space=pltpu.VMEM)
SCALARS = pl.BlockSpec(memory_space=pltpu.SMEM)
FAR = pl.BlockSpec(memory_space=pltpu.HBM)


def dot(a, b):
    return jnp.dot(a, b, preferred_element_type=F32)


def far(*arrays):
    return [pltpu.with_memory_space_constraint(x, pltpu.HBM) for x in arrays]


OUT_ORDER = (4, 7, 3, 2, 0, 1, 5, 6)
BACK_ORDER = (4, 2, 5, 3, 1, 0, 7, 6)


def order_of(order, peers):
    return order if len(order) == peers else tuple((j + peers // 2) % peers for j in range(peers))


def peer_at(order, j):
    return order[j] if isinstance(j, int) else lax.rem(j + len(order) // 2, len(order))


def exchange(x, order):
    return lax.all_to_all(x, "dom", split_axis=0, concat_axis=0, tiled=True, axis_index_groups=[list(order)])


def for_places(peers, body):
    together = max(k for k in range(1, 9) if peers % k == 0)
    if together == peers:
        body(range(peers))
    else:

        def some(g, _):
            body([g * together + k for k in range(together)])
            return 0

        lax.fori_loop(0, peers // together, some, 0)


def params(mib):
    return pltpu.CompilerParams(vmem_limit_bytes=int(mib * MIB))


def cost(flops, moved):
    return pl.CostEstimate(flops=int(flops), bytes_accessed=int(moved), transcendentals=0)


def gather_kernel(order, targets_far, feat_far, out, targets, feat, outgoing, sems, out_sem):
    pieces = sems.shape[0] - 1
    step = feat.shape[0] // pieces
    mine = lax.axis_index("grp") % 2
    fetches = [pltpu.make_async_copy(targets_far, targets, sems.at[pieces])]
    for k in range(pieces):
        place = pl.ds(k * step, step)
        fetches.append(pltpu.make_async_copy(feat_far.at[place, pl.ds(mine, 1)], feat.at[place], sems.at[k]))
    for fetch in fetches:
        fetch.start()
    for fetch in fetches:
        fetch.wait()
    slots = targets.shape[0]
    for j, p in enumerate(order):
        for s in range(slots):
            outgoing[j, s] = feat[targets[s, 0, p], 0]
        pltpu.make_async_copy(outgoing.at[j], out.at[j], out_sem).start()
    pltpu.make_async_copy(outgoing, out, out_sem).wait()


def gather_halves(features, targets, block, order):
    nodes, feat_width = features.shape
    loc, half = nodes // block, block // 2
    slots, _, peers = targets.shape
    return pl.pallas_call(
        functools.partial(gather_kernel, order),
        out_shape=jax.ShapeDtypeStruct((peers, slots, half, feat_width), BF16),
        in_specs=[FAR, FAR],
        out_specs=FAR,
        scratch_shapes=[
            pltpu.SMEM(targets.shape, jnp.int32),
            pltpu.VMEM((loc, 1, half, feat_width), BF16),
            pltpu.VMEM((peers, slots, half, feat_width), BF16),
            pltpu.SemaphoreType.DMA((5,)),
            pltpu.SemaphoreType.DMA,
        ],
        compiler_params=params(4 + 2 * peers * slots * half * feat_width / MIB),
        name="gather_halves",
    )(*far(targets, features.reshape(loc, 2, half, feat_width)))


def stage_kernel(
    rows_far, cols_far, outer_rows_far, live_far, targets_far, feat_far, inner_far, outer_far,
    rows, cols, outer_rows, live, targets, total, over, over_rows, feat,
    inner, outer, wide, degree_rows, sems, inner_sems,
):
    loc, block, feat_width = total.shape
    count, outer_count = inner.shape[0], outer.shape[0]
    slots, _, peers = targets.shape
    scalars = [
        pltpu.make_async_copy(source, place, sems.at[k])
        for k, (source, place) in enumerate((
            (rows_far, rows), (cols_far, cols), (outer_rows_far, outer_rows), (live_far, live), (targets_far, targets),
        ))
    ]
    tables = [
        pltpu.make_async_copy(source, place, sems.at[5 + k])
        for k, (source, place) in enumerate((
            (feat_far, feat), (outer_far, outer),
        ))
    ]
    groups = count // GROUP
    blocks = [
        pltpu.make_async_copy(
            inner_far.at[pl.ds(g * GROUP, GROUP)], inner.at[pl.ds(g * GROUP, GROUP)], inner_sems.at[g]
        )
        for g in range(groups)
    ]
    for copy in scalars + tables[:1] + blocks + tables[1:]:
        copy.start()
    for copy in scalars + tables[:1]:
        copy.wait()
    x = feat[...].reshape(loc, block, feat_width)
    wide[:, :, :feat_width] = x
    wide[:, :, feat_width:] = jnp.ones((loc, block, feat_width), BF16)
    total[...] = x.astype(F32)
    over[...] = jnp.ones((loc, block, feat_width), F32)
    degree_rows[...] = jnp.ones(degree_rows.shape, F32)
    few = jnp.ones((degree_rows.shape[1], block), BF16)
    for g in range(groups):
        blocks[g].wait()
        products = [dot(inner[g * GROUP + k], wide[cols[0, g * GROUP + k]]) for k in range(GROUP)]
        flat = [
            lax.dot_general(few, inner[g * GROUP + k], ROWS_LAST, preferred_element_type=F32) for k in range(GROUP)
        ]
        for k in range(GROUP):
            r = rows[0, g * GROUP + k]
            total[r] += products[k][:, :feat_width]
            over[r] += products[k][:, feat_width:]
            degree_rows[r] += flat[k]
    for copy in tables[1:]:
        copy.wait()

    def some(g, _):
        ones = jnp.ones((block, feat_width), BF16)
        products = [dot(outer[g * OUTER_GROUP + k], ones) for k in range(OUTER_GROUP)]
        flat = [
            lax.dot_general(few, outer[g * OUTER_GROUP + k], ROWS_LAST, preferred_element_type=F32) for k in range(OUTER_GROUP)
        ]
        for k in range(OUTER_GROUP):
            n = g * OUTER_GROUP + k
            alive = (n % slots < live[0, n // slots]).astype(F32)
            over[outer_rows[0, n]] += products[k] * alive
            degree_rows[outer_rows[0, n]] += flat[k] * alive
        return 0

    lax.fori_loop(0, outer_count // OUTER_GROUP, some, 0)
    over[...] = 1.0 / over[...]
    over_rows[...] = 1.0 / degree_rows[...]


def stage(rows, cols, outer_rows, live, targets, features, inner, outer):
    count, block, _ = inner.shape
    nodes, feat_width = features.shape
    loc = nodes // block
    scalars = (rows, cols, outer_rows, live, targets)
    sums = (loc, block, feat_width)
    return pl.pallas_call(
        stage_kernel,
        out_shape=tuple(pltpu.SMEM(x.shape, jnp.int32) for x in scalars)
        + (pltpu.VMEM(sums, F32), pltpu.VMEM(sums, F32), pltpu.VMEM((loc, 8, block), F32))
        + (pltpu.VMEM(features.shape, BF16),),
        in_specs=[FAR] * 8,
        out_specs=(SCALARS,) * 5 + (WHOLE,) * 4,
        scratch_shapes=[
            pltpu.VMEM(inner.shape, BF16),
            pltpu.VMEM(outer.shape, BF16),
            pltpu.VMEM((loc, block, 2 * feat_width), BF16),
            pltpu.VMEM((loc, 8, block), F32),
            pltpu.SemaphoreType.DMA((7,)),
            pltpu.SemaphoreType.DMA((count // GROUP,)),
        ],
        compiler_params=params(12 + outer.size * 2 / MIB),
        cost_estimate=cost(count * block * block * feat_width * 4, 6 * MIB),
        name="stage",
    )(*far(*scalars, features, inner, outer))


def fetch_kernel(
    outer_far, cot_far, self_far, neigh_far, outer, cot, weights, turned, w_self, w_neigh, sems
):
    feat_width = w_self.shape[0]
    part = feat_width // lax.axis_size("grp")
    me = lax.axis_index("grp")
    fetches = [
        pltpu.make_async_copy(source, place, sems.at[k])
        for k, (source, place) in enumerate((
            (self_far, w_self), (neigh_far, w_neigh), (outer_far, outer), (cot_far, cot),
        ))
    ]
    for fetch in fetches:
        fetch.start()
    for fetch in fetches[:2]:
        fetch.wait()
    weights[:feat_width] = w_self[...] * 0.5
    weights[feat_width:] = w_neigh[...] * 0.5
    for spot, away in enumerate((3, 1, 2, 0)):
        start = pl.multiple_of((me ^ away) * part, part)
        turned[pl.ds(spot * part, part)] = w_self[pl.ds(start, part)] * 0.5
        turned[pl.ds(feat_width + spot * part, part)] = w_neigh[pl.ds(start, part)] * 0.5
    for fetch in fetches[2:]:
        fetch.wait()


def fetch(outer, cotangent, w_self, w_neigh):
    both = (2 * w_self.shape[0], w_self.shape[1])
    return pl.pallas_call(
        fetch_kernel,
        out_shape=tuple(pltpu.VMEM(shape, BF16) for shape in (outer.shape, cotangent.shape, both, both)),
        in_specs=[FAR] * 4,
        out_specs=(WHOLE,) * 4,
        scratch_shapes=[
            pltpu.VMEM(w_self.shape, BF16),
            pltpu.VMEM(w_neigh.shape, BF16),
            pltpu.SemaphoreType.DMA((4,)),
        ],
        compiler_params=params(8 + outer.size * 2 / MIB),
        cost_estimate=cost(1e6, 3 * MIB),
        name="fetch",
    )(*far(outer, cotangent, w_self, w_neigh))


def layer_kernel(
    chunk_blocks, order,
    outer_rows, live, own, other, outer, total_in, over_all, over_rows, feat, cot, weights, turned,
    smooth, grad_pre_all, both_all, send_n, keep_n, send_s, keep_s, total,
):
    del total_in
    peers, slots, half, feat_width = own.shape
    count, block, _ = outer.shape
    loc = total.shape[0]
    chunks = loc // chunk_blocks
    rows = chunk_blocks * block
    part = feat_width // lax.axis_size("grp")
    mine = lax.axis_index("grp") % 2

    def some(places):
        blocks = [(j, k, peer_at(order, j) * slots + k) for j in places for k in range(slots)]
        products = []
        for j, k, n in blocks:
            near, away = own[j, k], other[j, k]
            x = jnp.concatenate([jnp.where(mine == 0, near, away), jnp.where(mine == 0, away, near)], axis=0)
            products.append(dot(outer[n], x))
        for (j, k, n), product in zip(blocks, products):
            alive = (k < live[0, peer_at(order, j)]).astype(F32)
            total[outer_rows[0, n]] += product * alive

    for_places(peers, some)
    for c in range(chunks):
        place = pl.ds(c * rows, rows)
        here = pl.ds(c * chunk_blocks, chunk_blocks)
        over = over_all[here].reshape(rows, feat_width)
        agg = (total[here].reshape(rows, feat_width) * over).astype(BF16)
        both = jnp.concatenate([feat[place], agg], axis=1)
        pre = dot(both, weights[...])
        bent = jnp.tanh(pre)
        twice = 1.0 + bent
        silu = pre * twice
        smooth[place] = silu.astype(BF16)
        grad_pre = (cot[place].astype(F32) * (twice + silu * (1.0 - bent))).astype(BF16)
        grad_pre_all[place] = grad_pre
        both_all[place] = both
        back = lax.dot_general(turned[...], grad_pre, ROWS_LAST, preferred_element_type=F32)
        for b in range(chunk_blocks):
            at = c * chunk_blocks + b
            lanes = slice(b * block, (b + 1) * block)
            self_t = back[:feat_width, lanes].astype(BF16)
            neigh_t = (back[feat_width:, lanes] * over_rows[at, :1]).astype(BF16)
            for y in range(2):
                send_n[y, at] = neigh_t[y * part : (y + 1) * part]
                keep_n[y, at] = neigh_t[(2 + y) * part : (3 + y) * part]
                send_s[y, at] = self_t[y * part : (y + 1) * part]
                keep_s[y, at] = self_t[(2 + y) * part : (3 + y) * part]


def layer(outer_rows, live, own, other, outer, total, over, over_rows, features, cotangent, weights, turned, order):
    feat_width = features.shape[1]
    loc, block, _ = total.shape
    chunk = 4
    part = feat_width // lax.axis_size("grp")
    piece = pltpu.VMEM((2, loc, part, block), BF16)
    return pl.pallas_call(
        functools.partial(layer_kernel, chunk, order),
        out_shape=(
            pltpu.VMEM(cotangent.shape, BF16),
            pltpu.VMEM(cotangent.shape, BF16),
            pltpu.VMEM((cotangent.shape[0], 2 * feat_width), BF16),
            piece, piece, piece, piece,
            pltpu.VMEM(total.shape, F32),
        ),
        in_specs=[SCALARS] * 2 + [WHOLE] * 10,
        out_specs=(WHOLE,) * 8,
        input_output_aliases={5: 7},
        compiler_params=params(16 + 4 * own.size * 2 / MIB),
        cost_estimate=cost(1.2e9, 8 * MIB),
        name="layer",
    )(outer_rows, live, own, other, outer, total, over, over_rows, features, cotangent, weights, turned)[:7]


def weight_grads_kernel(smooth, grad_pre, both, layer_out, grads, sems):
    pieces = sems.shape[0]
    rows = smooth.shape[0] // pieces
    copies = [
        pltpu.make_async_copy(smooth.at[pl.ds(c * rows, rows)], layer_out.at[pl.ds(c * rows, rows)], sems.at[c])
        for c in range(pieces)
    ]
    for copy in copies:
        copy.start()
    grown = lax.dot_general(both[...], grad_pre[...], ROWS_FIRST, preferred_element_type=F32)
    grads[...] = (0.5 * grown).astype(BF16)
    for copy in copies:
        copy.wait()


def weight_grads(smooth, grad_pre, both):
    return pl.pallas_call(
        weight_grads_kernel,
        out_shape=(
            jax.ShapeDtypeStruct(smooth.shape, BF16),
            pltpu.VMEM((both.shape[1], grad_pre.shape[1]), BF16),
        ),
        in_specs=[WHOLE] * 3,
        out_specs=(FAR, WHOLE),
        scratch_shapes=[pltpu.SemaphoreType.DMA((4,))],
        compiler_params=params(12),
        cost_estimate=cost(2 * grad_pre.size * both.shape[1], 4 * MIB),
        name="weight_grads",
    )(smooth, grad_pre, both)


def outer_back_kernel(
    order, outer_rows, live, keep, got, came, keep_s, got_s, outer, scaled, base, payload_far, payload, sem
):
    peers, slots, part, block = payload.shape
    near = (keep[1].astype(F32) + got[1].astype(F32) + came[...].astype(F32)).astype(BF16)
    scaled[...] = near
    base[...] = near.astype(F32) + keep_s[1].astype(F32) + got_s[1].astype(F32)

    def some(places):
        blocks = [(j, k, peer_at(order, j) * slots + k) for j in places for k in range(slots)]
        products = [dot(scaled[outer_rows[0, n]], outer[n]) for _, _, n in blocks]
        for (j, k, n), product in zip(blocks, products):
            alive = (k < live[0, peer_at(order, j)]).astype(F32)
            payload[j, k] = (product * alive).astype(BF16)
            if k == slots - 1:
                pltpu.make_async_copy(payload.at[j], payload_far.at[j], sem).start()

    for_places(peers, some)
    pltpu.make_async_copy(payload, payload_far, sem).wait()


def outer_back(outer_rows, live, keep, got, came, keep_s, got_s, outer, order):
    loc, part, block = came.shape
    count, peers = outer.shape[0], len(order)
    return pl.pallas_call(
        functools.partial(outer_back_kernel, order),
        out_shape=(
            pltpu.VMEM((loc, part, block), BF16),
            pltpu.VMEM((loc, part, block), F32),
            jax.ShapeDtypeStruct((peers, count // peers, part, block), BF16),
        ),
        in_specs=[SCALARS, SCALARS] + [WHOLE] * 6,
        out_specs=(WHOLE, WHOLE, FAR),
        scratch_shapes=[pltpu.VMEM((peers, count // peers, part, block), BF16), pltpu.SemaphoreType.DMA],
        compiler_params=params(8 + count * block * (block + part) * 2 / MIB),
        cost_estimate=cost(count * block * block * part * 2, 2 * MIB),
        name="outer_back",
    )(outer_rows, live, keep, got, came, keep_s, got_s, outer)


def inner_back_kernel(rows, cols, scaled, base, inner_far, total, inner, sems):
    groups = inner.shape[0] // GROUP
    blocks = [
        pltpu.make_async_copy(inner_far.at[pl.ds(g * GROUP, GROUP)], inner.at[pl.ds(g * GROUP, GROUP)], sems.at[g])
        for g in range(groups)
    ]
    for copy in blocks:
        copy.start()
    total[...] = base[...]
    for g in range(groups):
        blocks[g].wait()
        products = [dot(scaled[rows[0, g * GROUP + k]], inner[g * GROUP + k]) for k in range(GROUP)]
        for k in range(GROUP):
            total[cols[0, g * GROUP + k]] += products[k]


def inner_back(rows, cols, scaled, base, inner):
    count, block, _ = inner.shape
    return pl.pallas_call(
        inner_back_kernel,
        out_shape=pltpu.VMEM(base.shape, F32),
        in_specs=[SCALARS, SCALARS, WHOLE, WHOLE, FAR],
        out_specs=WHOLE,
        scratch_shapes=[pltpu.VMEM(inner.shape, BF16), pltpu.SemaphoreType.DMA((count // GROUP,))],
        compiler_params=params(8),
        cost_estimate=cost(count * block * block * scaled.shape[1] * 2, 3 * MIB),
        name="inner_back",
    )(rows, cols, scaled, base, *far(inner))


def add_came_kernel(total, came, out):
    out[...] = total[...] + came[...].astype(F32)


def add_came(total, came):
    return pl.pallas_call(
        add_came_kernel,
        out_shape=pltpu.VMEM(total.shape, F32),
        in_specs=[WHOLE, WHOLE],
        out_specs=WHOLE,
        compiler_params=params(4),
        cost_estimate=cost(total.size, total.size * 10),
        name="add_came",
    )(total, came)


def add_returned_kernel(order, targets, returned, total, out, summed):
    peers, slots, _, _ = returned.shape
    summed[...] = total[...]

    def some(places):
        for j in places:
            for k in range(slots):
                summed[targets[k, 0, peer_at(order, j)]] += returned[j, k].astype(F32)

    for_places(peers, some)
    out[...] = summed[...].astype(BF16)


def add_returned(targets, returned, total, order):
    return pl.pallas_call(
        functools.partial(add_returned_kernel, order),
        out_shape=pltpu.VMEM(total.shape, BF16),
        in_specs=[SCALARS, WHOLE, WHOLE],
        out_specs=WHOLE,
        scratch_shapes=[pltpu.VMEM(total.shape, F32)],
        compiler_params=params(8 + returned.size * 2 / MIB),
        cost_estimate=cost(total.size * 8, 2 * MIB),
        name="add_returned",
    )(targets, returned, total)


def pair_sum_kernel(a, b, out):
    out[...] = (a[...].astype(F32) + b[...].astype(F32)).astype(BF16)


def pair_sum(a, b):
    return pl.pallas_call(
        pair_sum_kernel,
        out_shape=jax.ShapeDtypeStruct(a.shape, BF16),
        in_specs=[WHOLE, WHOLE],
        out_specs=WHOLE,
        compiler_params=params(4),
        cost_estimate=cost(a.size * 2, a.size * 6),
        name="pair_sum",
    )(a, b)


def finish_kernel(mine, across, beside, opposite, grads, grads_came, out, self_out, neigh_out, turned, summed, sems):
    loc, part, block = mine.shape
    me = lax.axis_index("grp")
    feat_width = turned.shape[1]
    summed[...] = grads[...].astype(F32) + grads_came[...].astype(F32)
    copies = [
        pltpu.make_async_copy(summed.at[pl.ds(0, feat_width)], self_out, sems.at[0]),
        pltpu.make_async_copy(summed.at[pl.ds(feat_width, feat_width)], neigh_out, sems.at[1]),
    ]
    for copy in copies:
        copy.start()
    row = lax.broadcasted_iota(jnp.int32, (feat_width, feat_width), 0)
    lane = lax.broadcasted_iota(jnp.int32, (feat_width, feat_width), 1)
    stacked = row // part
    away = jnp.where(stacked == 1, 2, jnp.where(stacked == 2, 1, stacked))
    order = (((me ^ away) * part + row % part) == lane).astype(BF16)
    step = loc // 4
    for c in range(4):
        for b in range(c * step, (c + 1) * step):
            stack = jnp.concatenate([mine[b], across[b], beside[b], opposite[b]], axis=0)
            turned[b * block : (b + 1) * block] = lax.dot_general(stack, order, ROWS_FIRST, preferred_element_type=F32)
        place = pl.ds(c * step * block, step * block)
        copies.append(pltpu.make_async_copy(turned.at[place], out.at[place], sems.at[2 + c]))
        copies[-1].start()
    for copy in copies:
        copy.wait()


def finish(mine, across, beside, opposite, grads, grads_came):
    loc, part, block = mine.shape
    feat_width = grads.shape[0] // 2
    weight = jax.ShapeDtypeStruct((feat_width, grads.shape[1]), F32)
    return pl.pallas_call(
        finish_kernel,
        out_shape=(jax.ShapeDtypeStruct((loc * block, feat_width), F32), weight, weight),
        in_specs=[WHOLE] * 6,
        out_specs=(FAR, FAR, FAR),
        scratch_shapes=[
            pltpu.VMEM((loc * block, feat_width), F32),
            pltpu.VMEM(grads.shape, F32),
            pltpu.SemaphoreType.DMA((6,)),
        ],
        compiler_params=params(8),
        cost_estimate=cost(loc * block * feat_width * feat_width * 2, 2 * MIB),
        name="finish",
    )(mine, across, beside, opposite, grads, grads_came)


def swap(x, axis, bit):
    return lax.ppermute(x, axis, [(i, i ^ bit) for i in range(lax.axis_size(axis))])


def shards(
    features,
    weight_self,
    weight_neigh,
    cotangent,
    inner_rows,
    inner_cols,
    inner_values,
    send_blocks,
    outer_rows,
    outer_values,
    live_count,
):
    peers = lax.axis_size("dom")
    feat_width = features.shape[1]
    inner_a, outer_a = inner_values[0], outer_values[0]
    targets = send_blocks.transpose(2, 0, 1)
    block = inner_a.shape[-1]

    out_order, back_order = order_of(OUT_ORDER, peers), order_of(BACK_ORDER, peers)
    own = exchange(gather_halves(features, targets, block, out_order), out_order)
    rows, cols, outer_rows, live, targets, total, over, over_rows, features = stage(
        inner_rows, inner_cols, outer_rows, live_count, targets, features, inner_a, outer_a
    )
    own, total, outer_a = lax.optimization_barrier((own, total, outer_a))
    other = swap(own, "grp", 1)
    outer_a, cotangent, weights, turned = fetch(outer_a, cotangent, weight_self, weight_neigh)
    smooth, grad_pre, both, send_n, keep_n, send_s, keep_s = layer(
        outer_rows, live, own, other, outer_a, total, over, over_rows, features, cotangent, weights, turned, out_order
    )
    layer_out, grads = weight_grads(smooth, grad_pre, both)
    got_n = swap(send_n, "grp", 1)
    got_n, grads = lax.optimization_barrier((got_n, grads))
    came_n = swap((keep_n[0].astype(F32) + got_n[0].astype(F32)).astype(BF16), "grp", 2)
    got_s = swap(send_s, "grp", 1)
    came_s = swap((keep_s[0].astype(F32) + got_s[0].astype(F32)).astype(BF16), "grp", 2)
    scaled, base, payload = outer_back(outer_rows, live, keep_n, got_n, came_n, keep_s, got_s, outer_a, back_order)
    returned = exchange(payload, back_order)
    bit = peers // 2
    while bit > 2:
        came, came_s = lax.optimization_barrier((swap(grads, "dom", bit), came_s))
        grads = (grads.astype(F32) + came.astype(F32)).astype(BF16)
        bit //= 2
    base, grads = lax.optimization_barrier((base, grads))
    partial = add_came(inner_back(rows, cols, scaled, base, inner_a), came_s)
    grads = pair_sum(grads, swap(grads, "dom", 1))
    mine = add_returned(targets, returned, partial, back_order)
    across = swap(mine, "grp", 2)
    beside = swap(mine, "grp", 1)
    opposite = swap(across, "grp", 1)
    feature_grad, self_grad, neigh_grad = finish(mine, across, beside, opposite, grads, swap(grads, "dom", 2))
    return layer_out, feature_grad, self_grad, neigh_grad


def solution(mesh):
    placed = (
        P("dom", None),
        P(None, "grp"),
        P(None, "grp"),
        P("dom", "grp"),
        P("dom", None),
        P("dom", None),
        P("dom", None, None, None),
        P("dom", None, None),
        P("dom", None),
        P("dom", None, None, None),
        P("dom", None),
    )
    return jax.shard_map(
        shards,
        mesh=mesh,
        in_specs=placed,
        out_specs=(P("dom", "grp"), P("dom", None), P(None, "grp"), P(None, "grp")),
        check_vma=False,
    )
```

```python
import functools

import jax
import jax.numpy as jnp
from jax import lax
from jax.experimental import pallas as pl
from jax.experimental.pallas import tpu as pltpu
from jax.sharding import PartitionSpec as P

F32 = jnp.float32
BF16 = jnp.bfloat16
MIB = 1 << 20
GROUP = 16
OUTER_GROUP = 8
ROWS_LAST = (((1,), (1,)), ((), ()))
ROWS_FIRST = (((0,), (0,)), ((), ()))
WHOLE = pl.BlockSpec(memory_space=pltpu.VMEM)
SCALARS = pl.BlockSpec(memory_space=pltpu.SMEM)
FAR = pl.BlockSpec(memory_space=pltpu.HBM)


def dot(a, b):
    return jnp.dot(a, b, preferred_element_type=F32)


def far(*arrays):
    return [pltpu.with_memory_space_constraint(x, pltpu.HBM) for x in arrays]


OUT_ORDER = (4, 7, 3, 2, 0, 1, 5, 6)
BACK_ORDER = (4, 2, 5, 3, 1, 0, 7, 6)


def order_of(order, peers):
    return order if len(order) == peers else tuple((j + peers // 2) % peers for j in range(peers))


def peer_at(order, j):
    return order[j] if isinstance(j, int) else lax.rem(j + len(order) // 2, len(order))


def exchange(x, order):
    return lax.all_to_all(x, "dom", split_axis=0, concat_axis=0, tiled=True, axis_index_groups=[list(order)])


def for_places(peers, body):
    together = max(k for k in range(1, 9) if peers % k == 0)
    if together == peers:
        body(range(peers))
    else:

        def some(g, _):
            body([g * together + k for k in range(together)])
            return 0

        lax.fori_loop(0, peers // together, some, 0)


def params(mib):
    return pltpu.CompilerParams(vmem_limit_bytes=int(mib * MIB))


def cost(flops, moved):
    return pl.CostEstimate(flops=int(flops), bytes_accessed=int(moved), transcendentals=0)


def gather_kernel(order, targets_far, feat_far, out, targets, feat, outgoing, sems, out_sem):
    pieces = sems.shape[0] - 1
    step = feat.shape[0] // pieces
    mine = lax.axis_index("grp") % 2
    fetches = [pltpu.make_async_copy(targets_far, targets, sems.at[pieces])]
    for k in range(pieces):
        place = pl.ds(k * step, step)
        fetches.append(pltpu.make_async_copy(feat_far.at[place, pl.ds(mine, 1)], feat.at[place], sems.at[k]))
    for fetch in fetches:
        fetch.start()
    for fetch in fetches:
        fetch.wait()
    slots = targets.shape[0]
    for j, p in enumerate(order):
        for s in range(slots):
            outgoing[j, s] = feat[targets[s, 0, p], 0]
        pltpu.make_async_copy(outgoing.at[j], out.at[j], out_sem).start()
    pltpu.make_async_copy(outgoing, out, out_sem).wait()


def gather_halves(features, targets, block, order):
    nodes, feat_width = features.shape
    loc, half = nodes // block, block // 2
    slots, _, peers = targets.shape
    return pl.pallas_call(
        functools.partial(gather_kernel, order),
        out_shape=jax.ShapeDtypeStruct((peers, slots, half, feat_width), BF16),
        in_specs=[FAR, FAR],
        out_specs=FAR,
        scratch_shapes=[
            pltpu.SMEM(targets.shape, jnp.int32),
            pltpu.VMEM((loc, 1, half, feat_width), BF16),
            pltpu.VMEM((peers, slots, half, feat_width), BF16),
            pltpu.SemaphoreType.DMA((5,)),
            pltpu.SemaphoreType.DMA,
        ],
        compiler_params=params(4 + 2 * peers * slots * half * feat_width / MIB),
        name="gather_halves",
    )(*far(targets, features.reshape(loc, 2, half, feat_width)))


def stage_kernel(
    rows_far, cols_far, outer_rows_far, live_far, targets_far, feat_far, inner_far, outer_far,
    rows, cols, outer_rows, live, targets, total, over, over_rows, feat,
    inner, outer, wide, degree_rows, sems, inner_sems,
):
    loc, block, feat_width = total.shape
    count, outer_count = inner.shape[0], outer.shape[0]
    slots, _, peers = targets.shape
    scalars = [
        pltpu.make_async_copy(source, place, sems.at[k])
        for k, (source, place) in enumerate((
            (rows_far, rows), (cols_far, cols), (outer_rows_far, outer_rows), (live_far, live), (targets_far, targets),
        ))
    ]
    tables = [
        pltpu.make_async_copy(source, place, sems.at[5 + k])
        for k, (source, place) in enumerate((
            (feat_far, feat), (outer_far, outer),
        ))
    ]
    groups = count // GROUP
    blocks = [
        pltpu.make_async_copy(
            inner_far.at[pl.ds(g * GROUP, GROUP)], inner.at[pl.ds(g * GROUP, GROUP)], inner_sems.at[g]
        )
        for g in range(groups)
    ]
    for copy in scalars + tables[:1] + blocks + tables[1:]:
        copy.start()
    for copy in scalars + tables[:1]:
        copy.wait()
    x = feat[...].reshape(loc, block, feat_width)
    wide[:, :, :feat_width] = x
    wide[:, :, feat_width:] = jnp.ones((loc, block, feat_width), BF16)
    total[...] = x.astype(F32)
    over[...] = jnp.ones((loc, block, feat_width), F32)
    degree_rows[...] = jnp.ones(degree_rows.shape, F32)
    few = jnp.ones((degree_rows.shape[1], block), BF16)
    for g in range(groups):
        blocks[g].wait()
        products = [dot(inner[g * GROUP + k], wide[cols[0, g * GROUP + k]]) for k in range(GROUP)]
        flat = [
            lax.dot_general(few, inner[g * GROUP + k], ROWS_LAST, preferred_element_type=F32) for k in range(GROUP)
        ]
        for k in range(GROUP):
            r = rows[0, g * GROUP + k]
            total[r] += products[k][:, :feat_width]
            over[r] += products[k][:, feat_width:]
            degree_rows[r] += flat[k]
    for copy in tables[1:]:
        copy.wait()

    def some(g, _):
        ones = jnp.ones((block, feat_width), BF16)
        products = [dot(outer[g * OUTER_GROUP + k], ones) for k in range(OUTER_GROUP)]
        flat = [
            lax.dot_general(few, outer[g * OUTER_GROUP + k], ROWS_LAST, preferred_element_type=F32) for k in range(OUTER_GROUP)
        ]
        for k in range(OUTER_GROUP):
            n = g * OUTER_GROUP + k
            alive = (n % slots < live[0, n // slots]).astype(F32)
            over[outer_rows[0, n]] += products[k] * alive
            degree_rows[outer_rows[0, n]] += flat[k] * alive
        return 0

    lax.fori_loop(0, outer_count // OUTER_GROUP, some, 0)
    over[...] = 1.0 / over[...]
    over_rows[...] = 1.0 / degree_rows[...]


def stage(rows, cols, outer_rows, live, targets, features, inner, outer):
    count, block, _ = inner.shape
    nodes, feat_width = features.shape
    loc = nodes // block
    scalars = (rows, cols, outer_rows, live, targets)
    sums = (loc, block, feat_width)
    return pl.pallas_call(
        stage_kernel,
        out_shape=tuple(pltpu.SMEM(x.shape, jnp.int32) for x in scalars)
        + (pltpu.VMEM(sums, F32), pltpu.VMEM(sums, F32), pltpu.VMEM((loc, 8, block), F32))
        + (pltpu.VMEM(features.shape, BF16),),
        in_specs=[FAR] * 8,
        out_specs=(SCALARS,) * 5 + (WHOLE,) * 4,
        scratch_shapes=[
            pltpu.VMEM(inner.shape, BF16),
            pltpu.VMEM(outer.shape, BF16),
            pltpu.VMEM((loc, block, 2 * feat_width), BF16),
            pltpu.VMEM((loc, 8, block), F32),
            pltpu.SemaphoreType.DMA((7,)),
            pltpu.SemaphoreType.DMA((count // GROUP,)),
        ],
        compiler_params=params(12 + outer.size * 2 / MIB),
        cost_estimate=cost(count * block * block * feat_width * 4, 6 * MIB),
        name="stage",
    )(*far(*scalars, features, inner, outer))


def fetch_kernel(
    outer_far, cot_far, self_far, neigh_far, outer, cot, weights, turned, w_self, w_neigh, sems
):
    feat_width = w_self.shape[0]
    part = feat_width // lax.axis_size("grp")
    me = lax.axis_index("grp")
    fetches = [
        pltpu.make_async_copy(source, place, sems.at[k])
        for k, (source, place) in enumerate((
            (self_far, w_self), (neigh_far, w_neigh), (outer_far, outer),
        ))
    ]
    rows = cot.shape[0] // 4
    for k in range(4):
        place = pl.ds(k * rows, rows)
        fetches.append(pltpu.make_async_copy(cot_far.at[place], cot.at[place], sems.at[3 + k]))
    for fetch in fetches:
        fetch.start()
    for fetch in fetches[:2]:
        fetch.wait()
    weights[:feat_width] = w_self[...] * 0.5
    weights[feat_width:] = w_neigh[...] * 0.5
    for spot, away in enumerate((3, 1, 2, 0)):
        start = pl.multiple_of((me ^ away) * part, part)
        turned[pl.ds(spot * part, part)] = w_self[pl.ds(start, part)] * 0.5
        turned[pl.ds(feat_width + spot * part, part)] = w_neigh[pl.ds(start, part)] * 0.5
    for fetch in fetches[2:]:
        fetch.wait()


def fetch(outer, cotangent, w_self, w_neigh):
    both = (2 * w_self.shape[0], w_self.shape[1])
    return pl.pallas_call(
        fetch_kernel,
        out_shape=tuple(pltpu.VMEM(shape, BF16) for shape in (outer.shape, cotangent.shape, both, both)),
        in_specs=[FAR] * 4,
        out_specs=(WHOLE,) * 4,
        scratch_shapes=[
            pltpu.VMEM(w_self.shape, BF16),
            pltpu.VMEM(w_neigh.shape, BF16),
            pltpu.SemaphoreType.DMA((7,)),
        ],
        compiler_params=params(8 + outer.size * 2 / MIB),
        cost_estimate=cost(1e6, 3 * MIB),
        name="fetch",
    )(*far(outer, cotangent, w_self, w_neigh))


def layer_kernel(
    chunk_blocks, order,
    outer_rows, live, own, other, outer, total_in, over_all, over_rows, feat, cot, weights, turned,
    smooth, grad_pre_all, both_all, send_n, keep_n, send_s, keep_s, total,
):
    del total_in
    peers, slots, half, feat_width = own.shape
    count, block, _ = outer.shape
    loc = total.shape[0]
    chunks = loc // chunk_blocks
    rows = chunk_blocks * block
    part = feat_width // lax.axis_size("grp")
    mine = lax.axis_index("grp") % 2

    def some(places):
        blocks = [(j, k, peer_at(order, j) * slots + k) for j in places for k in range(slots)]
        products = []
        for j, k, n in blocks:
            near, away = own[j, k], other[j, k]
            x = jnp.concatenate([jnp.where(mine == 0, near, away), jnp.where(mine == 0, away, near)], axis=0)
            products.append(dot(outer[n], x))
        for (j, k, n), product in zip(blocks, products):
            alive = (k < live[0, peer_at(order, j)]).astype(F32)
            total[outer_rows[0, n]] += product * alive

    for_places(peers, some)
    for c in range(chunks):
        place = pl.ds(c * rows, rows)
        here = pl.ds(c * chunk_blocks, chunk_blocks)
        over = over_all[here].reshape(rows, feat_width)
        agg = (total[here].reshape(rows, feat_width) * over).astype(BF16)
        both = jnp.concatenate([feat[place], agg], axis=1)
        pre = dot(both, weights[...])
        bent = jnp.tanh(pre)
        twice = 1.0 + bent
        silu = pre * twice
        smooth[place] = silu.astype(BF16)
        grad_pre = (cot[place].astype(F32) * (twice + silu * (1.0 - bent))).astype(BF16)
        grad_pre_all[place] = grad_pre
        both_all[place] = both
        back = lax.dot_general(turned[...], grad_pre, ROWS_LAST, preferred_element_type=F32)
        for b in range(chunk_blocks):
            at = c * chunk_blocks + b
            lanes = slice(b * block, (b + 1) * block)
            self_t = back[:feat_width, lanes].astype(BF16)
            neigh_t = (back[feat_width:, lanes] * over_rows[at, :1]).astype(BF16)
            for y in range(2):
                send_n[y, at] = neigh_t[y * part : (y + 1) * part]
                keep_n[y, at] = neigh_t[(2 + y) * part : (3 + y) * part]
                send_s[y, at] = self_t[y * part : (y + 1) * part]
                keep_s[y, at] = self_t[(2 + y) * part : (3 + y) * part]


def layer(outer_rows, live, own, other, outer, total, over, over_rows, features, cotangent, weights, turned, order):
    feat_width = features.shape[1]
    loc, block, _ = total.shape
    chunk = 4
    part = feat_width // lax.axis_size("grp")
    piece = pltpu.VMEM((2, loc, part, block), BF16)
    return pl.pallas_call(
        functools.partial(layer_kernel, chunk, order),
        out_shape=(
            pltpu.VMEM(cotangent.shape, BF16),
            pltpu.VMEM(cotangent.shape, BF16),
            pltpu.VMEM((cotangent.shape[0], 2 * feat_width), BF16),
            piece, piece, piece, piece,
            pltpu.VMEM(total.shape, F32),
        ),
        in_specs=[SCALARS] * 2 + [WHOLE] * 10,
        out_specs=(WHOLE,) * 8,
        input_output_aliases={5: 7},
        compiler_params=params(16 + 4 * own.size * 2 / MIB),
        cost_estimate=cost(1.2e9, 8 * MIB),
        name="layer",
    )(outer_rows, live, own, other, outer, total, over, over_rows, features, cotangent, weights, turned)[:7]


def weight_grads_kernel(smooth, grad_pre, both, layer_out, grads, sems):
    pieces = sems.shape[0]
    rows = smooth.shape[0] // pieces
    copies = [
        pltpu.make_async_copy(smooth.at[pl.ds(c * rows, rows)], layer_out.at[pl.ds(c * rows, rows)], sems.at[c])
        for c in range(pieces)
    ]
    for copy in copies:
        copy.start()
    grown = lax.dot_general(both[...], grad_pre[...], ROWS_FIRST, preferred_element_type=F32)
    grads[...] = (0.5 * grown).astype(BF16)
    for copy in copies:
        copy.wait()


def weight_grads(smooth, grad_pre, both):
    return pl.pallas_call(
        weight_grads_kernel,
        out_shape=(
            jax.ShapeDtypeStruct(smooth.shape, BF16),
            pltpu.VMEM((both.shape[1], grad_pre.shape[1]), BF16),
        ),
        in_specs=[WHOLE] * 3,
        out_specs=(FAR, WHOLE),
        scratch_shapes=[pltpu.SemaphoreType.DMA((4,))],
        compiler_params=params(12),
        cost_estimate=cost(2 * grad_pre.size * both.shape[1], 4 * MIB),
        name="weight_grads",
    )(smooth, grad_pre, both)


def outer_back_kernel(
    order, outer_rows, live, keep, got, came, keep_s, got_s, outer, scaled, base, payload_far, payload, sem
):
    peers, slots, part, block = payload.shape
    near = (keep[1].astype(F32) + got[1].astype(F32) + came[...].astype(F32)).astype(BF16)
    scaled[...] = near
    base[...] = near.astype(F32) + keep_s[1].astype(F32) + got_s[1].astype(F32)

    def some(places):
        blocks = [(j, k, peer_at(order, j) * slots + k) for j in places for k in range(slots)]
        products = [dot(scaled[outer_rows[0, n]], outer[n]) for _, _, n in blocks]
        for (j, k, n), product in zip(blocks, products):
            alive = (k < live[0, peer_at(order, j)]).astype(F32)
            payload[j, k] = (product * alive).astype(BF16)
            if k == slots - 1:
                pltpu.make_async_copy(payload.at[j], payload_far.at[j], sem).start()

    for_places(peers, some)
    pltpu.make_async_copy(payload, payload_far, sem).wait()


def outer_back(outer_rows, live, keep, got, came, keep_s, got_s, outer, order):
    loc, part, block = came.shape
    count, peers = outer.shape[0], len(order)
    return pl.pallas_call(
        functools.partial(outer_back_kernel, order),
        out_shape=(
            pltpu.VMEM((loc, part, block), BF16),
            pltpu.VMEM((loc, part, block), F32),
            jax.ShapeDtypeStruct((peers, count // peers, part, block), BF16),
        ),
        in_specs=[SCALARS, SCALARS] + [WHOLE] * 6,
        out_specs=(WHOLE, WHOLE, FAR),
        scratch_shapes=[pltpu.VMEM((peers, count // peers, part, block), BF16), pltpu.SemaphoreType.DMA],
        compiler_params=params(8 + count * block * (block + part) * 2 / MIB),
        cost_estimate=cost(count * block * block * part * 2, 2 * MIB),
        name="outer_back",
    )(outer_rows, live, keep, got, came, keep_s, got_s, outer)


def inner_back_kernel(rows, cols, scaled, base, inner_far, total, inner, sems):
    groups = inner.shape[0] // GROUP
    blocks = [
        pltpu.make_async_copy(inner_far.at[pl.ds(g * GROUP, GROUP)], inner.at[pl.ds(g * GROUP, GROUP)], sems.at[g])
        for g in range(groups)
    ]
    for copy in blocks:
        copy.start()
    total[...] = base[...]
    for g in range(groups):
        blocks[g].wait()
        products = [dot(scaled[rows[0, g * GROUP + k]], inner[g * GROUP + k]) for k in range(GROUP)]
        for k in range(GROUP):
            total[cols[0, g * GROUP + k]] += products[k]


def inner_back(rows, cols, scaled, base, inner):
    count, block, _ = inner.shape
    return pl.pallas_call(
        inner_back_kernel,
        out_shape=pltpu.VMEM(base.shape, F32),
        in_specs=[SCALARS, SCALARS, WHOLE, WHOLE, FAR],
        out_specs=WHOLE,
        scratch_shapes=[pltpu.VMEM(inner.shape, BF16), pltpu.SemaphoreType.DMA((count // GROUP,))],
        compiler_params=params(8),
        cost_estimate=cost(count * block * block * scaled.shape[1] * 2, 3 * MIB),
        name="inner_back",
    )(rows, cols, scaled, base, *far(inner))


def add_came_kernel(total, came, out):
    out[...] = total[...] + came[...].astype(F32)


def add_came(total, came):
    return pl.pallas_call(
        add_came_kernel,
        out_shape=pltpu.VMEM(total.shape, F32),
        in_specs=[WHOLE, WHOLE],
        out_specs=WHOLE,
        compiler_params=params(4),
        cost_estimate=cost(total.size, total.size * 10),
        name="add_came",
    )(total, came)


def add_returned_kernel(order, targets, returned, total, out, summed):
    peers, slots, _, _ = returned.shape
    summed[...] = total[...]

    def some(places):
        for j in places:
            for k in range(slots):
                summed[targets[k, 0, peer_at(order, j)]] += returned[j, k].astype(F32)

    for_places(peers, some)
    out[...] = summed[...].astype(BF16)


def add_returned(targets, returned, total, order):
    return pl.pallas_call(
        functools.partial(add_returned_kernel, order),
        out_shape=pltpu.VMEM(total.shape, BF16),
        in_specs=[SCALARS, WHOLE, WHOLE],
        out_specs=WHOLE,
        scratch_shapes=[pltpu.VMEM(total.shape, F32)],
        compiler_params=params(8 + returned.size * 2 / MIB),
        cost_estimate=cost(total.size * 8, 2 * MIB),
        name="add_returned",
    )(targets, returned, total)


def pair_sum_kernel(a, b, out):
    out[...] = (a[...].astype(F32) + b[...].astype(F32)).astype(BF16)


def pair_sum(a, b):
    return pl.pallas_call(
        pair_sum_kernel,
        out_shape=jax.ShapeDtypeStruct(a.shape, BF16),
        in_specs=[WHOLE, WHOLE],
        out_specs=WHOLE,
        compiler_params=params(4),
        cost_estimate=cost(a.size * 2, a.size * 6),
        name="pair_sum",
    )(a, b)


def finish_kernel(mine, across, beside, opposite, grads, grads_came, out, self_out, neigh_out, turned, summed, sems):
    loc, part, block = mine.shape
    me = lax.axis_index("grp")
    feat_width = turned.shape[1]
    summed[...] = grads[...].astype(F32) + grads_came[...].astype(F32)
    copies = [
        pltpu.make_async_copy(summed.at[pl.ds(0, feat_width)], self_out, sems.at[0]),
        pltpu.make_async_copy(summed.at[pl.ds(feat_width, feat_width)], neigh_out, sems.at[1]),
    ]
    for copy in copies:
        copy.start()
    row = lax.broadcasted_iota(jnp.int32, (feat_width, feat_width), 0)
    lane = lax.broadcasted_iota(jnp.int32, (feat_width, feat_width), 1)
    stacked = row // part
    away = jnp.where(stacked == 1, 2, jnp.where(stacked == 2, 1, stacked))
    order = (((me ^ away) * part + row % part) == lane).astype(BF16)
    step = loc // 4
    for c in range(4):
        for b in range(c * step, (c + 1) * step):
            stack = jnp.concatenate([mine[b], across[b], beside[b], opposite[b]], axis=0)
            turned[b * block : (b + 1) * block] = lax.dot_general(stack, order, ROWS_FIRST, preferred_element_type=F32)
        place = pl.ds(c * step * block, step * block)
        copies.append(pltpu.make_async_copy(turned.at[place], out.at[place], sems.at[2 + c]))
        copies[-1].start()
    for copy in copies:
        copy.wait()


def finish(mine, across, beside, opposite, grads, grads_came):
    loc, part, block = mine.shape
    feat_width = grads.shape[0] // 2
    weight = jax.ShapeDtypeStruct((feat_width, grads.shape[1]), F32)
    return pl.pallas_call(
        finish_kernel,
        out_shape=(jax.ShapeDtypeStruct((loc * block, feat_width), F32), weight, weight),
        in_specs=[WHOLE] * 6,
        out_specs=(FAR, FAR, FAR),
        scratch_shapes=[
            pltpu.VMEM((loc * block, feat_width), F32),
            pltpu.VMEM(grads.shape, F32),
            pltpu.SemaphoreType.DMA((6,)),
        ],
        compiler_params=params(8),
        cost_estimate=cost(loc * block * feat_width * feat_width * 2, 2 * MIB),
        name="finish",
    )(mine, across, beside, opposite, grads, grads_came)


def swap(x, axis, bit):
    return lax.ppermute(x, axis, [(i, i ^ bit) for i in range(lax.axis_size(axis))])


def shards(
    features,
    weight_self,
    weight_neigh,
    cotangent,
    inner_rows,
    inner_cols,
    inner_values,
    send_blocks,
    outer_rows,
    outer_values,
    live_count,
):
    peers = lax.axis_size("dom")
    feat_width = features.shape[1]
    inner_a, outer_a = inner_values[0], outer_values[0]
    targets = send_blocks.transpose(2, 0, 1)
    block = inner_a.shape[-1]

    out_order, back_order = order_of(OUT_ORDER, peers), order_of(BACK_ORDER, peers)
    own = exchange(gather_halves(features, targets, block, out_order), out_order)
    rows, cols, outer_rows, live, targets, total, over, over_rows, features = stage(
        inner_rows, inner_cols, outer_rows, live_count, targets, features, inner_a, outer_a
    )
    own, total, outer_a = lax.optimization_barrier((own, total, outer_a))
    other = swap(own, "grp", 1)
    outer_a, cotangent, weights, turned = fetch(outer_a, cotangent, weight_self, weight_neigh)
    smooth, grad_pre, both, send_n, keep_n, send_s, keep_s = layer(
        outer_rows, live, own, other, outer_a, total, over, over_rows, features, cotangent, weights, turned, out_order
    )
    layer_out, grads = weight_grads(smooth, grad_pre, both)
    got_n = swap(send_n, "grp", 1)
    got_n, grads = lax.optimization_barrier((got_n, grads))
    came_n = swap((keep_n[0].astype(F32) + got_n[0].astype(F32)).astype(BF16), "grp", 2)
    got_s = swap(send_s, "grp", 1)
    came_s = swap((keep_s[0].astype(F32) + got_s[0].astype(F32)).astype(BF16), "grp", 2)
    scaled, base, payload = outer_back(outer_rows, live, keep_n, got_n, came_n, keep_s, got_s, outer_a, back_order)
    returned = exchange(payload, back_order)
    bit = peers // 2
    while bit > 2:
        came, came_s = lax.optimization_barrier((swap(grads, "dom", bit), came_s))
        grads = (grads.astype(F32) + came.astype(F32)).astype(BF16)
        bit //= 2
    base, grads = lax.optimization_barrier((base, grads))
    partial = add_came(inner_back(rows, cols, scaled, base, inner_a), came_s)
    grads = pair_sum(grads, swap(grads, "dom", 1))
    mine = add_returned(targets, returned, partial, back_order)
    across = swap(mine, "grp", 2)
    beside = swap(mine, "grp", 1)
    opposite = swap(across, "grp", 1)
    feature_grad, self_grad, neigh_grad = finish(mine, across, beside, opposite, grads, swap(grads, "dom", 2))
    return layer_out, feature_grad, self_grad, neigh_grad


def solution(mesh):
    placed = (
        P("dom", None),
        P(None, "grp"),
        P(None, "grp"),
        P("dom", "grp"),
        P("dom", None),
        P("dom", None),
        P("dom", None, None, None),
        P("dom", None, None),
        P("dom", None),
        P("dom", None, None, None),
        P("dom", None),
    )
    return jax.shard_map(
        shards,
        mesh=mesh,
        in_specs=placed,
        out_specs=(P("dom", "grp"), P("dom", None), P(None, "grp"), P(None, "grp")),
        check_vma=False,
    )
```
